32 devices in a mesh: groups: 2 (over y), seq: 4 (over z), tensor: 4 (over x, core).
Axes of the slice: x: 2, y: 2, z: 4, core: 2. Of those that a mesh axis runs over, the one named last changes fastest.
Arguments:
- queries: bfloat16 [2048, 4096], P(('groups', 'seq'), 'tensor'), parts along dimension 0, may hold values from -6 to 6
- key_rows: bfloat16 [2048, 2048], P(('groups', 'seq'), 'tensor'), parts along dimension 0, may hold values from -6 to 6
- value_rows: bfloat16 [2048, 2048], P(('groups', 'seq'), 'tensor'), parts along dimension 0, may hold values from -6 to 6
- positions: int32 [2048], P(('groups', 'seq')), parts along dimension 0, may hold values from 0 to 131071, as said below
- residual: bfloat16 [2048, 3840], P(('groups', 'seq'), 'tensor'), parts along dimension 0, may hold values from -16 to 16
- direction: float32 [7680], P('groups'), parts along dimension 0, may hold values from -90 to 90
- out_weight: bfloat16 [4096, 3840], P('tensor'), may hold values from -0.375 to 0.375
Outputs:
- ablated: bfloat16 [2048, 3840], P(('groups', 'seq'), 'tensor'), parts along dimension 0
The draws below stay inside these ranges and needn't reach their ends.
There are 2 independent parts, one for each index of `groups`. The reference program is written for one: setup_inputs(seed, part) draws one part's arguments, and reference() takes and returns one part's arrays. A program takes and returns all parts, laid end to end along the dimension named above; an argument that names none is the same for every part. Nothing has to cross between parts.
Inputs may be any that keep to these rules, and one draw needn't show every extreme that they name: positions strictly increase along the slab, by at most 4 from one token to the next; the slab ends at the prompt's last position.
All inputs are finite; a program needn't handle non-finite values.
Results may differ from the reference program's by a relative error of at most 0.017.
Values may be sent and summed in bfloat16 or wider, within the bound.
A program may use at most 64 MiB of HBM per device.

```python
import math
import jax
import jax.numpy as jnp
from jax import lax

D = 3840
HEADS = 16
KV_HEADS = 8
HD = 256
WINDOW = 1024
TOKENS = 1024
N_TENSOR = 4


def query_key_pair(key):
    pieces = jax.random.split(jax.random.fold_in(key, 11), 3)
    query_shape = (TOKENS, HEADS * HD)
    key_shape = (TOKENS, KV_HEADS * HD)
    query_vals = jnp.clip(2.0 * jax.random.normal(pieces[1], query_shape), -6.0, 6.0)
    key_vals = jnp.clip(jax.random.normal(pieces[2], key_shape), -6.0, 6.0)
    return (query_vals, key_vals)


def draw_queries(key, part):
    return query_key_pair(key)[0].astype(jnp.bfloat16)


def draw_key_rows(key, part):
    return query_key_pair(key)[1].astype(jnp.bfloat16)


def residual_direction_pair(key):
    pieces = jax.random.split(jax.random.fold_in(key, 23), 5)
    feature_ids = jnp.arange(D).astype(jnp.float32) / D
    jitter = jnp.exp(jax.random.uniform(pieces[1], (D,), minval=0.0, maxval=math.log(10.0)))
    ramp = 1.0 + 2.0 * feature_ids
    base_dir = jnp.clip(jax.random.normal(pieces[0], (D,)), -3.0, 3.0)
    noise_field = jnp.clip(jax.random.normal(pieces[4], (TOKENS, D)), -6.0, 6.0)
    raw_dir = base_dir * ramp * jitter
    magnitude = jnp.exp(jax.random.uniform(pieces[2], (TOKENS, 1), minval=math.log(5.0), maxval=math.log(60.0)))
    sign_col = jnp.where(jax.random.uniform(pieces[3], (TOKENS, 1)) < 0.5, -1.0, 1.0)
    resid_vals = noise_field + magnitude * sign_col * raw_dir[None, :] / 600.0
    return (resid_vals, raw_dir)


def draw_residual(key, part):
    return residual_direction_pair(key)[0].astype(jnp.bfloat16)


def draw_direction(key, part):
    return residual_direction_pair(key)[1].astype(jnp.float32)


def draw_positions(key, part):
    pieces = jax.random.split(jax.random.fold_in(key, 37), 2)
    rarely = (jax.random.randint(pieces[0], (TOKENS,), 0, 6) == 0).astype(jnp.int32)
    stride = 1 + rarely * jax.random.randint(pieces[1], (TOKENS,), 1, 4)
    after = jnp.cumsum(stride[::-1])[::-1] - stride
    return (131071 - after).astype(jnp.int32)


def shard_levels(own_key, dims, shards, least, high):
    def one(axis_at, shards_of):
        heights = jax.random.uniform(jax.random.fold_in(jax.random.fold_in(own_key, 6), axis_at), (shards_of,), jnp.float32, least / len(shards), high / len(shards))
        return jnp.repeat(jnp.exp(heights), dims[axis_at] // shards_of).reshape((-1,) + (1,) * (len(dims) - axis_at - 1))

    loudness = one(*shards[0])
    for cut in shards[1:]:
        loudness = loudness * one(*cut)
    return loudness


def bell_draw(key, extent, scale, bound, cuts=(), kind=jnp.bfloat16):
    factor_of = shard_levels(key, extent, cuts, -0.22, 0.18) if cuts else 1.0
    drawn = jax.random.normal(key, extent, jnp.float32) * scale * factor_of
    return jnp.minimum(jnp.maximum(drawn, -bound), bound).astype(kind)


def setup_inputs(seed: int = 0, part: int = 0) -> dict:
    seeds = jax.random.split(jax.random.key(seed), 8)
    own_keys = jax.random.split(jax.random.fold_in(seeds[7], part), 8)
    queries = draw_queries(jax.random.fold_in(jax.random.fold_in(seeds[7], part), 71), part)
    key_rows = draw_key_rows(jax.random.fold_in(jax.random.fold_in(seeds[7], part), 71), part)
    value_rows = bell_draw(own_keys[2], (TOKENS, KV_HEADS * HD), 1.0, 6.0, ((0, 4), (1, 4)))
    positions = draw_positions(jax.random.fold_in(jax.random.fold_in(seeds[7], part), 71), part)
    residual = draw_residual(jax.random.fold_in(jax.random.fold_in(seeds[7], part), 71), part)
    direction = draw_direction(jax.random.fold_in(jax.random.fold_in(seeds[7], part), 71), part)
    out_weight = bell_draw(seeds[6], (HEADS * HD, D), HD ** -0.5, 0.375, ((0, 4),))
    return {"queries": queries, "key_rows": key_rows, "value_rows": value_rows, "positions": positions, "residual": residual, "direction": direction, "out_weight": out_weight}


big_negative = -1e+30

def rotary_tables(positions, head_dim):
    half_dim = head_dim // 2
    freqs = jnp.power(10000.0, -jnp.arange(half_dim, dtype=jnp.float32) * 2.0 / head_dim)
    angles = positions.astype(jnp.float32)[:, None] * freqs[None, :]
    return (jnp.cos(angles)[:, None, :], jnp.sin(angles)[:, None, :])

def rotate_heads(block, cos_table, sin_table, head_dim):
    row_count = block.shape[0]
    head_count = block.shape[1] // head_dim
    half_dim = head_dim // 2
    widened = block.reshape(row_count, head_count, head_dim).astype(jnp.float32)
    first_half = widened[:, :, :half_dim]
    second_half = widened[:, :, half_dim:]
    turned = jnp.concatenate([first_half * cos_table - second_half * sin_table, second_half * cos_table + first_half * sin_table], axis=-1)
    return turned.reshape(row_count, head_count * head_dim)

def reference(queries, key_rows, value_rows, positions, residual, direction, out_weight):
    cos_table, sin_table = rotary_tables(positions, HD)
    rot_queries = (rotate_heads(queries, cos_table, sin_table, HD) * HD ** (-0.5)).astype(jnp.bfloat16)
    rot_keys = rotate_heads(key_rows, cos_table, sin_table, HD).astype(jnp.bfloat16)
    group_size = HEADS // KV_HEADS
    padding = jnp.zeros((WINDOW, KV_HEADS * HD), jnp.bfloat16)
    padded_keys = jnp.concatenate([padding, rot_keys], axis=0)
    padded_values = jnp.concatenate([padding, value_rows], axis=0)

    def attend(block_id):
        start = block_id * WINDOW
        query_part = lax.dynamic_slice_in_dim(rot_queries, start, WINDOW, 0).reshape(WINDOW, KV_HEADS, group_size, HD).astype(jnp.float32)
        key_part = lax.dynamic_slice_in_dim(padded_keys, start, 2 * WINDOW, 0).reshape(2 * WINDOW, KV_HEADS, HD).astype(jnp.float32)
        value_part = lax.dynamic_slice_in_dim(padded_values, start, 2 * WINDOW, 0).reshape(2 * WINDOW, KV_HEADS, HD).astype(jnp.float32)
        scores = jnp.einsum('qkgd,skd->kgqs', query_part, key_part)
        query_index = start + jnp.arange(WINDOW, dtype=jnp.int32)
        key_index = start - WINDOW + jnp.arange(2 * WINDOW, dtype=jnp.int32)
        gap_grid = query_index[:, None] - key_index[None, :]
        allowed = (gap_grid >= 0) & (gap_grid < WINDOW) & (key_index[None, :] >= 0)
        scores = jnp.where(allowed, scores, big_negative)
        row_max = lax.optimization_barrier(jnp.max(scores, axis=-1, keepdims=True))
        shifted = jnp.exp(scores - row_max)
        row_sum = lax.optimization_barrier(jnp.sum(shifted, axis=-1, keepdims=True))
        weights = (shifted / row_sum).astype(jnp.bfloat16)
        mixed = jnp.einsum('kgqs,skd->qkgd', weights.astype(jnp.float32), value_part)
        return mixed.astype(jnp.bfloat16).reshape(WINDOW, HEADS * HD)
    blocks = lax.map(attend, jnp.arange(TOKENS // WINDOW, dtype=jnp.int32))
    attended = blocks.reshape(TOKENS, HEADS * HD)
    rows_each = HEADS * HD // N_TENSOR
    attn_out = jnp.zeros((TOKENS, D), jnp.float32)
    for shard in range(N_TENSOR):
        piece = jnp.dot(attended[:, shard * rows_each:(shard + 1) * rows_each], out_weight[shard * rows_each:(shard + 1) * rows_each], preferred_element_type=jnp.float32)
        attn_out = attn_out + piece.astype(jnp.bfloat16).astype(jnp.float32)
    hidden_state = residual.astype(jnp.float32) + attn_out
    unit_dir = direction / jnp.sqrt(jnp.sum(direction * direction) + 1e-06)
    along = jnp.dot(hidden_state, unit_dir, precision=lax.Precision.HIGHEST)
    return (hidden_state - along[:, None] * unit_dir[None, :]).astype(jnp.bfloat16)
```

```python
import functools

import jax
import jax.numpy as jnp
from jax import lax
from jax.experimental import pallas as pl
from jax.experimental.pallas import tpu as pltpu
from jax.sharding import PartitionSpec as P

HD = 256
WINDOW = 1024


big_negative = -1e30


def shifted_2(value, axis, steps):
    count = lax.axis_size(axis)
    first, last = (max(0, -steps), min(count, count - steps))
    return lax.ppermute(value, axis, [(source, source + steps) for source in range(first, last)])


def rotary_tables(positions, head_dim):
    half_dim = head_dim // 2
    freqs = jnp.power(10000.0, -jnp.arange(half_dim, dtype=jnp.float32) * 2.0 / head_dim)
    angles = positions.astype(jnp.float32)[:, None] * freqs[None, :]
    return (jnp.cos(angles)[:, None, :], jnp.sin(angles)[:, None, :])


def rotate_heads(block, cos_table, sin_table, head_dim):
    row_count = block.shape[0]
    head_count = block.shape[1] // head_dim
    half_dim = head_dim // 2
    widened = block.reshape(row_count, head_count, head_dim).astype(jnp.float32)
    first_half = widened[:, :, :half_dim]
    second_half = widened[:, :, half_dim:]
    turned = jnp.concatenate(
        [
            first_half * cos_table - second_half * sin_table,
            second_half * cos_table + first_half * sin_table,
        ],
        axis=-1,
    )
    return turned.reshape(row_count, head_count * head_dim)


def body(queries, key_rows, value_rows, positions, residual, direction, out_weight):
    tokens_here = queries.shape[0]
    query_heads = queries.shape[1] // HD
    kv_heads = key_rows.shape[1] // HD
    group_size = query_heads // kv_heads
    span_blocks = WINDOW // tokens_here
    seq_index = lax.axis_index("seq")
    cos_table, sin_table = rotary_tables(positions, HD)
    rot_queries = (rotate_heads(queries, cos_table, sin_table, HD) * HD ** (-0.5)).astype(
        jnp.bfloat16
    )
    rot_keys = rotate_heads(key_rows, cos_table, sin_table, HD).astype(jnp.bfloat16)
    query_blocks = rot_queries.reshape(tokens_here, kv_heads, group_size, HD)
    own_scores = jnp.einsum(
        "qkgd,skd->kgqs",
        query_blocks,
        rot_keys.reshape(tokens_here, kv_heads, HD),
        preferred_element_type=jnp.float32,
    )
    earlier_keys = []
    earlier_values = []
    for distance in range(span_blocks, 0, -1):
        moved_keys, moved_values = shifted_2((rot_keys, value_rows), "seq", distance)
        earlier_keys.append(moved_keys)
        earlier_values.append(moved_values)
    far_keys = jnp.concatenate(earlier_keys, axis=0)
    far_values = jnp.concatenate(earlier_values, axis=0)
    far_scores = jnp.einsum(
        "qkgd,skd->kgqs",
        query_blocks,
        far_keys.reshape(-1, kv_heads, HD),
        preferred_element_type=jnp.float32,
    )
    scores = jnp.concatenate([far_scores, own_scores], axis=-1)
    query_index = seq_index * tokens_here + jnp.arange(tokens_here, dtype=jnp.int32)
    key_index = (seq_index - span_blocks) * tokens_here + jnp.arange(
        (span_blocks + 1) * tokens_here, dtype=jnp.int32
    )
    gap_grid = query_index[:, None] - key_index[None, :]
    allowed = (gap_grid >= 0) & (gap_grid < WINDOW) & (key_index[None, :] >= 0)
    scores = jnp.where(allowed, scores, big_negative)
    row_max = jnp.max(scores, axis=-1, keepdims=True)
    shifted = jnp.exp(scores - row_max)
    row_sum = jnp.sum(shifted, axis=-1, keepdims=True)
    weights = (shifted / row_sum).astype(jnp.bfloat16)
    every_value = jnp.concatenate([far_values, value_rows], axis=0).reshape(-1, kv_heads, HD)
    mixed = jnp.einsum("kgqs,skd->qkgd", weights, every_value, preferred_element_type=jnp.float32)
    attended = mixed.astype(jnp.bfloat16).reshape(tokens_here, query_heads * HD)
    partial_value = jnp.dot(attended, out_weight, preferred_element_type=jnp.float32)
    unit_dir = direction / jnp.sqrt(jnp.sum(direction * direction) + 1e-06)
    column_width = residual.shape[1]
    tensor_index = lax.axis_index("tensor")
    local_dir = lax.dynamic_slice_in_dim(unit_dir, tensor_index * column_width, column_width, 0)
    base_state = residual.astype(jnp.float32)
    rounded_terms = partial_value.astype(jnp.bfloat16).astype(jnp.float32)
    dot_terms = jnp.sum(rounded_terms * unit_dir[None, :], axis=1) + jnp.sum(
        base_state * local_dir[None, :], axis=1
    )
    along = lax.psum(dot_terms, "tensor")
    summed = lax.psum_scatter(
        partial_value.astype(jnp.bfloat16), "tensor", scatter_dimension=1, tiled=True
    ).astype(jnp.float32)
    hidden_state = base_state + summed
    ablated = (hidden_state - along[:, None] * local_dir[None, :]).astype(jnp.bfloat16)
    return ablated


BF = jnp.bfloat16
F32 = jnp.float32
MESH = pl.DeviceIdType.MESH

(K0A_2, V0A_2, K0B_1, V0B_1, K0A_1, V0A_1, K1A_2, V1A_2, Q3A_2, Q3B_2, Q3B_1, Q2B_1,
 O3A, L3A, O3B, L3B, OB_0, OB_1, LB_0, LB_1, OC_0, OC_1, LC_0, LC_1, SEQ_COPIES) = range(25)


def rot(x, cos, sin):
    x = x.astype(F32)
    a, b = x[:, :128], x[:, 128:]
    return jnp.concatenate([a * cos - b * sin, b * cos + a * sin], axis=1)


def attend(q, blocks, diag):
    scores = [
        lax.dot_general(k, q, (((1,), (1,)), ((), ())), preferred_element_type=F32)
        for k, _ in blocks
    ]
    if diag:
        s = scores[-1]
        key = lax.broadcasted_iota(jnp.int32, s.shape, 0)
        lane = lax.broadcasted_iota(jnp.int32, s.shape, 1)
        row = (lane // 256) * 128 + lane % 128
        scores[-1] = jnp.where(key <= row, s, big_negative)
    m = functools.reduce(jnp.maximum, [jnp.max(s, axis=0, keepdims=True) for s in scores])
    acc, l = 0.0, 0.0
    for s, (_, v) in zip(scores, blocks):
        p = jnp.exp(s - m)
        l = l + jnp.sum(p, axis=0, keepdims=True)
        acc = acc + lax.dot_general(
            v, p.astype(BF), (((0,), (0,)), ((), ())), preferred_element_type=F32
        )
    return acc, m, l


def merge(state, out, lse):
    acc, m, l = state
    top = jnp.maximum(m, lse)
    mine, other = jnp.exp(m - top), jnp.exp(lse - top)
    return acc * mine + out.astype(F32) * other, top, l * mine + other


def kernel(q_ref, k_ref, v_ref, cos_ref, sin_ref, res_ref, dir_ref, w_hbm, out_ref,
           wbuf, rq, rk, kv0, kv1, rq3, rq2, o_a, o_b2, o_b1, l_a, l_b2, l_b1,
           s_a, s_b2, s_c, t_a, t_b2, t_c, st_acc, st_ml, att, keep,
           a_send, a_recv, b_send, b_recv, al_send, al_recv,
           ssem, rsem, wsem, xs, xr, als, alr):
    s = lax.axis_index("seq")
    t = lax.axis_index("tensor")
    core = t % 2
    x_here = t // 2
    x_other = 1 - x_here
    core_peer = t + 1 - 2 * core
    x_peer = (t + 2) % 4
    half = wbuf.shape[2]
    width = half // 2

    def w_copy(i, x):
        cols = pl.ds(pl.multiple_of(x * half, 128), half)
        return pltpu.make_async_copy(w_hbm.at[:, cols], wbuf.at[i], wsem.at[i])

    w_copies = [w_copy(0, x_other), w_copy(1, x_here)]
    for c in w_copies:
        c.start()

    barrier = pltpu.get_barrier_semaphore()
    for j in (1, 2, 3):
        pl.semaphore_signal(barrier, inc=1, device_id={"seq": (s + j) % 4}, device_id_type=MESH)
        pl.semaphore_signal(barrier, inc=1, device_id={"tensor": (t + j) % 4}, device_id_type=MESH)
    pl.semaphore_wait(barrier, 6)

    def to(dev, src, dst, si, ri=None):
        ri = si if ri is None else ri
        return pltpu.make_async_remote_copy(
            src_ref=src, dst_ref=dst, send_sem=ssem.at[si], recv_sem=rsem.at[ri],
            device_id={"seq": dev}, device_id_type=MESH)

    def vcol(g):
        return v_ref.at[:, 256 * g:256 * g + 256]

    copies = {
        V0A_2: to(2, vcol(0), kv0.at[1], V0A_2),
        K0A_2: to(2, rk.at[0], kv0.at[0], K0A_2),
        V0B_1: to(1, vcol(1), kv0.at[3], V0B_1),
        K0B_1: to(1, rk.at[1], kv0.at[2], K0B_1),
        V0A_1: to(1, vcol(0), kv0.at[1], V0A_1),
        K0A_1: to(1, rk.at[0], kv0.at[0], K0A_1),
        V1A_2: to(2, vcol(0), kv1.at[1], V1A_2),
        K1A_2: to(2, rk.at[0], kv1.at[0], K1A_2),
        Q3A_2: to(2, rq.at[0], rq3.at[0], Q3A_2),
        Q3B_2: to(2, rq.at[1], rq3.at[1], Q3B_2),
        Q3B_1: to(1, rq.at[1], rq3.at[1], Q3B_1),
        Q2B_1: to(1, rq.at[1], rq2, Q2B_1),
        O3A: to(3, s_a, o_a, O3A),
        L3A: to(3, t_a, l_a, L3A),
        O3B: to(3, s_b2, o_b2, O3B),
        L3B: to(3, t_b2, l_b2, L3B),
    }
    for c in (0, 1):
        copies[OB_0 + c] = to(2, s_c.at[0, c], o_b1.at[c], OB_0 + c)
        copies[LB_0 + c] = to(2, t_c.at[0, c], l_b1.at[c], LB_0 + c)
        copies[OC_0 + c] = to(3, s_c.at[1, c], o_b1.at[c], OC_0 + c, OB_0 + c)
        copies[LC_0 + c] = to(3, t_c.at[1, c], l_b1.at[c], LC_0 + c, LB_0 + c)

    def start(*names):
        for n in names:
            copies[n].start()

    def recv(*names):
        for n in names:
            copies[n].wait_recv()

    def sent(*names):
        for n in names:
            copies[n].wait_send()

    @pl.when(s == 0)
    def _():
        start(V0A_2)

    @pl.when(s == 1)
    def _():
        start(V1A_2)

    cos, sin = cos_ref[...], sin_ref[...]
    for g in (0, 1):
        rk[g] = rot(k_ref[:, 256 * g:256 * g + 256], cos, sin).astype(BF)

    @pl.when(s == 0)
    def _():
        start(K0A_2, V0B_1, K0B_1, V0A_1, K0A_1)

    @pl.when(s == 1)
    def _():
        start(K1A_2)

    for g in (1, 0):
        for h in (0, 1):
            at = 256 * (2 * g + h)
            r = (rot(q_ref[:, at:at + 256], cos, sin) * HD ** (-0.5)).astype(BF)
            for c in (0, 1):
                rq[g, 256 * c + 128 * h:256 * c + 128 * h + 128, :] = r[128 * c:128 * c + 128]

    @pl.when(s == 3)
    def _():
        start(Q3B_1, Q3A_2, Q3B_2)

    @pl.when(s == 2)
    def _():
        start(Q2B_1)

    def own(g):
        return rk[g], v_ref[:, 256 * g:256 * g + 256]

    def first(g):
        return kv0[2 * g], kv0[2 * g + 1]

    def second():
        return kv1[0], kv1[1]

    def put(g, state, chunks):
        acc, _, l = state
        out = acc / l
        for i, c in enumerate(chunks):
            for h in (0, 1):
                at = 256 * i + 128 * h
                col = 256 * (2 * g + h)
                att[128 * c:128 * c + 128, col:col + 256] = out[:, at:at + 128].T.astype(BF)

    def send_state(state, out_to, lse_to, *names):
        acc, m, l = state
        out_to[...] = (acc / l).astype(BF)
        lse_to[...] = jnp.broadcast_to(m + jnp.log(l), lse_to.shape)
        start(*names)

    def hold(state):
        acc, m, l = state
        st_acc[...] = acc
        st_ml[0:8] = jnp.broadcast_to(m, (8, 512))
        st_ml[8:16] = jnp.broadcast_to(l, (8, 512))

    @pl.when(s == 0)
    def _():
        for g in (0, 1):
            put(g, attend(rq[g], [own(g)], True), (0, 1))

    @pl.when(s == 1)
    def _():
        recv(Q2B_1, V0B_1, K0B_1)
        for c in (0, 1):
            state = attend(rq2[256 * c:256 * c + 256, :], [first(1), own(1)], False)
            send_state(state, s_c.at[0, c], t_c.at[0, c], OB_0 + c, LB_0 + c)
        recv(Q3B_1)
        for c in (0, 1):
            state = attend(rq3[1, 256 * c:256 * c + 256, :], [first(1), own(1)], False)
            send_state(state, s_c.at[1, c], t_c.at[1, c], OC_0 + c, LC_0 + c)
        put(1, attend(rq[1], [first(1), own(1)], True), (0, 1))
        recv(V0A_1, K0A_1)
        put(0, attend(rq[0], [first(0), own(0)], True), (0, 1))

    @pl.when(s == 2)
    def _():
        hold(attend(rq[1], [own(1)], True))
        recv(Q3A_2, Q3B_2)
        send_state(attend(rq3[1], [own(1)], False), s_b2, t_b2, O3B, L3B)
        recv(V0A_2, K0A_2, V1A_2, K1A_2)
        send_state(attend(rq3[0], [first(0), second(), own(0)], False), s_a, t_a, O3A, L3A)
        put(0, attend(rq[0], [first(0), second(), own(0)], True), (0, 1))

    @pl.when(s == 3)
    def _():
        state = attend(rq[1], [own(1)], True)
        recv(O3B, L3B)
        hold(merge(state, o_b2[...], l_b2[0:1]))
        state = attend(rq[0], [own(0)], True)
        recv(O3A, L3A)
        put(0, merge(state, o_a[...], l_a[0:1]), (0, 1))

    def x_copy(src, dst, i, dev):
        return pltpu.make_async_remote_copy(
            src_ref=src, dst_ref=dst, send_sem=xs.at[i], recv_sem=xr.at[i],
            device_id={"tensor": dev}, device_id_type=MESH)

    direction = dir_ref[...]
    scale = 1.0 / jnp.sqrt(jnp.sum(direction * direction, axis=1, keepdims=True) + 1e-06)

    def dir_half(x):
        return dir_ref[:, pl.ds(pl.multiple_of(x * half, 128), half)] * scale

    unit_halves = [dir_half(x_other), dir_half(x_here)]
    local_dir = jnp.where(core == 0, unit_halves[1][:, :width], unit_halves[1][:, width:])
    first_core = core == 0
    waits = []
    a_copies, b_copies, al_copies = {}, {}, {}
    for c in (0, 1):
        rows = slice(128 * c, 128 * c + 128)

        @pl.when(s >= 2)
        def _(c=c):
            recv(OB_0 + c, LB_0 + c)
            lanes = slice(256 * c, 256 * c + 256)
            state = (st_acc[:, lanes], st_ml[0:1, lanes], st_ml[8:9, lanes])
            put(1, merge(state, o_b1[c], l_b1[c, 0:1]), (c,))

        dots = 0.0
        for i in (0, 1):
            if c == 0:
                w_copies[i].wait()
            part = jnp.dot(att[rows, :], wbuf[i], preferred_element_type=F32)
            dots = dots + jnp.sum(part * unit_halves[i], axis=1, keepdims=True)
            low, high = part[:, :width], part[:, width:]
            a_send[c, i] = jnp.where(first_core, high, low).astype(BF)
            a_copies[c, i] = x_copy(a_send.at[c, i], a_recv.at[c, i], 2 * c + i, core_peer)
            a_copies[c, i].start()
            keep[i, rows, :] = jnp.where(first_core, low, high)
        a_copies[c, 0].wait_recv()
        b_send[c] = (keep[0, rows, :] + a_recv[c, 0].astype(F32)).astype(BF)
        b_copies[c] = x_copy(b_send.at[c], b_recv.at[c], 4 + c, x_peer)
        b_copies[c].start()
        dots = dots + jnp.sum(res_ref[rows, :].astype(F32) * local_dir, axis=1, keepdims=True)
        al_send[c] = jnp.broadcast_to(dots, (128, 128)).T[0:8]
        for j in (1, 2, 3):
            i = 3 * c + j - 1
            al_copies[c, j] = pltpu.make_async_remote_copy(
                src_ref=al_send.at[c], dst_ref=al_recv.at[c, j - 1],
                send_sem=als.at[i], recv_sem=alr.at[i],
                device_id={"tensor": (t + j) % 4}, device_id_type=MESH)
            al_copies[c, j].start()

    for c in (0, 1):
        rows = slice(128 * c, 128 * c + 128)
        along = al_send[c]
        for j in (1, 2, 3):
            al_copies[c, j].wait_recv()
            along = along + al_recv[c, j - 1]
        along = jnp.broadcast_to(along[0:1], (128, 128)).T[:, 0:1]
        a_copies[c, 1].wait_recv()
        hidden = res_ref[rows, :].astype(F32) + keep[1, rows, :] + a_recv[c, 1].astype(F32)
        hidden = hidden - along * local_dir
        b_copies[c].wait_recv()
        out_ref[rows, :] = (hidden + b_recv[c].astype(F32)).astype(BF)

    for c in (0, 1):
        a_copies[c, 0].wait_send()
        a_copies[c, 1].wait_send()
        b_copies[c].wait_send()
        for j in (1, 2, 3):
            al_copies[c, j].wait_send()

    @pl.when(s == 0)
    def _():
        sent(V0A_2, K0A_2, V0B_1, K0B_1, V0A_1, K0A_1)

    @pl.when(s == 1)
    def _():
        sent(V1A_2, K1A_2, OB_0, OB_1, LB_0, LB_1, OC_0, OC_1, LC_0, LC_1)

    @pl.when(s == 2)
    def _():
        sent(Q2B_1, O3A, L3A, O3B, L3B)

    @pl.when(s == 3)
    def _():
        sent(Q3B_1, Q3A_2, Q3B_2)


def fused_body(queries, key_rows, value_rows, positions, residual, direction, out_weight):
    cos, sin = rotary_tables(positions, HD)
    cos, sin = cos[:, 0, :], sin[:, 0, :]
    width = residual.shape[1]
    vmem = pl.BlockSpec(memory_space=pltpu.VMEM)
    dma = pltpu.SemaphoreType.DMA
    return pl.pallas_call(
        kernel,
        out_shape=jax.ShapeDtypeStruct(residual.shape, BF),
        in_specs=[vmem] * 7 + [pl.BlockSpec(memory_space=pl.ANY)],
        out_specs=vmem,
        scratch_shapes=[
            pltpu.VMEM((2, out_weight.shape[0], 2 * width), BF),
            pltpu.VMEM((2, 512, 256), BF),
            pltpu.VMEM((2, 256, 256), BF),
            pltpu.VMEM((4, 256, 256), BF),
            pltpu.VMEM((2, 256, 256), BF),
            pltpu.VMEM((2, 512, 256), BF),
            pltpu.VMEM((512, 256), BF),
            pltpu.VMEM((256, 512), BF),
            pltpu.VMEM((256, 512), BF),
            pltpu.VMEM((2, 256, 256), BF),
            pltpu.VMEM((8, 512), F32),
            pltpu.VMEM((8, 512), F32),
            pltpu.VMEM((2, 8, 256), F32),
            pltpu.VMEM((256, 512), BF),
            pltpu.VMEM((256, 512), BF),
            pltpu.VMEM((2, 2, 256, 256), BF),
            pltpu.VMEM((8, 512), F32),
            pltpu.VMEM((8, 512), F32),
            pltpu.VMEM((2, 2, 8, 256), F32),
            pltpu.VMEM((256, 512), F32),
            pltpu.VMEM((16, 512), F32),
            pltpu.VMEM((256, 1024), BF),
            pltpu.VMEM((2, 256, width), F32),
            pltpu.VMEM((2, 2, 128, width), BF),
            pltpu.VMEM((2, 2, 128, width), BF),
            pltpu.VMEM((2, 128, width), BF),
            pltpu.VMEM((2, 128, width), BF),
            pltpu.VMEM((2, 8, 128), F32),
            pltpu.VMEM((2, 3, 8, 128), F32),
            dma((SEQ_COPIES,)),
            dma((SEQ_COPIES,)),
            dma((2,)),
            dma((6,)),
            dma((6,)),
            dma((6,)),
            dma((6,)),
        ],
        compiler_params=pltpu.CompilerParams(
            collective_id=0, has_side_effects=True, vmem_limit_bytes=48 * 1024 * 1024
        ),
    )(queries, key_rows, value_rows, cos, sin, residual, direction[None, :], out_weight)


def device_body(*args):
    queries, key_rows, _, _, residual, direction, _ = args
    fits = (
        lax.axis_size("seq") == 4
        and lax.axis_size("tensor") == 4
        and queries.shape == (256, 1024)
        and key_rows.shape == (256, 512)
        and residual.shape[1] * 4 == direction.shape[0]
        and residual.shape[1] % 64 == 0
        and WINDOW == 1024
    )
    return fused_body(*args) if fits else body(*args)


def solution(mesh):
    return jax.shard_map(
        device_body,
        mesh=mesh,
        in_specs=(
            P(("groups", "seq"), "tensor"),
            P(("groups", "seq"), "tensor"),
            P(("groups", "seq"), "tensor"),
            P(("groups", "seq")),
            P(("groups", "seq"), "tensor"),
            P("groups"),
            P("tensor", None),
        ),
        out_specs=P(("groups", "seq"), "tensor"),
        check_vma=False,
    )
```

```python
import functools

import jax
import jax.numpy as jnp
from jax import lax
from jax.experimental import pallas as pl
from jax.experimental.pallas import tpu as pltpu
from jax.sharding import PartitionSpec as P

HD = 256
WINDOW = 1024


big_negative = -1e30


def shifted_2(value, axis, steps):
    count = lax.axis_size(axis)
    first, last = (max(0, -steps), min(count, count - steps))
    return lax.ppermute(value, axis, [(source, source + steps) for source in range(first, last)])


def rotary_tables(positions, head_dim):
    half_dim = head_dim // 2
    freqs = jnp.power(10000.0, -jnp.arange(half_dim, dtype=jnp.float32) * 2.0 / head_dim)
    angles = positions.astype(jnp.float32)[:, None] * freqs[None, :]
    return (jnp.cos(angles)[:, None, :], jnp.sin(angles)[:, None, :])


def rotate_heads(block, cos_table, sin_table, head_dim):
    row_count = block.shape[0]
    head_count = block.shape[1] // head_dim
    half_dim = head_dim // 2
    widened = block.reshape(row_count, head_count, head_dim).astype(jnp.float32)
    first_half = widened[:, :, :half_dim]
    second_half = widened[:, :, half_dim:]
    turned = jnp.concatenate(
        [
            first_half * cos_table - second_half * sin_table,
            second_half * cos_table + first_half * sin_table,
        ],
        axis=-1,
    )
    return turned.reshape(row_count, head_count * head_dim)


def body(queries, key_rows, value_rows, positions, residual, direction, out_weight):
    tokens_here = queries.shape[0]
    query_heads = queries.shape[1] // HD
    kv_heads = key_rows.shape[1] // HD
    group_size = query_heads // kv_heads
    span_blocks = WINDOW // tokens_here
    seq_index = lax.axis_index("seq")
    cos_table, sin_table = rotary_tables(positions, HD)
    rot_queries = (rotate_heads(queries, cos_table, sin_table, HD) * HD ** (-0.5)).astype(
        jnp.bfloat16
    )
    rot_keys = rotate_heads(key_rows, cos_table, sin_table, HD).astype(jnp.bfloat16)
    query_blocks = rot_queries.reshape(tokens_here, kv_heads, group_size, HD)
    own_scores = jnp.einsum(
        "qkgd,skd->kgqs",
        query_blocks,
        rot_keys.reshape(tokens_here, kv_heads, HD),
        preferred_element_type=jnp.float32,
    )
    earlier_keys = []
    earlier_values = []
    for distance in range(span_blocks, 0, -1):
        moved_keys, moved_values = shifted_2((rot_keys, value_rows), "seq", distance)
        earlier_keys.append(moved_keys)
        earlier_values.append(moved_values)
    far_keys = jnp.concatenate(earlier_keys, axis=0)
    far_values = jnp.concatenate(earlier_values, axis=0)
    far_scores = jnp.einsum(
        "qkgd,skd->kgqs",
        query_blocks,
        far_keys.reshape(-1, kv_heads, HD),
        preferred_element_type=jnp.float32,
    )
    scores = jnp.concatenate([far_scores, own_scores], axis=-1)
    query_index = seq_index * tokens_here + jnp.arange(tokens_here, dtype=jnp.int32)
    key_index = (seq_index - span_blocks) * tokens_here + jnp.arange(
        (span_blocks + 1) * tokens_here, dtype=jnp.int32
    )
    gap_grid = query_index[:, None] - key_index[None, :]
    allowed = (gap_grid >= 0) & (gap_grid < WINDOW) & (key_index[None, :] >= 0)
    scores = jnp.where(allowed, scores, big_negative)
    row_max = jnp.max(scores, axis=-1, keepdims=True)
    shifted = jnp.exp(scores - row_max)
    row_sum = jnp.sum(shifted, axis=-1, keepdims=True)
    weights = (shifted / row_sum).astype(jnp.bfloat16)
    every_value = jnp.concatenate([far_values, value_rows], axis=0).reshape(-1, kv_heads, HD)
    mixed = jnp.einsum("kgqs,skd->qkgd", weights, every_value, preferred_element_type=jnp.float32)
    attended = mixed.astype(jnp.bfloat16).reshape(tokens_here, query_heads * HD)
    partial_value = jnp.dot(attended, out_weight, preferred_element_type=jnp.float32)
    unit_dir = direction / jnp.sqrt(jnp.sum(direction * direction) + 1e-06)
    column_width = residual.shape[1]
    tensor_index = lax.axis_index("tensor")
    local_dir = lax.dynamic_slice_in_dim(unit_dir, tensor_index * column_width, column_width, 0)
    base_state = residual.astype(jnp.float32)
    rounded_terms = partial_value.astype(jnp.bfloat16).astype(jnp.float32)
    dot_terms = jnp.sum(rounded_terms * unit_dir[None, :], axis=1) + jnp.sum(
        base_state * local_dir[None, :], axis=1
    )
    along = lax.psum(dot_terms, "tensor")
    summed = lax.psum_scatter(
        partial_value.astype(jnp.bfloat16), "tensor", scatter_dimension=1, tiled=True
    ).astype(jnp.float32)
    hidden_state = base_state + summed
    ablated = (hidden_state - along[:, None] * local_dir[None, :]).astype(jnp.bfloat16)
    return ablated


BF = jnp.bfloat16
F32 = jnp.float32
MESH = pl.DeviceIdType.MESH

def rot(x, cos, sin):
    x = x.astype(F32)
    a, b = x[:, :128], x[:, 128:]
    return jnp.concatenate([a * cos - b * sin, b * cos + a * sin], axis=1)


def attend(q, blocks, diag):
    scores = [
        lax.dot_general(k, q, (((1,), (1,)), ((), ())), preferred_element_type=F32)
        for k, _ in blocks
    ]
    if diag:
        s = scores[-1]
        key = lax.broadcasted_iota(jnp.int32, s.shape, 0)
        lane = lax.broadcasted_iota(jnp.int32, s.shape, 1)
        row = (lane // 256) * 128 + lane % 128
        scores[-1] = jnp.where(key <= row, s, big_negative)
    m = functools.reduce(jnp.maximum, [jnp.max(s, axis=0, keepdims=True) for s in scores])
    acc, l = 0.0, 0.0
    for s, (_, v) in zip(scores, blocks):
        p = jnp.exp(s - m)
        l = l + jnp.sum(p, axis=0, keepdims=True)
        acc = acc + lax.dot_general(
            v, p.astype(BF), (((0,), (0,)), ((), ())), preferred_element_type=F32
        )
    return acc, m, l


def merge(state, out, lse):
    acc, m, l = state
    top = jnp.maximum(m, lse)
    mine, other = jnp.exp(m - top), jnp.exp(lse - top)
    return acc * mine + out.astype(F32) * other, top, l * mine + other


def kernel(pos_hbm, freq_ref, q_hbm, k_hbm, v_hbm, res_hbm, dir_hbm, w_hbm, out_ref,
           pos, direction, q, k, v, res, wbuf, wt, ucol, rq, rk, kv0, kv1, rq3, rq2,
           o_a, o_b2, o_b1, l_a, l_b2, l_b1, s_a, s_b2, s_c, t_a, t_b2, t_c,
           st_acc, st_ml, att, keep, a_send, a_recv, b_send, b_recv, al_send, al_recv,
           lsem, ssem, rsem, xs, xr, als, alr):
    s = lax.axis_index("seq")
    t = lax.axis_index("tensor")
    core = t % 2
    x_here = t // 2
    x_other = 1 - x_here
    core_peer = t + 1 - 2 * core
    x_peer = (t + 2) % 4
    half = wbuf.shape[2]
    width = half // 2

    local = {}

    def fetch(name, src, dst):
        local[name] = pltpu.make_async_copy(src, dst, lsem.at[len(local)])
        local[name].start()

    fetch("pos", pos_hbm, pos)
    fetch("k", k_hbm, k)
    fetch("q", q_hbm, q)
    fetch("v", v_hbm, v)
    for i, x in enumerate((x_other, x_here)):
        cols = pl.ds(pl.multiple_of(x * half, 128), half)
        fetch(i, w_hbm.at[:, cols], wbuf.at[i])
    fetch("dir", dir_hbm, direction)
    fetch("res", res_hbm, res)

    barrier = pltpu.get_barrier_semaphore()
    for j in (1, 2, 3):
        pl.semaphore_signal(barrier, inc=1, device_id={"seq": (s + j) % 4}, device_id_type=MESH)
        pl.semaphore_signal(barrier, inc=1, device_id={"tensor": (t + j) % 4}, device_id_type=MESH)
    pl.semaphore_wait(barrier, 6)

    copies, index = {}, {}

    def add(name, dev, src, dst, lands_as=None):
        i = index[name] = len(index)
        copies[name] = pltpu.make_async_remote_copy(
            src_ref=src, dst_ref=dst, send_sem=ssem.at[i],
            recv_sem=rsem.at[i if lands_as is None else index[lands_as]],
            device_id={"seq": dev}, device_id_type=MESH)

    for g, name in ((0, "a"), (1, "b")):
        cols = slice(256 * g, 256 * g + 256)
        add("v0" + name + "1", 1, v_hbm.at[:, cols], kv0.at[2 * g + 1])
        add("k0" + name + "1", 1, rk.at[g], kv0.at[2 * g])
    add("v0a2", 2, v_hbm.at[:, 0:256], kv0.at[1])
    add("k0a2", 2, rk.at[0], kv0.at[0])
    add("v1a2", 2, v_hbm.at[:, 0:256], kv1.at[1])
    add("k1a2", 2, rk.at[0], kv1.at[0])
    add("q3a2", 2, rq.at[0], rq3.at[0])
    add("o3b", 3, s_b2, o_b2)
    add("l3b", 3, t_b2, l_b2)
    for c in (0, 1):
        rows = slice(256 * c, 256 * c + 256)
        n = str(c)
        add("q3b2" + n, 2, rq.at[1, rows], rq3.at[1, rows])
        add("f3b1" + n, 1, rq3.at[1, rows], rq3.at[1, rows])
        add("q2b1" + n, 1, rq.at[1, rows], rq2.at[rows])
        add("o3a" + n, 3, s_a.at[c], o_a.at[c])
        add("l3a" + n, 3, t_a.at[c], l_a.at[c])
        add("o2b" + n, 2, s_c.at[0, c], o_b1.at[c])
        add("l2b" + n, 2, t_c.at[0, c], l_b1.at[c])
        add("o3c" + n, 3, s_c.at[1, c], o_b1.at[c], "o2b" + n)
        add("l3c" + n, 3, t_c.at[1, c], l_b1.at[c], "l2b" + n)

    def start(*names):
        for n in names:
            copies[n].start()

    def recv(*names):
        for n in names:
            copies[n].wait_recv()

    def sent(*names):
        for n in names:
            copies[n].wait_send()

    @pl.when(s == 0)
    def _():
        start("v0b1")

    @pl.when(s == 1)
    def _():
        start("v1a2")

    local["pos"].wait()
    freqs = freq_ref[...]
    tokens = pos[...].astype(F32).reshape(1, 256)
    angles = jnp.concatenate(
        [jnp.broadcast_to(tokens[:, 128 * c:128 * c + 128], (128, 128)).T for c in (0, 1)], axis=0
    ) * freqs
    cos, sin = jnp.cos(angles), jnp.sin(angles)
    local["k"].wait()
    for g in (1, 0):
        rk[g] = rot(k[:, 256 * g:256 * g + 256], cos, sin).astype(BF)

    @pl.when(s == 0)
    def _():
        start("k0b1")

    @pl.when(s == 1)
    def _():
        start("k1a2")

    local["q"].wait()
    for g in (1, 0):
        for h in (0, 1):
            at = 256 * (2 * g + h)
            r = (rot(q[:, at:at + 256], cos, sin) * HD ** (-0.5)).astype(BF)
            for c in (0, 1):
                rq[g, 256 * c + 128 * h:256 * c + 128 * h + 128, :] = r[128 * c:128 * c + 128]
        if g == 1:
            @pl.when(s == 3)
            def _():
                start("q3b20")

            @pl.when(s == 2)
            def _():
                start("q2b10")

    local["v"].wait()

    def own(g):
        return rk[g], v[:, 256 * g:256 * g + 256]

    def first(g):
        return kv0[2 * g], kv0[2 * g + 1]

    def second():
        return kv1[0], kv1[1]

    def put(g, state, chunks):
        acc, _, l = state
        out = (acc / l).astype(BF)
        for i, c in enumerate(chunks):
            for h in (0, 1):
                at = 256 * i + 128 * h
                row = 256 * (2 * g + h)
                att[c, row:row + 256, :] = out[:, at:at + 128]

    def send_state(state, out_to, lse_to, *names):
        acc, m, l = state
        out_to[...] = (acc / l).astype(BF)
        lse_to[...] = jnp.broadcast_to(m + jnp.log(l), lse_to.shape)
        start(*names)

    def hold(g, state):
        acc, m, l = state
        st_acc[g] = acc
        st_ml[g, 0:8] = jnp.broadcast_to(m, (8, 512))
        st_ml[g, 8:16] = jnp.broadcast_to(l, (8, 512))

    def held(g, c):
        lanes = slice(256 * c, 256 * c + 256)
        return st_acc[g, :, lanes], st_ml[g, 0:1, lanes], st_ml[g, 8:9, lanes]

    def prepare_weight():
        local["dir"].wait()
        whole = direction[...].reshape(1, 2 * half)
        scale = 1.0 / jnp.sqrt(jnp.sum(whole * whole, axis=1, keepdims=True) + 1e-06)
        for i, x in enumerate((x_other, x_here)):
            local[i].wait()
            mine = jnp.where(x == 0, whole[:, :half], whole[:, half:]) * scale
            for j in range(half // 128):
                at = slice(128 * j, 128 * j + 128)
                wt[i, at, :] = wbuf[i, :, at].T
                ucol[i, at, :] = jnp.broadcast_to(mine[:, at], (128, 128)).T

    @pl.when(s == 0)
    def _():
        put(1, attend(rq[1], [own(1)], True), (0, 1))
        sent("v0b1")
        start("v0a2")
        put(0, attend(rq[0], [own(0)], True), (0, 1))
        sent("k0b1")
        start("k0a2")

    @pl.when(s == 2)
    def _():
        recv("q3b20")
        start("f3b10")
        sent("q2b10")
        start("q2b11")
        hold(1, attend(rq[1], [own(1)], True))
        recv("q3b21")
        start("f3b11")
        send_state(attend(rq3[1], [own(1)], False), s_b2, t_b2, "o3b", "l3b")

    @pl.when(s == 3)
    def _():
        sent("q3b20")
        start("q3b21")
        hold(0, attend(rq[0], [own(0)], True))
        sent("q3b21")
        start("q3a2")
        hold(1, attend(rq[1], [own(1)], True))

    prepare_weight()

    @pl.when(s == 0)
    def _():
        sent("v0a2")
        start("v0a1")
        sent("k0a2")
        start("k0a1")

    @pl.when(s == 1)
    def _():
        recv("v0b1", "k0b1")
        for c in (0, 1):
            n = str(c)
            rows = slice(256 * c, 256 * c + 256)
            recv("q2b1" + n)
            state = attend(rq2[rows, :], [first(1), own(1)], False)
            send_state(state, s_c.at[0, c], t_c.at[0, c], "o2b" + n, "l2b" + n)
            recv("f3b1" + n)
            state = attend(rq3[1, rows, :], [first(1), own(1)], False)
            send_state(state, s_c.at[1, c], t_c.at[1, c], "o3c" + n, "l3c" + n)
        put(1, attend(rq[1], [first(1), own(1)], True), (0, 1))
        recv("v0a1", "k0a1")
        put(0, attend(rq[0], [first(0), own(0)], True), (0, 1))

    @pl.when(s == 2)
    def _():
        recv("v1a2", "k1a2", "q3a2", "v0a2", "k0a2")
        for c in (0, 1):
            n = str(c)
            rows = slice(256 * c, 256 * c + 256)
            state = attend(rq3[0, rows, :], [first(0), second(), own(0)], False)
            send_state(state, s_a.at[c], t_a.at[c], "o3a" + n, "l3a" + n)
        put(0, attend(rq[0], [first(0), second(), own(0)], True), (0, 1))

    @pl.when(s == 3)
    def _():
        recv("o3b", "l3b")
        acc, m, l = st_acc[1], st_ml[1, 0:1], st_ml[1, 8:9]
        hold(1, merge((acc, m, l), o_b2[...], l_b2[0:1]))

    def x_copy(src, dst, i, dev):
        return pltpu.make_async_remote_copy(
            src_ref=src, dst_ref=dst, send_sem=xs.at[i], recv_sem=xr.at[i],
            device_id={"tensor": dev}, device_id_type=MESH)

    local["res"].wait()
    first_core = core == 0
    local_dir = jnp.where(first_core, ucol[1, :width], ucol[1, width:])
    a_copies, b_copies, al_copies = {}, {}, {}
    for c in (0, 1):
        lanes = slice(128 * c, 128 * c + 128)

        @pl.when(s == 3)
        def _(c=c):
            recv("o3a" + str(c), "l3a" + str(c))
            put(0, merge(held(0, c), o_a[c], l_a[c, 0:1]), (c,))

        @pl.when(s >= 2)
        def _(c=c):
            recv("o2b" + str(c), "l2b" + str(c))
            put(1, merge(held(1, c), o_b1[c], l_b1[c, 0:1]), (c,))

        dots = jnp.sum(res[:, lanes].astype(F32) * local_dir, axis=0, keepdims=True)
        for i in (0, 1):
            part = jnp.dot(wt[i], att[c], preferred_element_type=F32)
            dots = dots + jnp.sum(part * ucol[i], axis=0, keepdims=True)
            low, high = part[:width], part[width:]
            a_send[c, i] = jnp.where(first_core, high, low).astype(BF)
            a_copies[c, i] = x_copy(a_send.at[c, i], a_recv.at[c, i], 2 * c + i, core_peer)
            a_copies[c, i].start()
            keep[c, i] = jnp.where(first_core, low, high)
            if i == 0:
                a_copies[c, 0].wait_recv()
                b_send[c] = (keep[c, 0] + a_recv[c, 0].astype(F32)).astype(BF)
                b_copies[c] = x_copy(b_send.at[c], b_recv.at[c], 4 + c, x_peer)
                b_copies[c].start()
        al_send[c] = jnp.broadcast_to(dots, (8, 128))
        for j in (1, 2, 3):
            i = 3 * c + j - 1
            al_copies[c, j] = pltpu.make_async_remote_copy(
                src_ref=al_send.at[c], dst_ref=al_recv.at[c, j - 1],
                send_sem=als.at[i], recv_sem=alr.at[i],
                device_id={"tensor": (t + j) % 4}, device_id_type=MESH)
            al_copies[c, j].start()

    for c in (0, 1):
        lanes = slice(128 * c, 128 * c + 128)
        along = al_send[c]
        for j in (1, 2, 3):
            al_copies[c, j].wait_recv()
            along = along + al_recv[c, j - 1]
        a_copies[c, 1].wait_recv()
        hidden = res[:, lanes].astype(F32) + keep[c, 1] + a_recv[c, 1].astype(F32)
        keep[c, 1] = hidden - along[0:1] * local_dir
        b_copies[c].wait_recv()
        out_ref[:, lanes] = (keep[c, 1] + b_recv[c].astype(F32)).astype(BF)

    for c in (0, 1):
        a_copies[c, 0].wait_send()
        a_copies[c, 1].wait_send()
        b_copies[c].wait_send()
        for j in (1, 2, 3):
            al_copies[c, j].wait_send()

    @pl.when(s == 0)
    def _():
        sent("v0a1", "k0a1")

    @pl.when(s == 1)
    def _():
        sent("v1a2", "k1a2", "o2b0", "l2b0", "o2b1", "l2b1", "o3c0", "l3c0", "o3c1", "l3c1")

    @pl.when(s == 2)
    def _():
        sent("q2b11", "f3b10", "f3b11", "o3b", "l3b", "o3a0", "l3a0", "o3a1", "l3a1")

    @pl.when(s == 3)
    def _():
        sent("q3a2")


def fused_body(queries, key_rows, value_rows, positions, residual, direction, out_weight):
    freqs = jnp.power(10000.0, -jnp.arange(HD // 2, dtype=F32) * 2.0 / HD)[None, :]
    rows, width = residual.shape
    depth = out_weight.shape[0]
    vmem = pl.BlockSpec(memory_space=pltpu.VMEM)
    anywhere = pl.BlockSpec(memory_space=pl.ANY)
    dma = pltpu.SemaphoreType.DMA
    out = pl.pallas_call(
        kernel,
        out_shape=jax.ShapeDtypeStruct((width, rows), BF),
        in_specs=[anywhere, vmem] + [anywhere] * 6,
        out_specs=vmem,
        scratch_shapes=[
            pltpu.VMEM(positions.shape, jnp.int32),
            pltpu.VMEM(direction.shape, F32),
            pltpu.VMEM(queries.shape, BF),
            pltpu.VMEM(key_rows.shape, BF),
            pltpu.VMEM(value_rows.shape, BF),
            pltpu.VMEM((width, rows), BF),
            pltpu.VMEM((2, depth, 2 * width), BF),
            pltpu.VMEM((2, 2 * width, depth), BF),
            pltpu.VMEM((2, 2 * width, 128), F32),
            pltpu.VMEM((2, 512, 256), BF),
            pltpu.VMEM((2, 256, 256), BF),
            pltpu.VMEM((4, 256, 256), BF),
            pltpu.VMEM((2, 256, 256), BF),
            pltpu.VMEM((2, 512, 256), BF),
            pltpu.VMEM((512, 256), BF),
            pltpu.VMEM((2, 256, 256), BF),
            pltpu.VMEM((256, 512), BF),
            pltpu.VMEM((2, 256, 256), BF),
            pltpu.VMEM((2, 8, 256), F32),
            pltpu.VMEM((8, 512), F32),
            pltpu.VMEM((2, 8, 256), F32),
            pltpu.VMEM((2, 256, 256), BF),
            pltpu.VMEM((256, 512), BF),
            pltpu.VMEM((2, 2, 256, 256), BF),
            pltpu.VMEM((2, 8, 256), F32),
            pltpu.VMEM((8, 512), F32),
            pltpu.VMEM((2, 2, 8, 256), F32),
            pltpu.VMEM((2, 256, 512), F32),
            pltpu.VMEM((2, 16, 512), F32),
            pltpu.VMEM((2, depth, 128), BF),
            pltpu.VMEM((2, 2, width, 128), F32),
            pltpu.VMEM((2, 2, width, 128), BF),
            pltpu.VMEM((2, 2, width, 128), BF),
            pltpu.VMEM((2, width, 128), BF),
            pltpu.VMEM((2, width, 128), BF),
            pltpu.VMEM((2, 8, 128), F32),
            pltpu.VMEM((2, 3, 8, 128), F32),
            dma((8,)),
            dma((29,)),
            dma((29,)),
            dma((6,)),
            dma((6,)),
            dma((6,)),
            dma((6,)),
        ],
        compiler_params=pltpu.CompilerParams(
            collective_id=0, has_side_effects=True, vmem_limit_bytes=60 * 1024 * 1024
        ),
    )(positions, freqs, queries, key_rows, value_rows, residual.T, direction, out_weight)
    return out.T


def device_body(*args):
    queries, key_rows, _, _, residual, direction, _ = args
    fits = (
        lax.axis_size("seq") == 4
        and lax.axis_size("tensor") == 4
        and queries.shape == (256, 1024)
        and key_rows.shape == (256, 512)
        and residual.shape[1] * 4 == direction.shape[0]
        and residual.shape[1] % 64 == 0
        and WINDOW == 1024
    )
    return fused_body(*args) if fits else body(*args)


def solution(mesh):
    return jax.shard_map(
        device_body,
        mesh=mesh,
        in_specs=(
            P(("groups", "seq"), "tensor"),
            P(("groups", "seq"), "tensor"),
            P(("groups", "seq"), "tensor"),
            P(("groups", "seq")),
            P(("groups", "seq"), "tensor"),
            P("groups"),
            P("tensor", None),
        ),
        out_specs=P(("groups", "seq"), "tensor"),
        check_vma=False,
    )
```

```python
import functools

import jax
import jax.numpy as jnp
from jax import lax
from jax.experimental import pallas as pl
from jax.experimental.pallas import tpu as pltpu
from jax.sharding import PartitionSpec as P

HD = 256
WINDOW = 1024


big_negative = -1e30


def shifted_2(value, axis, steps):
    count = lax.axis_size(axis)
    first, last = (max(0, -steps), min(count, count - steps))
    return lax.ppermute(value, axis, [(source, source + steps) for source in range(first, last)])


def rotary_tables(positions, head_dim):
    half_dim = head_dim // 2
    freqs = jnp.power(10000.0, -jnp.arange(half_dim, dtype=jnp.float32) * 2.0 / head_dim)
    angles = positions.astype(jnp.float32)[:, None] * freqs[None, :]
    return (jnp.cos(angles)[:, None, :], jnp.sin(angles)[:, None, :])


def rotate_heads(block, cos_table, sin_table, head_dim):
    row_count = block.shape[0]
    head_count = block.shape[1] // head_dim
    half_dim = head_dim // 2
    widened = block.reshape(row_count, head_count, head_dim).astype(jnp.float32)
    first_half = widened[:, :, :half_dim]
    second_half = widened[:, :, half_dim:]
    turned = jnp.concatenate(
        [
            first_half * cos_table - second_half * sin_table,
            second_half * cos_table + first_half * sin_table,
        ],
        axis=-1,
    )
    return turned.reshape(row_count, head_count * head_dim)


def body(queries, key_rows, value_rows, positions, residual, direction, out_weight):
    tokens_here = queries.shape[0]
    query_heads = queries.shape[1] // HD
    kv_heads = key_rows.shape[1] // HD
    group_size = query_heads // kv_heads
    span_blocks = WINDOW // tokens_here
    seq_index = lax.axis_index("seq")
    cos_table, sin_table = rotary_tables(positions, HD)
    rot_queries = (rotate_heads(queries, cos_table, sin_table, HD) * HD ** (-0.5)).astype(
        jnp.bfloat16
    )
    rot_keys = rotate_heads(key_rows, cos_table, sin_table, HD).astype(jnp.bfloat16)
    query_blocks = rot_queries.reshape(tokens_here, kv_heads, group_size, HD)
    own_scores = jnp.einsum(
        "qkgd,skd->kgqs",
        query_blocks,
        rot_keys.reshape(tokens_here, kv_heads, HD),
        preferred_element_type=jnp.float32,
    )
    earlier_keys = []
    earlier_values = []
    for distance in range(span_blocks, 0, -1):
        moved_keys, moved_values = shifted_2((rot_keys, value_rows), "seq", distance)
        earlier_keys.append(moved_keys)
        earlier_values.append(moved_values)
    far_keys = jnp.concatenate(earlier_keys, axis=0)
    far_values = jnp.concatenate(earlier_values, axis=0)
    far_scores = jnp.einsum(
        "qkgd,skd->kgqs",
        query_blocks,
        far_keys.reshape(-1, kv_heads, HD),
        preferred_element_type=jnp.float32,
    )
    scores = jnp.concatenate([far_scores, own_scores], axis=-1)
    query_index = seq_index * tokens_here + jnp.arange(tokens_here, dtype=jnp.int32)
    key_index = (seq_index - span_blocks) * tokens_here + jnp.arange(
        (span_blocks + 1) * tokens_here, dtype=jnp.int32
    )
    gap_grid = query_index[:, None] - key_index[None, :]
    allowed = (gap_grid >= 0) & (gap_grid < WINDOW) & (key_index[None, :] >= 0)
    scores = jnp.where(allowed, scores, big_negative)
    row_max = jnp.max(scores, axis=-1, keepdims=True)
    shifted = jnp.exp(scores - row_max)
    row_sum = jnp.sum(shifted, axis=-1, keepdims=True)
    weights = (shifted / row_sum).astype(jnp.bfloat16)
    every_value = jnp.concatenate([far_values, value_rows], axis=0).reshape(-1, kv_heads, HD)
    mixed = jnp.einsum("kgqs,skd->qkgd", weights, every_value, preferred_element_type=jnp.float32)
    attended = mixed.astype(jnp.bfloat16).reshape(tokens_here, query_heads * HD)
    partial_value = jnp.dot(attended, out_weight, preferred_element_type=jnp.float32)
    unit_dir = direction / jnp.sqrt(jnp.sum(direction * direction) + 1e-06)
    column_width = residual.shape[1]
    tensor_index = lax.axis_index("tensor")
    local_dir = lax.dynamic_slice_in_dim(unit_dir, tensor_index * column_width, column_width, 0)
    base_state = residual.astype(jnp.float32)
    rounded_terms = partial_value.astype(jnp.bfloat16).astype(jnp.float32)
    dot_terms = jnp.sum(rounded_terms * unit_dir[None, :], axis=1) + jnp.sum(
        base_state * local_dir[None, :], axis=1
    )
    along = lax.psum(dot_terms, "tensor")
    summed = lax.psum_scatter(
        partial_value.astype(jnp.bfloat16), "tensor", scatter_dimension=1, tiled=True
    ).astype(jnp.float32)
    hidden_state = base_state + summed
    ablated = (hidden_state - along[:, None] * local_dir[None, :]).astype(jnp.bfloat16)
    return ablated


BF = jnp.bfloat16
F32 = jnp.float32
MESH = pl.DeviceIdType.MESH

def rot(x, cos, sin):
    x = x.astype(F32)
    a, b = x[:, :128], x[:, 128:]
    return jnp.concatenate([a * cos - b * sin, b * cos + a * sin], axis=1)


def attend(q, blocks, diag):
    scores = [
        lax.dot_general(k, q, (((1,), (1,)), ((), ())), preferred_element_type=F32)
        for k, _ in blocks
    ]
    if diag:
        s = scores[-1]
        key = lax.broadcasted_iota(jnp.int32, s.shape, 0)
        lane = lax.broadcasted_iota(jnp.int32, s.shape, 1)
        row = (lane // 256) * 128 + lane % 128
        scores[-1] = jnp.where(key <= row, s, big_negative)
    m = functools.reduce(jnp.maximum, [jnp.max(s, axis=0, keepdims=True) for s in scores])
    acc, l = 0.0, 0.0
    for s, (_, v) in zip(scores, blocks):
        p = jnp.exp(s - m)
        l = l + jnp.sum(p, axis=0, keepdims=True)
        acc = acc + lax.dot_general(
            v, p.astype(BF), (((0,), (0,)), ((), ())), preferred_element_type=F32
        )
    return acc, m, l


def merge(state, out, lse):
    acc, m, l = state
    top = jnp.maximum(m, lse)
    mine, other = jnp.exp(m - top), jnp.exp(lse - top)
    return acc * mine + out.astype(F32) * other, top, l * mine + other


def kernel(pos_hbm, freq_ref, q_hbm, k_hbm, v_hbm, res_hbm, dir_hbm, w_hbm, out_ref,
           pos, direction, q, k, v, res, wbuf, wt, ucol, rq, rk, kv0, kv1, rq3, rq2,
           o_a, o_b2, o_b1, l_a, l_b2, l_b1, s_a, s_b2, s_c, t_a, t_b2, t_c,
           st_acc, st_ml, att, keep, a_send, a_recv, b_send, b_recv, al_send, al_recv,
           lsem, ssem, rsem, xs, xr, als, alr):
    s = lax.axis_index("seq")
    t = lax.axis_index("tensor")
    core = t % 2
    x_here = t // 2
    x_other = 1 - x_here
    core_peer = t + 1 - 2 * core
    x_peer = (t + 2) % 4
    half = wbuf.shape[2]
    width = half // 2

    local = {}

    def fetch(name, src, dst):
        local[name] = pltpu.make_async_copy(src, dst, lsem.at[len(local)])
        local[name].start()

    fetch("pos", pos_hbm, pos)
    fetch("k", k_hbm, k)
    fetch("q", q_hbm, q)
    fetch("v", v_hbm, v)
    for i, x in enumerate((x_other, x_here)):
        cols = pl.ds(pl.multiple_of(x * half, 128), half)
        fetch(i, w_hbm.at[:, cols], wbuf.at[i])
    fetch("dir", dir_hbm, direction)
    fetch("res", res_hbm, res)

    barrier = pltpu.get_barrier_semaphore()
    for j in (1, 2, 3):
        pl.semaphore_signal(barrier, inc=1, device_id={"seq": (s + j) % 4}, device_id_type=MESH)
        pl.semaphore_signal(barrier, inc=1, device_id={"tensor": (t + j) % 4}, device_id_type=MESH)
    pl.semaphore_wait(barrier, 6)

    copies, index = {}, {}

    def add(name, dev, src, dst, lands_as=None):
        i = index[name] = len(index)
        copies[name] = pltpu.make_async_remote_copy(
            src_ref=src, dst_ref=dst, send_sem=ssem.at[i],
            recv_sem=rsem.at[i if lands_as is None else index[lands_as]],
            device_id={"seq": dev}, device_id_type=MESH)

    for g, name in ((0, "a"), (1, "b")):
        cols = slice(256 * g, 256 * g + 256)
        add("v0" + name + "1", 1, v_hbm.at[:, cols], kv0.at[2 * g + 1])
        add("k0" + name + "1", 1, rk.at[g], kv0.at[2 * g])
    add("v0a2", 2, v_hbm.at[:, 0:256], kv0.at[1])
    add("k0a2", 2, rk.at[0], kv0.at[0])
    add("v1a2", 2, v_hbm.at[:, 0:256], kv1.at[1])
    add("k1a2", 2, rk.at[0], kv1.at[0])
    add("q3a2", 2, rq.at[0], rq3.at[0])
    add("o3b", 3, s_b2, o_b2)
    add("l3b", 3, t_b2, l_b2)
    for c in (0, 1):
        rows = slice(256 * c, 256 * c + 256)
        n = str(c)
        add("q3b2" + n, 2, rq.at[1, rows], rq3.at[1, rows])
        add("f3b1" + n, 1, rq3.at[1, rows], rq3.at[1, rows])
        add("q2b1" + n, 1, rq.at[1, rows], rq2.at[rows])
        add("o3a" + n, 3, s_a.at[c], o_a.at[c])
        add("l3a" + n, 3, t_a.at[c], l_a.at[c])
        add("o2b" + n, 2, s_c.at[0, c], o_b1.at[c])
        add("l2b" + n, 2, t_c.at[0, c], l_b1.at[c])
        add("o3c" + n, 3, s_c.at[1, c], o_b1.at[c], "o2b" + n)
        add("l3c" + n, 3, t_c.at[1, c], l_b1.at[c], "l2b" + n)

    def start(*names):
        for n in names:
            copies[n].start()

    def recv(*names):
        for n in names:
            copies[n].wait_recv()

    def sent(*names):
        for n in names:
            copies[n].wait_send()

    @pl.when(s == 0)
    def _():
        start("v0b1", "v0a2")

    @pl.when(s == 1)
    def _():
        start("v1a2")

    local["pos"].wait()
    freqs = freq_ref[...]
    tokens = pos[...].astype(F32).reshape(1, 256)
    angles = jnp.concatenate(
        [jnp.broadcast_to(tokens[:, 128 * c:128 * c + 128], (128, 128)).T for c in (0, 1)], axis=0
    ) * freqs
    cos, sin = jnp.cos(angles), jnp.sin(angles)
    local["k"].wait()
    for g in (1, 0):
        rk[g] = rot(k[:, 256 * g:256 * g + 256], cos, sin).astype(BF)

    @pl.when(s == 0)
    def _():
        start("k0b1", "k0a2")

    @pl.when(s == 1)
    def _():
        start("k1a2")

    local["q"].wait()
    for g in (1, 0):
        for h in (0, 1):
            at = 256 * (2 * g + h)
            r = (rot(q[:, at:at + 256], cos, sin) * HD ** (-0.5)).astype(BF)
            for c in (0, 1):
                rq[g, 256 * c + 128 * h:256 * c + 128 * h + 128, :] = r[128 * c:128 * c + 128]
        if g == 1:
            @pl.when(s == 3)
            def _():
                start("q3b20")

            @pl.when(s == 2)
            def _():
                start("q2b10")

    local["v"].wait()

    def own(g):
        return rk[g], v[:, 256 * g:256 * g + 256]

    def first(g):
        return kv0[2 * g], kv0[2 * g + 1]

    def second():
        return kv1[0], kv1[1]

    def put(g, state, chunks):
        acc, _, l = state
        out = (acc / l).astype(BF)
        for i, c in enumerate(chunks):
            for h in (0, 1):
                at = 256 * i + 128 * h
                row = 256 * (2 * g + h)
                att[c, row:row + 256, :] = out[:, at:at + 128]

    def send_state(state, out_to, lse_to, *names):
        acc, m, l = state
        out_to[...] = (acc / l).astype(BF)
        lse_to[...] = jnp.broadcast_to(m + jnp.log(l), lse_to.shape)
        start(*names)

    def hold(g, state):
        acc, m, l = state
        st_acc[g] = acc
        st_ml[g, 0:8] = jnp.broadcast_to(m, (8, 512))
        st_ml[g, 8:16] = jnp.broadcast_to(l, (8, 512))

    def held(g, c):
        lanes = slice(256 * c, 256 * c + 256)
        return st_acc[g, :, lanes], st_ml[g, 0:1, lanes], st_ml[g, 8:9, lanes]

    def prepare_weight():
        local["dir"].wait()
        whole = direction[...].reshape(1, 2 * half)
        scale = 1.0 / jnp.sqrt(jnp.sum(whole * whole, axis=1, keepdims=True) + 1e-06)
        for i, x in enumerate((x_other, x_here)):
            local[i].wait()
            mine = jnp.where(x == 0, whole[:, :half], whole[:, half:]) * scale
            for j in range(half // 128):
                at = slice(128 * j, 128 * j + 128)
                wt[i, at, :] = wbuf[i, :, at].T
                ucol[i, at, :] = jnp.broadcast_to(mine[:, at], (128, 128)).T

    @pl.when(s == 0)
    def _():
        put(1, attend(rq[1], [own(1)], True), (0, 1))
        sent("v0b1", "v0a2")
        start("v0a1", "k0a1")
        put(0, attend(rq[0], [own(0)], True), (0, 1))

    @pl.when(s == 2)
    def _():
        recv("q3b20")
        start("f3b10")
        sent("q2b10")
        start("q2b11")
        hold(1, attend(rq[1], [own(1)], True))
        recv("q3b21")
        start("f3b11")
        send_state(attend(rq3[1], [own(1)], False), s_b2, t_b2, "o3b", "l3b")

    @pl.when(s == 3)
    def _():
        sent("q3b20")
        start("q3b21")
        hold(0, attend(rq[0], [own(0)], True))
        sent("q3b21")
        start("q3a2")
        hold(1, attend(rq[1], [own(1)], True))

    @pl.when(s != 1)
    def _():
        prepare_weight()

    @pl.when(s == 1)
    def _():
        recv("v0b1", "k0b1")
        for c in (0, 1):
            n = str(c)
            rows = slice(256 * c, 256 * c + 256)
            recv("q2b1" + n)
            state = attend(rq2[rows, :], [first(1), own(1)], False)
            send_state(state, s_c.at[0, c], t_c.at[0, c], "o2b" + n, "l2b" + n)
            recv("f3b1" + n)
            state = attend(rq3[1, rows, :], [first(1), own(1)], False)
            send_state(state, s_c.at[1, c], t_c.at[1, c], "o3c" + n, "l3c" + n)
        put(1, attend(rq[1], [first(1), own(1)], True), (0, 1))
        prepare_weight()
        recv("v0a1", "k0a1")
        put(0, attend(rq[0], [first(0), own(0)], True), (0, 1))

    @pl.when(s == 2)
    def _():
        recv("v1a2", "k1a2", "q3a2", "v0a2", "k0a2")
        for c in (0, 1):
            n = str(c)
            rows = slice(256 * c, 256 * c + 256)
            state = attend(rq3[0, rows, :], [first(0), second(), own(0)], False)
            send_state(state, s_a.at[c], t_a.at[c], "o3a" + n, "l3a" + n)
        put(0, attend(rq[0], [first(0), second(), own(0)], True), (0, 1))

    @pl.when(s == 3)
    def _():
        recv("o3b", "l3b")
        acc, m, l = st_acc[1], st_ml[1, 0:1], st_ml[1, 8:9]
        hold(1, merge((acc, m, l), o_b2[...], l_b2[0:1]))

    def x_copy(src, dst, i, dev):
        return pltpu.make_async_remote_copy(
            src_ref=src, dst_ref=dst, send_sem=xs.at[i], recv_sem=xr.at[i],
            device_id={"tensor": dev}, device_id_type=MESH)

    local["res"].wait()
    own_part = pl.ds(pl.multiple_of(core * width, 64), width)
    peer_part = pl.ds(pl.multiple_of((1 - core) * width, 64), width)
    local_dir = ucol[1, own_part, :]
    a_copies, b_copies, al_copies = {}, {}, {}
    for c in (0, 1):
        lanes = slice(128 * c, 128 * c + 128)

        @pl.when(s == 3)
        def _(c=c):
            recv("o3a" + str(c), "l3a" + str(c))
            put(0, merge(held(0, c), o_a[c], l_a[c, 0:1]), (c,))

        @pl.when(s >= 2)
        def _(c=c):
            recv("o2b" + str(c), "l2b" + str(c))
            put(1, merge(held(1, c), o_b1[c], l_b1[c, 0:1]), (c,))

        dots = jnp.sum(res[:, lanes].astype(F32) * local_dir, axis=0, keepdims=True)
        for i in (0, 1):
            part = jnp.dot(wt[i, peer_part, :], att[c], preferred_element_type=F32)
            a_send[c, i] = part.astype(BF)
            a_copies[c, i] = x_copy(a_send.at[c, i], a_recv.at[c, i], 2 * c + i, core_peer)
            a_copies[c, i].start()
            dots = dots + jnp.sum(part * ucol[i, peer_part, :], axis=0, keepdims=True)
            part = jnp.dot(wt[i, own_part, :], att[c], preferred_element_type=F32)
            if i == 0:
                a_copies[c, 0].wait_recv()
                b_send[c] = (part + a_recv[c, 0].astype(F32)).astype(BF)
                b_copies[c] = x_copy(b_send.at[c], b_recv.at[c], 4 + c, x_peer)
                b_copies[c].start()
            else:
                keep[c] = part
            dots = dots + jnp.sum(part * ucol[i, own_part, :], axis=0, keepdims=True)
        al_send[c] = jnp.broadcast_to(dots, (8, 128))
        for j in (1, 2, 3):
            i = 3 * c + j - 1
            al_copies[c, j] = pltpu.make_async_remote_copy(
                src_ref=al_send.at[c], dst_ref=al_recv.at[c, j - 1],
                send_sem=als.at[i], recv_sem=alr.at[i],
                device_id={"tensor": (t + j) % 4}, device_id_type=MESH)
            al_copies[c, j].start()

    for c in (0, 1):
        lanes = slice(128 * c, 128 * c + 128)
        along = al_send[c]
        for j in (1, 2, 3):
            al_copies[c, j].wait_recv()
            along = along + al_recv[c, j - 1]
        a_copies[c, 1].wait_recv()
        hidden = res[:, lanes].astype(F32) + keep[c] + a_recv[c, 1].astype(F32)
        keep[c] = hidden - along[0:1] * local_dir
        b_copies[c].wait_recv()
        out_ref[:, lanes] = (keep[c] + b_recv[c].astype(F32)).astype(BF)

    for c in (0, 1):
        a_copies[c, 0].wait_send()
        a_copies[c, 1].wait_send()
        b_copies[c].wait_send()
        for j in (1, 2, 3):
            al_copies[c, j].wait_send()

    @pl.when(s == 0)
    def _():
        sent("k0b1", "k0a2", "v0a1", "k0a1")

    @pl.when(s == 1)
    def _():
        sent("v1a2", "k1a2", "o2b0", "l2b0", "o2b1", "l2b1", "o3c0", "l3c0", "o3c1", "l3c1")

    @pl.when(s == 2)
    def _():
        sent("q2b11", "f3b10", "f3b11", "o3b", "l3b", "o3a0", "l3a0", "o3a1", "l3a1")

    @pl.when(s == 3)
    def _():
        sent("q3a2")


def fused_body(queries, key_rows, value_rows, positions, residual, direction, out_weight):
    freqs = jnp.power(10000.0, -jnp.arange(HD // 2, dtype=F32) * 2.0 / HD)[None, :]
    rows, width = residual.shape
    depth = out_weight.shape[0]
    vmem = pl.BlockSpec(memory_space=pltpu.VMEM)
    anywhere = pl.BlockSpec(memory_space=pl.ANY)
    dma = pltpu.SemaphoreType.DMA
    out = pl.pallas_call(
        kernel,
        out_shape=jax.ShapeDtypeStruct((width, rows), BF),
        in_specs=[anywhere, vmem] + [anywhere] * 6,
        out_specs=vmem,
        scratch_shapes=[
            pltpu.VMEM(positions.shape, jnp.int32),
            pltpu.VMEM(direction.shape, F32),
            pltpu.VMEM(queries.shape, BF),
            pltpu.VMEM(key_rows.shape, BF),
            pltpu.VMEM(value_rows.shape, BF),
            pltpu.VMEM((width, rows), BF),
            pltpu.VMEM((2, depth, 2 * width), BF),
            pltpu.VMEM((2, 2 * width, depth), BF),
            pltpu.VMEM((2, 2 * width, 128), F32),
            pltpu.VMEM((2, 512, 256), BF),
            pltpu.VMEM((2, 256, 256), BF),
            pltpu.VMEM((4, 256, 256), BF),
            pltpu.VMEM((2, 256, 256), BF),
            pltpu.VMEM((2, 512, 256), BF),
            pltpu.VMEM((512, 256), BF),
            pltpu.VMEM((2, 256, 256), BF),
            pltpu.VMEM((256, 512), BF),
            pltpu.VMEM((2, 256, 256), BF),
            pltpu.VMEM((2, 8, 256), F32),
            pltpu.VMEM((8, 512), F32),
            pltpu.VMEM((2, 8, 256), F32),
            pltpu.VMEM((2, 256, 256), BF),
            pltpu.VMEM((256, 512), BF),
            pltpu.VMEM((2, 2, 256, 256), BF),
            pltpu.VMEM((2, 8, 256), F32),
            pltpu.VMEM((8, 512), F32),
            pltpu.VMEM((2, 2, 8, 256), F32),
            pltpu.VMEM((2, 256, 512), F32),
            pltpu.VMEM((2, 16, 512), F32),
            pltpu.VMEM((2, depth, 128), BF),
            pltpu.VMEM((2, width, 128), F32),
            pltpu.VMEM((2, 2, width, 128), BF),
            pltpu.VMEM((2, 2, width, 128), BF),
            pltpu.VMEM((2, width, 128), BF),
            pltpu.VMEM((2, width, 128), BF),
            pltpu.VMEM((2, 8, 128), F32),
            pltpu.VMEM((2, 3, 8, 128), F32),
            dma((8,)),
            dma((29,)),
            dma((29,)),
            dma((6,)),
            dma((6,)),
            dma((6,)),
            dma((6,)),
        ],
        compiler_params=pltpu.CompilerParams(
            collective_id=0, has_side_effects=True, vmem_limit_bytes=60 * 1024 * 1024
        ),
    )(positions, freqs, queries, key_rows, value_rows, residual.T, direction, out_weight)
    return out.T


def device_body(*args):
    queries, key_rows, _, _, residual, direction, _ = args
    fits = (
        lax.axis_size("seq") == 4
        and lax.axis_size("tensor") == 4
        and queries.shape == (256, 1024)
        and key_rows.shape == (256, 512)
        and residual.shape[1] * 4 == direction.shape[0]
        and residual.shape[1] % 64 == 0
        and WINDOW == 1024
    )
    return fused_body(*args) if fits else body(*args)


def solution(mesh):
    return jax.shard_map(
        device_body,
        mesh=mesh,
        in_specs=(
            P(("groups", "seq"), "tensor"),
            P(("groups", "seq"), "tensor"),
            P(("groups", "seq"), "tensor"),
            P(("groups", "seq")),
            P(("groups", "seq"), "tensor"),
            P("groups"),
            P("tensor", None),
        ),
        out_specs=P(("groups", "seq"), "tensor"),
        check_vma=False,
    )
```

```python
import functools

import jax
import jax.numpy as jnp
from jax import lax
from jax.experimental import pallas as pl
from jax.experimental.pallas import tpu as pltpu
from jax.sharding import PartitionSpec as P

HD = 256
WINDOW = 1024


big_negative = -1e30


def shifted_2(value, axis, steps):
    count = lax.axis_size(axis)
    first, last = (max(0, -steps), min(count, count - steps))
    return lax.ppermute(value, axis, [(source, source + steps) for source in range(first, last)])


def rotary_tables(positions, head_dim):
    half_dim = head_dim // 2
    freqs = jnp.power(10000.0, -jnp.arange(half_dim, dtype=jnp.float32) * 2.0 / head_dim)
    angles = positions.astype(jnp.float32)[:, None] * freqs[None, :]
    return (jnp.cos(angles)[:, None, :], jnp.sin(angles)[:, None, :])


def rotate_heads(block, cos_table, sin_table, head_dim):
    row_count = block.shape[0]
    head_count = block.shape[1] // head_dim
    half_dim = head_dim // 2
    widened = block.reshape(row_count, head_count, head_dim).astype(jnp.float32)
    first_half = widened[:, :, :half_dim]
    second_half = widened[:, :, half_dim:]
    turned = jnp.concatenate(
        [
            first_half * cos_table - second_half * sin_table,
            second_half * cos_table + first_half * sin_table,
        ],
        axis=-1,
    )
    return turned.reshape(row_count, head_count * head_dim)


def body(queries, key_rows, value_rows, positions, residual, direction, out_weight):
    tokens_here = queries.shape[0]
    query_heads = queries.shape[1] // HD
    kv_heads = key_rows.shape[1] // HD
    group_size = query_heads // kv_heads
    span_blocks = WINDOW // tokens_here
    seq_index = lax.axis_index("seq")
    cos_table, sin_table = rotary_tables(positions, HD)
    rot_queries = (rotate_heads(queries, cos_table, sin_table, HD) * HD ** (-0.5)).astype(
        jnp.bfloat16
    )
    rot_keys = rotate_heads(key_rows, cos_table, sin_table, HD).astype(jnp.bfloat16)
    query_blocks = rot_queries.reshape(tokens_here, kv_heads, group_size, HD)
    own_scores = jnp.einsum(
        "qkgd,skd->kgqs",
        query_blocks,
        rot_keys.reshape(tokens_here, kv_heads, HD),
        preferred_element_type=jnp.float32,
    )
    earlier_keys = []
    earlier_values = []
    for distance in range(span_blocks, 0, -1):
        moved_keys, moved_values = shifted_2((rot_keys, value_rows), "seq", distance)
        earlier_keys.append(moved_keys)
        earlier_values.append(moved_values)
    far_keys = jnp.concatenate(earlier_keys, axis=0)
    far_values = jnp.concatenate(earlier_values, axis=0)
    far_scores = jnp.einsum(
        "qkgd,skd->kgqs",
        query_blocks,
        far_keys.reshape(-1, kv_heads, HD),
        preferred_element_type=jnp.float32,
    )
    scores = jnp.concatenate([far_scores, own_scores], axis=-1)
    query_index = seq_index * tokens_here + jnp.arange(tokens_here, dtype=jnp.int32)
    key_index = (seq_index - span_blocks) * tokens_here + jnp.arange(
        (span_blocks + 1) * tokens_here, dtype=jnp.int32
    )
    gap_grid = query_index[:, None] - key_index[None, :]
    allowed = (gap_grid >= 0) & (gap_grid < WINDOW) & (key_index[None, :] >= 0)
    scores = jnp.where(allowed, scores, big_negative)
    row_max = jnp.max(scores, axis=-1, keepdims=True)
    shifted = jnp.exp(scores - row_max)
    row_sum = jnp.sum(shifted, axis=-1, keepdims=True)
    weights = (shifted / row_sum).astype(jnp.bfloat16)
    every_value = jnp.concatenate([far_values, value_rows], axis=0).reshape(-1, kv_heads, HD)
    mixed = jnp.einsum("kgqs,skd->qkgd", weights, every_value, preferred_element_type=jnp.float32)
    attended = mixed.astype(jnp.bfloat16).reshape(tokens_here, query_heads * HD)
    partial_value = jnp.dot(attended, out_weight, preferred_element_type=jnp.float32)
    unit_dir = direction / jnp.sqrt(jnp.sum(direction * direction) + 1e-06)
    column_width = residual.shape[1]
    tensor_index = lax.axis_index("tensor")
    local_dir = lax.dynamic_slice_in_dim(unit_dir, tensor_index * column_width, column_width, 0)
    base_state = residual.astype(jnp.float32)
    rounded_terms = partial_value.astype(jnp.bfloat16).astype(jnp.float32)
    dot_terms = jnp.sum(rounded_terms * unit_dir[None, :], axis=1) + jnp.sum(
        base_state * local_dir[None, :], axis=1
    )
    along = lax.psum(dot_terms, "tensor")
    summed = lax.psum_scatter(
        partial_value.astype(jnp.bfloat16), "tensor", scatter_dimension=1, tiled=True
    ).astype(jnp.float32)
    hidden_state = base_state + summed
    ablated = (hidden_state - along[:, None] * local_dir[None, :]).astype(jnp.bfloat16)
    return ablated


BF = jnp.bfloat16
F32 = jnp.float32
MESH = pl.DeviceIdType.MESH

def rot(x, cos, sin):
    x = x.astype(F32)
    a, b = x[:, :128], x[:, 128:]
    return jnp.concatenate([a * cos - b * sin, b * cos + a * sin], axis=1)


def attend(q, blocks, diag):
    scores = [
        lax.dot_general(k, q, (((1,), (1,)), ((), ())), preferred_element_type=F32)
        for k, _ in blocks
    ]
    if diag:
        s = scores[-1]
        key = lax.broadcasted_iota(jnp.int32, s.shape, 0)
        lane = lax.broadcasted_iota(jnp.int32, s.shape, 1)
        row = (lane // 256) * 128 + lane % 128
        scores[-1] = jnp.where(key <= row, s, big_negative)
    m = functools.reduce(jnp.maximum, [jnp.max(s, axis=0, keepdims=True) for s in scores])
    acc, l = 0.0, 0.0
    for s, (_, v) in zip(scores, blocks):
        p = jnp.exp(s - m)
        l = l + jnp.sum(p, axis=0, keepdims=True)
        acc = acc + lax.dot_general(
            v, p.astype(BF), (((0,), (0,)), ((), ())), preferred_element_type=F32
        )
    return acc, m, l


def merge(state, out, lse):
    acc, m, l = state
    top = jnp.maximum(m, lse)
    mine, other = jnp.exp(m - top), jnp.exp(lse - top)
    return acc * mine + out.astype(F32) * other, top, l * mine + other


def kernel(pos_hbm, freq_ref, q_hbm, k_hbm, v_hbm, res_hbm, dir_hbm, w_hbm, out_ref,
           pos, direction, q, k, v, res, wbuf, urow, ldir, rq, rk, kv0, kv1, rq3, rq2,
           o_a, o_b2, o_b1, l_a, l_b2, l_b1, s_a, s_b2, s_c, t_a, t_b2, t_c,
           st_acc, st_ml, att, keep, turn, last, a_send, a_recv, b_send, b_recv, al_send, al_recv,
           lsem, ssem, rsem, xs, xr, als, alr):
    s = lax.axis_index("seq")
    t = lax.axis_index("tensor")
    core = t % 2
    x_here = t // 2
    x_other = 1 - x_here
    core_peer = t + 1 - 2 * core
    x_peer = (t + 2) % 4
    half = wbuf.shape[2]
    width = half // 2
    shift = (width // 128) * 128
    window = half - shift

    local = {}

    def fetch(name, src, dst):
        local[name] = pltpu.make_async_copy(src, dst, lsem.at[len(local)])
        local[name].start()

    fetch("pos", pos_hbm, pos)
    fetch("k", k_hbm, k)
    fetch("q", q_hbm, q)
    fetch("v", v_hbm, v)
    for i, x in enumerate((x_other, x_here)):
        cols = pl.ds(pl.multiple_of(x * half, 128), half)
        fetch(i, w_hbm.at[:, cols], wbuf.at[i])
    fetch("dir", dir_hbm, direction)
    fetch("res", res_hbm, res)

    barrier = pltpu.get_barrier_semaphore()
    for j in (1, 2, 3):
        pl.semaphore_signal(barrier, inc=1, device_id={"seq": (s + j) % 4}, device_id_type=MESH)
        pl.semaphore_signal(barrier, inc=1, device_id={"tensor": (t + j) % 4}, device_id_type=MESH)
    pl.semaphore_wait(barrier, 6)

    copies, index = {}, {}

    def add(name, dev, src, dst, lands_as=None):
        i = index[name] = len(index)
        copies[name] = pltpu.make_async_remote_copy(
            src_ref=src, dst_ref=dst, send_sem=ssem.at[i],
            recv_sem=rsem.at[i if lands_as is None else index[lands_as]],
            device_id={"seq": dev}, device_id_type=MESH)

    for g, name in ((0, "a"), (1, "b")):
        cols = slice(256 * g, 256 * g + 256)
        add("v0" + name + "1", 1, v_hbm.at[:, cols], kv0.at[2 * g + 1])
        add("k0" + name + "1", 1, rk.at[g], kv0.at[2 * g])
    add("v0a2", 2, v_hbm.at[:, 0:256], kv0.at[1])
    add("k0a2", 2, rk.at[0], kv0.at[0])
    add("v1a2", 2, v_hbm.at[:, 0:256], kv1.at[1])
    add("k1a2", 2, rk.at[0], kv1.at[0])
    add("q3a2", 2, rq.at[0], rq3.at[0])
    add("o3b", 3, s_b2, o_b2)
    add("l3b", 3, t_b2, l_b2)
    for c in (0, 1):
        rows = slice(256 * c, 256 * c + 256)
        n = str(c)
        add("q3b2" + n, 2, rq.at[1, rows], rq3.at[1, rows])
        add("f3b1" + n, 1, rq3.at[1, rows], rq3.at[1, rows])
        add("q2b1" + n, 1, rq.at[1, rows], rq2.at[rows])
        add("o3a" + n, 3, s_a.at[c], o_a.at[c])
        add("l3a" + n, 3, t_a.at[c], l_a.at[c])
        add("o2b" + n, 2, s_c.at[0, c], o_b1.at[c])
        add("l2b" + n, 2, t_c.at[0, c], l_b1.at[c])
        add("o3c" + n, 3, s_c.at[1, c], o_b1.at[c], "o2b" + n)
        add("l3c" + n, 3, t_c.at[1, c], l_b1.at[c], "l2b" + n)

    def start(*names):
        for n in names:
            copies[n].start()

    def recv(*names):
        for n in names:
            copies[n].wait_recv()

    def sent(*names):
        for n in names:
            copies[n].wait_send()

    @pl.when(s == 0)
    def _():
        start("v0b1", "v0a2")

    @pl.when(s == 1)
    def _():
        start("v1a2")

    local["pos"].wait()
    freqs = freq_ref[...]
    tokens = pos[...].astype(F32).reshape(1, 256)
    angles = jnp.concatenate(
        [jnp.broadcast_to(tokens[:, 128 * c:128 * c + 128], (128, 128)).T for c in (0, 1)], axis=0
    ) * freqs
    cos, sin = jnp.cos(angles), jnp.sin(angles)
    local["k"].wait()
    for g in (1, 0):
        rk[g] = rot(k[:, 256 * g:256 * g + 256], cos, sin).astype(BF)

    @pl.when(s == 0)
    def _():
        start("k0b1", "k0a2")

    @pl.when(s == 1)
    def _():
        start("k1a2")

    local["q"].wait()
    for g in (1, 0):
        for h in (0, 1):
            at = 256 * (2 * g + h)
            r = (rot(q[:, at:at + 256], cos, sin) * HD ** (-0.5)).astype(BF)
            for c in (0, 1):
                rq[g, 256 * c + 128 * h:256 * c + 128 * h + 128, :] = r[128 * c:128 * c + 128]
        if g == 1:
            @pl.when(s == 3)
            def _():
                start("q3b20")

            @pl.when(s == 2)
            def _():
                start("q2b10")

    local["v"].wait()

    def own(g):
        return rk[g], v[:, 256 * g:256 * g + 256]

    def first(g):
        return kv0[2 * g], kv0[2 * g + 1]

    def second():
        return kv1[0], kv1[1]

    def put(g, state, chunks):
        acc, _, l = state
        out = acc / l
        for i, c in enumerate(chunks):
            for h in (0, 1):
                at = 256 * i + 128 * h
                col = 256 * (2 * g + h)
                att[c, :, col:col + 256] = out[:, at:at + 128].T.astype(BF)

    def send_state(state, out_to, lse_to, *names):
        acc, m, l = state
        out_to[...] = (acc / l).astype(BF)
        lse_to[...] = jnp.broadcast_to(m + jnp.log(l), lse_to.shape)
        start(*names)

    def hold(g, state):
        acc, m, l = state
        st_acc[g] = acc
        st_ml[g, 0:8] = jnp.broadcast_to(m, (8, 512))
        st_ml[g, 8:16] = jnp.broadcast_to(l, (8, 512))

    def held(g, c):
        lanes = slice(256 * c, 256 * c + 256)
        return st_acc[g, :, lanes], st_ml[g, 0:1, lanes], st_ml[g, 8:9, lanes]

    def prepare_direction():
        local["dir"].wait()
        whole = direction[...].reshape(1, 2 * half)
        scale = 1.0 / jnp.sqrt(jnp.sum(whole * whole, axis=1, keepdims=True) + 1e-06)
        lane = lax.broadcasted_iota(jnp.int32, (1, window), 1)
        shared = jnp.where(core == 0, 0, shift)
        keep_lane = (lane < shared) | (lane >= shared + (window - shift))
        for i, x in enumerate((x_other, x_here)):
            mine = jnp.where(x == 0, whole[:, :half], whole[:, half:]) * scale
            low, high = mine[:, :window], mine[:, shift:]
            urow[2 * i:2 * i + 1] = jnp.where(keep_lane, jnp.where(core == 0, high, low), 0.0)
            urow[2 * i + 1:2 * i + 2] = jnp.where(core == 0, low, high)
        for at in range(0, window, 128):
            ldir[at:at + 128, :] = jnp.broadcast_to(urow[3:4, at:at + 128], (128, 128)).T

    @pl.when(s == 0)
    def _():
        put(1, attend(rq[1], [own(1)], True), (0, 1))
        sent("v0b1", "v0a2")
        start("v0a1", "k0a1")
        put(0, attend(rq[0], [own(0)], True), (0, 1))

    @pl.when(s == 2)
    def _():
        recv("q3b20")
        start("f3b10")
        sent("q2b10")
        start("q2b11")
        hold(1, attend(rq[1], [own(1)], True))
        recv("q3b21")
        start("f3b11")
        send_state(attend(rq3[1], [own(1)], False), s_b2, t_b2, "o3b", "l3b")

    @pl.when(s == 3)
    def _():
        sent("q3b20")
        start("q3b21")
        hold(0, attend(rq[0], [own(0)], True))
        sent("q3b21")
        start("q3a2")
        hold(1, attend(rq[1], [own(1)], True))

    prepare_direction()

    @pl.when(s == 1)
    def _():
        recv("v0b1", "k0b1")
        for c in (0, 1):
            n = str(c)
            rows = slice(256 * c, 256 * c + 256)
            recv("q2b1" + n)
            state = attend(rq2[rows, :], [first(1), own(1)], False)
            send_state(state, s_c.at[0, c], t_c.at[0, c], "o2b" + n, "l2b" + n)
            recv("f3b1" + n)
            state = attend(rq3[1, rows, :], [first(1), own(1)], False)
            send_state(state, s_c.at[1, c], t_c.at[1, c], "o3c" + n, "l3c" + n)
        put(1, attend(rq[1], [first(1), own(1)], True), (0, 1))
        recv("v0a1", "k0a1")
        put(0, attend(rq[0], [first(0), own(0)], True), (0, 1))

    @pl.when(s == 2)
    def _():
        recv("v1a2", "k1a2", "q3a2", "v0a2", "k0a2")
        for c in (0, 1):
            n = str(c)
            rows = slice(256 * c, 256 * c + 256)
            state = attend(rq3[0, rows, :], [first(0), second(), own(0)], False)
            send_state(state, s_a.at[c], t_a.at[c], "o3a" + n, "l3a" + n)
        put(0, attend(rq[0], [first(0), second(), own(0)], True), (0, 1))

    @pl.when(s == 3)
    def _():
        recv("o3b", "l3b")
        acc, m, l = st_acc[1], st_ml[1, 0:1], st_ml[1, 8:9]
        hold(1, merge((acc, m, l), o_b2[...], l_b2[0:1]))

    def x_copy(src, dst, i, dev):
        return pltpu.make_async_remote_copy(
            src_ref=src, dst_ref=dst, send_sem=xs.at[i], recv_sem=xr.at[i],
            device_id={"tensor": dev}, device_id_type=MESH)

    local["res"].wait()
    own_window = pl.ds(pl.multiple_of(core * shift, 128), window)
    peer_window = pl.ds(pl.multiple_of((1 - core) * shift, 128), window)
    own_rows = pl.ds(pl.multiple_of(core * (width - shift), 64), width)
    local_dir = ldir[own_rows, :]
    local[0].wait()
    local[1].wait()
    a_copies, b_copies, al_copies = {}, {}, {}
    for c in (0, 1):
        lanes = slice(128 * c, 128 * c + 128)

        @pl.when(s == 3)
        def _(c=c):
            recv("o3a" + str(c), "l3a" + str(c))
            put(0, merge(held(0, c), o_a[c], l_a[c, 0:1]), (c,))

        @pl.when(s >= 2)
        def _(c=c):
            recv("o2b" + str(c), "l2b" + str(c))
            put(1, merge(held(1, c), o_b1[c], l_b1[c, 0:1]), (c,))

        dots = 0.0
        for i in (0, 1):
            part = jnp.dot(att[c], wbuf[i, :, peer_window], preferred_element_type=F32)
            a_send[c, i] = part.astype(BF)
            a_copies[c, i] = x_copy(a_send.at[c, i], a_recv.at[c, i], 2 * c + i, core_peer)
            a_copies[c, i].start()
            dots = dots + jnp.sum(part * urow[2 * i:2 * i + 1], axis=1, keepdims=True)
            part = jnp.dot(att[c], wbuf[i, :, own_window], preferred_element_type=F32)
            dots = dots + jnp.sum(part * urow[2 * i + 1:2 * i + 2], axis=1, keepdims=True)
            keep[c, i] = part
            if i == 0:
                a_copies[c, 0].wait_recv()
                turn[...] = (keep[c, 0] + a_recv[c, 0].astype(F32)).T
                b_send[c] = turn[own_rows, :].astype(BF)
                b_copies[c] = x_copy(b_send.at[c], b_recv.at[c], 4 + c, x_peer)
                b_copies[c].start()
        dots = jnp.broadcast_to(dots, (128, 128)).T[0:1]
        dots = dots + jnp.sum(res[:, lanes].astype(F32) * local_dir, axis=0, keepdims=True)
        al_send[c] = jnp.broadcast_to(dots, (8, 128))
        for j in (1, 2, 3):
            i = 3 * c + j - 1
            al_copies[c, j] = pltpu.make_async_remote_copy(
                src_ref=al_send.at[c], dst_ref=al_recv.at[c, j - 1],
                send_sem=als.at[i], recv_sem=alr.at[i],
                device_id={"tensor": (t + j) % 4}, device_id_type=MESH)
            al_copies[c, j].start()

    for c in (0, 1):
        lanes = slice(128 * c, 128 * c + 128)
        along = al_send[c]
        for j in (1, 2, 3):
            al_copies[c, j].wait_recv()
            along = along + al_recv[c, j - 1]
        a_copies[c, 1].wait_recv()
        turn[...] = (keep[c, 1] + a_recv[c, 1].astype(F32)).T
        hidden = res[:, lanes].astype(F32) + turn[own_rows, :]
        last[c] = hidden - along[0:1] * local_dir
        b_copies[c].wait_recv()
        out_ref[:, lanes] = (last[c] + b_recv[c].astype(F32)).astype(BF)

    for c in (0, 1):
        a_copies[c, 0].wait_send()
        a_copies[c, 1].wait_send()
        b_copies[c].wait_send()
        for j in (1, 2, 3):
            al_copies[c, j].wait_send()

    @pl.when(s == 0)
    def _():
        sent("k0b1", "k0a2", "v0a1", "k0a1")

    @pl.when(s == 1)
    def _():
        sent("v1a2", "k1a2", "o2b0", "l2b0", "o2b1", "l2b1", "o3c0", "l3c0", "o3c1", "l3c1")

    @pl.when(s == 2)
    def _():
        sent("q2b11", "f3b10", "f3b11", "o3b", "l3b", "o3a0", "l3a0", "o3a1", "l3a1")

    @pl.when(s == 3)
    def _():
        sent("q3a2")


def fused_body(queries, key_rows, value_rows, positions, residual, direction, out_weight):
    freqs = jnp.power(10000.0, -jnp.arange(HD // 2, dtype=F32) * 2.0 / HD)[None, :]
    rows, width = residual.shape
    depth = out_weight.shape[0]
    window = 2 * width - (width // 128) * 128
    vmem = pl.BlockSpec(memory_space=pltpu.VMEM)
    anywhere = pl.BlockSpec(memory_space=pl.ANY)
    dma = pltpu.SemaphoreType.DMA
    out = pl.pallas_call(
        kernel,
        out_shape=jax.ShapeDtypeStruct((width, rows), BF),
        in_specs=[anywhere, vmem] + [anywhere] * 6,
        out_specs=vmem,
        scratch_shapes=[
            pltpu.VMEM(positions.shape, jnp.int32),
            pltpu.VMEM(direction.shape, F32),
            pltpu.VMEM(queries.shape, BF),
            pltpu.VMEM(key_rows.shape, BF),
            pltpu.VMEM(value_rows.shape, BF),
            pltpu.VMEM((width, rows), BF),
            pltpu.VMEM((2, depth, 2 * width), BF),
            pltpu.VMEM((8, window), F32),
            pltpu.VMEM((window, 128), F32),
            pltpu.VMEM((2, 512, 256), BF),
            pltpu.VMEM((2, 256, 256), BF),
            pltpu.VMEM((4, 256, 256), BF),
            pltpu.VMEM((2, 256, 256), BF),
            pltpu.VMEM((2, 512, 256), BF),
            pltpu.VMEM((512, 256), BF),
            pltpu.VMEM((2, 256, 256), BF),
            pltpu.VMEM((256, 512), BF),
            pltpu.VMEM((2, 256, 256), BF),
            pltpu.VMEM((2, 8, 256), F32),
            pltpu.VMEM((8, 512), F32),
            pltpu.VMEM((2, 8, 256), F32),
            pltpu.VMEM((2, 256, 256), BF),
            pltpu.VMEM((256, 512), BF),
            pltpu.VMEM((2, 2, 256, 256), BF),
            pltpu.VMEM((2, 8, 256), F32),
            pltpu.VMEM((8, 512), F32),
            pltpu.VMEM((2, 2, 8, 256), F32),
            pltpu.VMEM((2, 256, 512), F32),
            pltpu.VMEM((2, 16, 512), F32),
            pltpu.VMEM((2, 128, depth), BF),
            pltpu.VMEM((2, 2, 128, window), F32),
            pltpu.VMEM((window, 128), F32),
            pltpu.VMEM((2, width, 128), F32),
            pltpu.VMEM((2, 2, 128, window), BF),
            pltpu.VMEM((2, 2, 128, window), BF),
            pltpu.VMEM((2, width, 128), BF),
            pltpu.VMEM((2, width, 128), BF),
            pltpu.VMEM((2, 8, 128), F32),
            pltpu.VMEM((2, 3, 8, 128), F32),
            dma((8,)),
            dma((29,)),
            dma((29,)),
            dma((6,)),
            dma((6,)),
            dma((6,)),
            dma((6,)),
        ],
        compiler_params=pltpu.CompilerParams(
            collective_id=0, has_side_effects=True, vmem_limit_bytes=60 * 1024 * 1024
        ),
    )(positions, freqs, queries, key_rows, value_rows, residual.T, direction, out_weight)
    return out.T


def device_body(*args):
    queries, key_rows, _, _, residual, direction, _ = args
    fits = (
        lax.axis_size("seq") == 4
        and lax.axis_size("tensor") == 4
        and queries.shape == (256, 1024)
        and key_rows.shape == (256, 512)
        and residual.shape[1] * 4 == direction.shape[0]
        and residual.shape[1] % 128 == 64
        and WINDOW == 1024
    )
    return fused_body(*args) if fits else body(*args)


def solution(mesh):
    return jax.shard_map(
        device_body,
        mesh=mesh,
        in_specs=(
            P(("groups", "seq"), "tensor"),
            P(("groups", "seq"), "tensor"),
            P(("groups", "seq"), "tensor"),
            P(("groups", "seq")),
            P(("groups", "seq"), "tensor"),
            P("groups"),
            P("tensor", None),
        ),
        out_specs=P(("groups", "seq"), "tensor"),
        check_vma=False,
    )
```

```python
import functools

import jax
import jax.numpy as jnp
from jax import lax
from jax.experimental import pallas as pl
from jax.experimental.pallas import tpu as pltpu
from jax.sharding import PartitionSpec as P

HD = 256
WINDOW = 1024


big_negative = -1e30


def shifted_2(value, axis, steps):
    count = lax.axis_size(axis)
    first, last = (max(0, -steps), min(count, count - steps))
    return lax.ppermute(value, axis, [(source, source + steps) for source in range(first, last)])


def rotary_tables(positions, head_dim):
    half_dim = head_dim // 2
    freqs = jnp.power(10000.0, -jnp.arange(half_dim, dtype=jnp.float32) * 2.0 / head_dim)
    angles = positions.astype(jnp.float32)[:, None] * freqs[None, :]
    return (jnp.cos(angles)[:, None, :], jnp.sin(angles)[:, None, :])


def rotate_heads(block, cos_table, sin_table, head_dim):
    row_count = block.shape[0]
    head_count = block.shape[1] // head_dim
    half_dim = head_dim // 2
    widened = block.reshape(row_count, head_count, head_dim).astype(jnp.float32)
    first_half = widened[:, :, :half_dim]
    second_half = widened[:, :, half_dim:]
    turned = jnp.concatenate(
        [
            first_half * cos_table - second_half * sin_table,
            second_half * cos_table + first_half * sin_table,
        ],
        axis=-1,
    )
    return turned.reshape(row_count, head_count * head_dim)


def body(queries, key_rows, value_rows, positions, residual, direction, out_weight):
    tokens_here = queries.shape[0]
    query_heads = queries.shape[1] // HD
    kv_heads = key_rows.shape[1] // HD
    group_size = query_heads // kv_heads
    span_blocks = WINDOW // tokens_here
    seq_index = lax.axis_index("seq")
    cos_table, sin_table = rotary_tables(positions, HD)
    rot_queries = (rotate_heads(queries, cos_table, sin_table, HD) * HD ** (-0.5)).astype(
        jnp.bfloat16
    )
    rot_keys = rotate_heads(key_rows, cos_table, sin_table, HD).astype(jnp.bfloat16)
    query_blocks = rot_queries.reshape(tokens_here, kv_heads, group_size, HD)
    own_scores = jnp.einsum(
        "qkgd,skd->kgqs",
        query_blocks,
        rot_keys.reshape(tokens_here, kv_heads, HD),
        preferred_element_type=jnp.float32,
    )
    earlier_keys = []
    earlier_values = []
    for distance in range(span_blocks, 0, -1):
        moved_keys, moved_values = shifted_2((rot_keys, value_rows), "seq", distance)
        earlier_keys.append(moved_keys)
        earlier_values.append(moved_values)
    far_keys = jnp.concatenate(earlier_keys, axis=0)
    far_values = jnp.concatenate(earlier_values, axis=0)
    far_scores = jnp.einsum(
        "qkgd,skd->kgqs",
        query_blocks,
        far_keys.reshape(-1, kv_heads, HD),
        preferred_element_type=jnp.float32,
    )
    scores = jnp.concatenate([far_scores, own_scores], axis=-1)
    query_index = seq_index * tokens_here + jnp.arange(tokens_here, dtype=jnp.int32)
    key_index = (seq_index - span_blocks) * tokens_here + jnp.arange(
        (span_blocks + 1) * tokens_here, dtype=jnp.int32
    )
    gap_grid = query_index[:, None] - key_index[None, :]
    allowed = (gap_grid >= 0) & (gap_grid < WINDOW) & (key_index[None, :] >= 0)
    scores = jnp.where(allowed, scores, big_negative)
    row_max = jnp.max(scores, axis=-1, keepdims=True)
    shifted = jnp.exp(scores - row_max)
    row_sum = jnp.sum(shifted, axis=-1, keepdims=True)
    weights = (shifted / row_sum).astype(jnp.bfloat16)
    every_value = jnp.concatenate([far_values, value_rows], axis=0).reshape(-1, kv_heads, HD)
    mixed = jnp.einsum("kgqs,skd->qkgd", weights, every_value, preferred_element_type=jnp.float32)
    attended = mixed.astype(jnp.bfloat16).reshape(tokens_here, query_heads * HD)
    partial_value = jnp.dot(attended, out_weight, preferred_element_type=jnp.float32)
    unit_dir = direction / jnp.sqrt(jnp.sum(direction * direction) + 1e-06)
    column_width = residual.shape[1]
    tensor_index = lax.axis_index("tensor")
    local_dir = lax.dynamic_slice_in_dim(unit_dir, tensor_index * column_width, column_width, 0)
    base_state = residual.astype(jnp.float32)
    rounded_terms = partial_value.astype(jnp.bfloat16).astype(jnp.float32)
    dot_terms = jnp.sum(rounded_terms * unit_dir[None, :], axis=1) + jnp.sum(
        base_state * local_dir[None, :], axis=1
    )
    along = lax.psum(dot_terms, "tensor")
    summed = lax.psum_scatter(
        partial_value.astype(jnp.bfloat16), "tensor", scatter_dimension=1, tiled=True
    ).astype(jnp.float32)
    hidden_state = base_state + summed
    ablated = (hidden_state - along[:, None] * local_dir[None, :]).astype(jnp.bfloat16)
    return ablated


BF = jnp.bfloat16
F32 = jnp.float32
MESH = pl.DeviceIdType.MESH

def rot(x, cos, sin):
    x = x.astype(F32)
    a, b = x[:, :128], x[:, 128:]
    return jnp.concatenate([a * cos - b * sin, b * cos + a * sin], axis=1)


def cos_sin(x):
    n = jnp.floor(x * 0.15915494309189535 + 0.5)
    r = ((x - n * 6.28125) - n * (507.0 / 262144.0)) - n * 1.2556659146019e-06
    k = jnp.floor(r * 0.6366197723675814 + 0.5)
    y = (r - k * 1.5707963705062866) + k * 4.371139000186241e-08
    z = y * y
    sin = y + y * z * (-1.0 / 6 + z * (1.0 / 120 + z * (-1.0 / 5040 + z * (1.0 / 362880))))
    cos = 1.0 + z * (-0.5 + z * (1.0 / 24 + z * (-1.0 / 720 + z * (1.0 / 40320))))
    odd = jnp.abs(k) == 1.0
    flip = jnp.abs(k) == 2.0
    cos_out = jnp.where(odd, -k * sin, jnp.where(flip, -cos, cos))
    sin_out = jnp.where(odd, k * cos, jnp.where(flip, -sin, sin))
    return cos_out, sin_out


def attend(q, blocks, diag):
    scores = [
        lax.dot_general(k, q, (((1,), (1,)), ((), ())), preferred_element_type=F32)
        for k, _ in blocks
    ]
    if diag:
        s = scores[-1]
        key = lax.broadcasted_iota(jnp.int32, s.shape, 0)
        lane = lax.broadcasted_iota(jnp.int32, s.shape, 1)
        row = (lane // 256) * 128 + lane % 128
        scores[-1] = jnp.where(key <= row, s, big_negative)
    m = functools.reduce(jnp.maximum, [jnp.max(s, axis=0, keepdims=True) for s in scores])
    acc, l = 0.0, 0.0
    for s, (_, v) in zip(scores, blocks):
        p = jnp.exp(s - m)
        l = l + jnp.sum(p, axis=0, keepdims=True)
        acc = acc + lax.dot_general(
            v, p.astype(BF), (((0,), (0,)), ((), ())), preferred_element_type=F32
        )
    return acc, m, l


def merge(state, out, lse):
    acc, m, l = state
    top = jnp.maximum(m, lse)
    mine, other = jnp.exp(m - top), jnp.exp(lse - top)
    return acc * mine + out.astype(F32) * other, top, l * mine + other


def kernel(pos_hbm, freq_ref, q_hbm, k_hbm, v_hbm, res_hbm, dir_hbm, w_hbm, out_ref,
           pos, direction, q, k, v, res, wbuf, urow, ldir, rq, rk, kv0, kv1, rq3, rq2,
           o_a, o_b2, o_b1, l_a, l_b2, l_b1, s_a, s_b2, s_c, t_a, t_b2, t_c,
           st_acc, st_ml, att, keep, dots, turn, last, a_send, a_recv, b_send, b_recv,
           c_send, c_recv, al_send, al_recv,
           lsem, ssem, rsem, xs, xr, als, alr):
    s = lax.axis_index("seq")
    t = lax.axis_index("tensor")
    core = t % 2
    x_here = t // 2
    x_other = 1 - x_here
    core_peer = t + 1 - 2 * core
    x_peer = (t + 2) % 4
    half = wbuf.shape[2]
    width = half // 2
    shift = (width // 128) * 128
    window = half - shift

    local = {}

    def fetch(name, src, dst):
        local[name] = pltpu.make_async_copy(src, dst, lsem.at[len(local)])
        local[name].start()

    fetch("pos", pos_hbm, pos)
    fetch("k", k_hbm, k)
    fetch("q", q_hbm, q)
    fetch("v", v_hbm, v)
    for i, x in enumerate((x_other, x_here)):
        cols = pl.ds(pl.multiple_of(x * half, 128), half)
        fetch(i, w_hbm.at[:, cols], wbuf.at[i])
    fetch("dir", dir_hbm, direction)
    fetch("res", res_hbm, res)

    barrier = pltpu.get_barrier_semaphore()
    for j in (1, 2, 3):
        pl.semaphore_signal(barrier, inc=1, device_id={"seq": (s + j) % 4}, device_id_type=MESH)
        pl.semaphore_signal(barrier, inc=1, device_id={"tensor": (t + j) % 4}, device_id_type=MESH)
    pl.semaphore_wait(barrier, 6)

    copies, index = {}, {}

    def add(name, dev, src, dst, lands_as=None):
        i = index[name] = len(index)
        copies[name] = pltpu.make_async_remote_copy(
            src_ref=src, dst_ref=dst, send_sem=ssem.at[i],
            recv_sem=rsem.at[i if lands_as is None else index[lands_as]],
            device_id={"seq": dev}, device_id_type=MESH)

    for g, name in ((0, "a"), (1, "b")):
        cols = slice(256 * g, 256 * g + 256)
        add("v0" + name + "1", 1, v_hbm.at[:, cols], kv0.at[2 * g + 1])
        add("k0" + name + "1", 1, rk.at[g], kv0.at[2 * g])
    add("v0a2", 2, v_hbm.at[:, 0:256], kv0.at[1])
    add("k0a2", 2, rk.at[0], kv0.at[0])
    add("v1a2", 2, v_hbm.at[:, 0:256], kv1.at[1])
    add("k1a2", 2, rk.at[0], kv1.at[0])
    for c in (0, 1):
        rows = slice(256 * c, 256 * c + 256)
        n = str(c)
        add("q3b2" + n, 2, rq.at[1, rows], rq3.at[1, rows])
        add("q3a2" + n, 2, rq.at[0, rows], rq3.at[0, rows])
        add("o3b" + n, 3, s_b2.at[c], o_b2.at[c])
        add("l3b" + n, 3, t_b2.at[c], l_b2.at[c])
        add("f3b1" + n, 1, rq3.at[1, rows], rq3.at[1, rows])
        add("q2b1" + n, 1, rq.at[1, rows], rq2.at[rows])
        add("o3a" + n, 3, s_a.at[c], o_a.at[c])
        add("l3a" + n, 3, t_a.at[c], l_a.at[c])
        add("o2b" + n, 2, s_c.at[0, c], o_b1.at[c])
        add("l2b" + n, 2, t_c.at[0, c], l_b1.at[c])
        add("o3c" + n, 3, s_c.at[1, c], o_b1.at[c], "o2b" + n)
        add("l3c" + n, 3, t_c.at[1, c], l_b1.at[c], "l2b" + n)

    def start(*names):
        for n in names:
            copies[n].start()

    def recv(*names):
        for n in names:
            copies[n].wait_recv()

    def sent(*names):
        for n in names:
            copies[n].wait_send()

    @pl.when(s == 0)
    def _():
        start("v0b1")

    @pl.when(s == 1)
    def _():
        start("v1a2")

    local["pos"].wait()
    freqs = freq_ref[...]
    tokens = pos[...].astype(F32).reshape(1, 256)
    angles = jnp.concatenate(
        [jnp.broadcast_to(tokens[:, 128 * c:128 * c + 128], (128, 128)).T for c in (0, 1)], axis=0
    ) * freqs
    cos, sin = cos_sin(angles)
    def rotate_keys():
        local["k"].wait()
        for g in (1, 0):
            rk[g] = rot(k[:, 256 * g:256 * g + 256], cos, sin).astype(BF)

    @pl.when(s == 0)
    def _():
        rotate_keys()
        start("k0b1")

    @pl.when(s == 1)
    def _():
        rotate_keys()
        start("k1a2")

    local["q"].wait()
    for g in (1, 0):
        for h in (0, 1):
            at = 256 * (2 * g + h)
            r = (rot(q[:, at:at + 256], cos, sin) * HD ** (-0.5)).astype(BF)
            for c in (0, 1):
                rq[g, 256 * c + 128 * h:256 * c + 128 * h + 128, :] = r[128 * c:128 * c + 128]
        if g == 1:
            @pl.when(s == 3)
            def _():
                start("q3b20")

            @pl.when(s == 2)
            def _():
                start("q2b10")

    @pl.when(s >= 2)
    def _():
        rotate_keys()

    local["v"].wait()

    def own(g):
        return rk[g], v[:, 256 * g:256 * g + 256]

    def first(g):
        return kv0[2 * g], kv0[2 * g + 1]

    def second():
        return kv1[0], kv1[1]

    def put(g, state, chunks):
        acc, _, l = state
        out = acc / l
        for i, c in enumerate(chunks):
            for h in (0, 1):
                at = 256 * i + 128 * h
                col = 256 * (2 * g + h)
                att[128 * c:128 * c + 128, col:col + 256] = out[:, at:at + 128].T.astype(BF)

    def send_state(state, out_to, lse_to, *names):
        acc, m, l = state
        out_to[...] = (acc / l).astype(BF)
        lse_to[...] = jnp.broadcast_to(m + jnp.log(l), lse_to.shape)
        start(*names)

    def hold(g, state):
        acc, m, l = state
        st_acc[g] = acc
        st_ml[g, 0:8] = jnp.broadcast_to(m, (8, 512))
        st_ml[g, 8:16] = jnp.broadcast_to(l, (8, 512))

    def held(g, c):
        lanes = slice(256 * c, 256 * c + 256)
        return st_acc[g, :, lanes], st_ml[g, 0:1, lanes], st_ml[g, 8:9, lanes]

    def prepare_direction():
        local["dir"].wait()
        whole = direction[...].reshape(1, 2 * half)
        scale = 1.0 / jnp.sqrt(jnp.sum(whole * whole, axis=1, keepdims=True) + 1e-06)
        lane = lax.broadcasted_iota(jnp.int32, (1, window), 1)
        shared = jnp.where(core == 0, 0, shift)
        keep_lane = (lane < shared) | (lane >= shared + (window - shift))
        for i, x in enumerate((x_other, x_here)):
            mine = jnp.where(x == 0, whole[:, :half], whole[:, half:]) * scale
            low, high = mine[:, :window], mine[:, shift:]
            urow[2 * i:2 * i + 1] = jnp.where(keep_lane, jnp.where(core == 0, high, low), 0.0)
            urow[2 * i + 1:2 * i + 2] = jnp.where(core == 0, low, high)
        for at in range(0, window, 128):
            ldir[at:at + 128, :] = jnp.broadcast_to(urow[3:4, at:at + 128], (128, 128)).T

    @pl.when(s == 0)
    def _():
        sent("v0b1")
        start("v0a2")
        put(1, attend(rq[1], [own(1)], True), (0, 1))
        sent("k0b1")
        start("k0a2")
        put(0, attend(rq[0], [own(0)], True), (0, 1))

    @pl.when(s == 2)
    def _():
        recv("q3b20")
        start("f3b10")
        sent("q2b10")
        start("q2b11")
        state = attend(rq3[1, 0:256, :], [own(1)], False)
        send_state(state, s_b2.at[0], t_b2.at[0], "o3b0", "l3b0")
        hold(1, attend(rq[1], [own(1)], True))

    @pl.when(s == 3)
    def _():
        sent("q3b20")
        start("q3a20")
        hold(0, attend(rq[0], [own(0)], True))
        sent("q3a20")
        start("q3b21")
        hold(1, attend(rq[1], [own(1)], True))

    prepare_direction()

    @pl.when(s == 0)
    def _():
        sent("v0a2", "k0a2")
        start("v0a1", "k0a1")

    @pl.when(s == 1)
    def _():
        recv("v0b1", "k0b1")
        for c in (0, 1):
            n = str(c)
            rows = slice(256 * c, 256 * c + 256)
            recv("q2b1" + n)
            state = attend(rq2[rows, :], [first(1), own(1)], False)
            send_state(state, s_c.at[0, c], t_c.at[0, c], "o2b" + n, "l2b" + n)
            recv("f3b1" + n)
            state = attend(rq3[1, rows, :], [first(1), own(1)], False)
            send_state(state, s_c.at[1, c], t_c.at[1, c], "o3c" + n, "l3c" + n)
        put(1, attend(rq[1], [first(1), own(1)], True), (0, 1))
        recv("v0a1", "k0a1")
        put(0, attend(rq[0], [first(0), own(0)], True), (0, 1))

    @pl.when(s == 2)
    def _():
        recv("q3b21")
        start("f3b11")
        state = attend(rq3[1, 256:512, :], [own(1)], False)
        send_state(state, s_b2.at[1], t_b2.at[1], "o3b1", "l3b1")
        recv("v1a2", "k1a2", "v0a2", "k0a2")
        for c in (0, 1):
            n = str(c)
            recv("q3a2" + n)
            rows = slice(256 * c, 256 * c + 256)
            state = attend(rq3[0, rows, :], [first(0), second(), own(0)], False)
            send_state(state, s_a.at[c], t_a.at[c], "o3a" + n, "l3a" + n)
        put(0, attend(rq[0], [first(0), second(), own(0)], True), (0, 1))

    @pl.when(s == 3)
    def _():
        sent("q3b21")
        start("q3a21")

    def x_copy(src, dst, i, dev):
        return pltpu.make_async_remote_copy(
            src_ref=src, dst_ref=dst, send_sem=xs.at[i], recv_sem=xr.at[i],
            device_id={"tensor": dev}, device_id_type=MESH)

    local["res"].wait()
    own_window = pl.ds(pl.multiple_of(core * shift, 128), window)
    peer_window = pl.ds(pl.multiple_of((1 - core) * shift, 128), window)
    own_rows = pl.ds(pl.multiple_of(core * (width - shift), 64), width)
    local_dir = ldir[own_rows, :]
    local[0].wait()
    local[1].wait()
    a_copies, b_copies, al_copies = {}, {}, {}
    for c in (0, 1):
        @pl.when(s == 3)
        def _(c=c):
            n = str(c)
            recv("o3b" + n, "l3b" + n, "o3a" + n, "l3a" + n)
            put(0, merge(held(0, c), o_a[c], l_a[c, 0:1]), (c,))
            state = merge(held(1, c), o_b2[c], l_b2[c, 0:1])
            recv("o2b" + n, "l2b" + n)
            put(1, merge(state, o_b1[c], l_b1[c, 0:1]), (c,))

        @pl.when(s == 2)
        def _(c=c):
            recv("o2b" + str(c), "l2b" + str(c))
            put(1, merge(held(1, c), o_b1[c], l_b1[c, 0:1]), (c,))

        rows = slice(128 * c, 128 * c + 128)
        part = jnp.dot(att[rows, :], wbuf[0, :, peer_window], preferred_element_type=F32)
        a_send[c] = part.astype(BF)
        a_copies[c] = x_copy(a_send.at[c], a_recv.at[c], c, core_peer)
        a_copies[c].start()
        dots[rows, :] = part * urow[0:1]
        part = jnp.dot(att[rows, :], wbuf[0, :, own_window], preferred_element_type=F32)
        dots[rows, :] += part * urow[1:2]
        keep[rows, :] = part
        a_copies[c].wait_recv()
        turn[...] = (keep[rows, :] + a_recv[c].astype(F32)).T
        b_send[c] = turn[own_rows, :].astype(BF)
        b_copies[c] = x_copy(b_send.at[c], b_recv.at[c], 4 + c, x_peer)
        b_copies[c].start()

    part = jnp.dot(att[...], wbuf[1, :, peer_window], preferred_element_type=F32)
    c_send[...] = part.astype(BF)
    c_copy = x_copy(c_send, c_recv, 2, core_peer)
    c_copy.start()
    dots[...] += part * urow[2:3]
    part = jnp.dot(att[...], wbuf[1, :, own_window], preferred_element_type=F32)
    keep[...] = part
    total = jnp.sum(dots[...] + part * urow[3:4], axis=1, keepdims=True)
    for c in (0, 1):
        lanes = slice(128 * c, 128 * c + 128)
        line = jnp.broadcast_to(total[lanes], (128, 128)).T[0:1]
        line = line + jnp.sum(res[:, lanes].astype(F32) * local_dir, axis=0, keepdims=True)
        al_send[:, lanes] = jnp.broadcast_to(line, (8, 128))
    for j in (1, 2, 3):
        al_copies[j] = pltpu.make_async_remote_copy(
            src_ref=al_send, dst_ref=al_recv.at[j - 1],
            send_sem=als.at[j - 1], recv_sem=alr.at[j - 1],
            device_id={"tensor": (t + j) % 4}, device_id_type=MESH)
        al_copies[j].start()
    c_copy.wait_recv()
    for c in (0, 1):
        lanes = slice(128 * c, 128 * c + 128)
        turn[...] = (keep[lanes, :] + c_recv[lanes, :].astype(F32)).T
        last[:, lanes] = res[:, lanes].astype(F32) + turn[own_rows, :]
    along = al_send[0:1]
    for j in (1, 2, 3):
        al_copies[j].wait_recv()
        along = along + al_recv[j - 1, 0:1]
    for c in (0, 1):
        lanes = slice(128 * c, 128 * c + 128)
        last[:, lanes] = last[:, lanes] - along[:, lanes] * local_dir
        b_copies[c].wait_recv()
        out_ref[:, lanes] = (last[:, lanes] + b_recv[c].astype(F32)).astype(BF)

    c_copy.wait_send()
    for j in (1, 2, 3):
        al_copies[j].wait_send()
    for c in (0, 1):
        a_copies[c].wait_send()
        b_copies[c].wait_send()

    @pl.when(s == 0)
    def _():
        sent("v0a1", "k0a1")

    @pl.when(s == 1)
    def _():
        sent("v1a2", "k1a2", "o2b0", "l2b0", "o2b1", "l2b1", "o3c0", "l3c0", "o3c1", "l3c1")

    @pl.when(s == 2)
    def _():
        sent("q2b11", "f3b10", "f3b11", "o3b0", "l3b0", "o3b1", "l3b1", "o3a0", "l3a0", "o3a1", "l3a1")

    @pl.when(s == 3)
    def _():
        sent("q3a21")


def fused_body(queries, key_rows, value_rows, positions, residual, direction, out_weight):
    freqs = jnp.power(10000.0, -jnp.arange(HD // 2, dtype=F32) * 2.0 / HD)[None, :]
    rows, width = residual.shape
    depth = out_weight.shape[0]
    window = 2 * width - (width // 128) * 128
    vmem = pl.BlockSpec(memory_space=pltpu.VMEM)
    anywhere = pl.BlockSpec(memory_space=pl.ANY)
    dma = pltpu.SemaphoreType.DMA
    out = pl.pallas_call(
        kernel,
        out_shape=jax.ShapeDtypeStruct((width, rows), BF),
        in_specs=[anywhere, vmem] + [anywhere] * 6,
        out_specs=vmem,
        scratch_shapes=[
            pltpu.VMEM(positions.shape, jnp.int32),
            pltpu.VMEM(direction.shape, F32),
            pltpu.VMEM(queries.shape, BF),
            pltpu.VMEM(key_rows.shape, BF),
            pltpu.VMEM(value_rows.shape, BF),
            pltpu.VMEM((width, rows), BF),
            pltpu.VMEM((2, depth, 2 * width), BF),
            pltpu.VMEM((8, window), F32),
            pltpu.VMEM((window, 128), F32),
            pltpu.VMEM((2, 512, 256), BF),
            pltpu.VMEM((2, 256, 256), BF),
            pltpu.VMEM((4, 256, 256), BF),
            pltpu.VMEM((2, 256, 256), BF),
            pltpu.VMEM((2, 512, 256), BF),
            pltpu.VMEM((512, 256), BF),
            pltpu.VMEM((2, 256, 256), BF),
            pltpu.VMEM((2, 256, 256), BF),
            pltpu.VMEM((2, 256, 256), BF),
            pltpu.VMEM((2, 8, 256), F32),
            pltpu.VMEM((2, 8, 256), F32),
            pltpu.VMEM((2, 8, 256), F32),
            pltpu.VMEM((2, 256, 256), BF),
            pltpu.VMEM((2, 256, 256), BF),
            pltpu.VMEM((2, 2, 256, 256), BF),
            pltpu.VMEM((2, 8, 256), F32),
            pltpu.VMEM((2, 8, 256), F32),
            pltpu.VMEM((2, 2, 8, 256), F32),
            pltpu.VMEM((2, 256, 512), F32),
            pltpu.VMEM((2, 16, 512), F32),
            pltpu.VMEM((256, depth), BF),
            pltpu.VMEM((256, window), F32),
            pltpu.VMEM((256, window), F32),
            pltpu.VMEM((window, 128), F32),
            pltpu.VMEM((width, 256), F32),
            pltpu.VMEM((2, 128, window), BF),
            pltpu.VMEM((2, 128, window), BF),
            pltpu.VMEM((2, width, 128), BF),
            pltpu.VMEM((2, width, 128), BF),
            pltpu.VMEM((256, window), BF),
            pltpu.VMEM((256, window), BF),
            pltpu.VMEM((8, 256), F32),
            pltpu.VMEM((3, 8, 256), F32),
            dma((8,)),
            dma((32,)),
            dma((32,)),
            dma((6,)),
            dma((6,)),
            dma((6,)),
            dma((6,)),
        ],
        compiler_params=pltpu.CompilerParams(
            collective_id=0, has_side_effects=True, vmem_limit_bytes=60 * 1024 * 1024
        ),
    )(positions, freqs, queries, key_rows, value_rows, residual.T, direction, out_weight)
    return out.T


def device_body(*args):
    queries, key_rows, _, _, residual, direction, _ = args
    fits = (
        lax.axis_size("seq") == 4
        and lax.axis_size("tensor") == 4
        and queries.shape == (256, 1024)
        and key_rows.shape == (256, 512)
        and residual.shape[1] * 4 == direction.shape[0]
        and residual.shape[1] % 128 == 64
        and WINDOW == 1024
    )
    return fused_body(*args) if fits else body(*args)


def solution(mesh):
    return jax.shard_map(
        device_body,
        mesh=mesh,
        in_specs=(
            P(("groups", "seq"), "tensor"),
            P(("groups", "seq"), "tensor"),
            P(("groups", "seq"), "tensor"),
            P(("groups", "seq")),
            P(("groups", "seq"), "tensor"),
            P("groups"),
            P("tensor", None),
        ),
        out_specs=P(("groups", "seq"), "tensor"),
        check_vma=False,
    )
```

```python
import functools

import jax
import jax.numpy as jnp
from jax import lax
from jax.experimental import pallas as pl
from jax.experimental.pallas import tpu as pltpu
from jax.sharding import PartitionSpec as P

HD = 256
WINDOW = 1024


big_negative = -1e30


def shifted_2(value, axis, steps):
    count = lax.axis_size(axis)
    first, last = (max(0, -steps), min(count, count - steps))
    return lax.ppermute(value, axis, [(source, source + steps) for source in range(first, last)])


def rotary_tables(positions, head_dim):
    half_dim = head_dim // 2
    freqs = jnp.power(10000.0, -jnp.arange(half_dim, dtype=jnp.float32) * 2.0 / head_dim)
    angles = positions.astype(jnp.float32)[:, None] * freqs[None, :]
    return (jnp.cos(angles)[:, None, :], jnp.sin(angles)[:, None, :])


def rotate_heads(block, cos_table, sin_table, head_dim):
    row_count = block.shape[0]
    head_count = block.shape[1] // head_dim
    half_dim = head_dim // 2
    widened = block.reshape(row_count, head_count, head_dim).astype(jnp.float32)
    first_half = widened[:, :, :half_dim]
    second_half = widened[:, :, half_dim:]
    turned = jnp.concatenate(
        [
            first_half * cos_table - second_half * sin_table,
            second_half * cos_table + first_half * sin_table,
        ],
        axis=-1,
    )
    return turned.reshape(row_count, head_count * head_dim)


def body(queries, key_rows, value_rows, positions, residual, direction, out_weight):
    tokens_here = queries.shape[0]
    query_heads = queries.shape[1] // HD
    kv_heads = key_rows.shape[1] // HD
    group_size = query_heads // kv_heads
    span_blocks = WINDOW // tokens_here
    seq_index = lax.axis_index("seq")
    cos_table, sin_table = rotary_tables(positions, HD)
    rot_queries = (rotate_heads(queries, cos_table, sin_table, HD) * HD ** (-0.5)).astype(
        jnp.bfloat16
    )
    rot_keys = rotate_heads(key_rows, cos_table, sin_table, HD).astype(jnp.bfloat16)
    query_blocks = rot_queries.reshape(tokens_here, kv_heads, group_size, HD)
    own_scores = jnp.einsum(
        "qkgd,skd->kgqs",
        query_blocks,
        rot_keys.reshape(tokens_here, kv_heads, HD),
        preferred_element_type=jnp.float32,
    )
    earlier_keys = []
    earlier_values = []
    for distance in range(span_blocks, 0, -1):
        moved_keys, moved_values = shifted_2((rot_keys, value_rows), "seq", distance)
        earlier_keys.append(moved_keys)
        earlier_values.append(moved_values)
    far_keys = jnp.concatenate(earlier_keys, axis=0)
    far_values = jnp.concatenate(earlier_values, axis=0)
    far_scores = jnp.einsum(
        "qkgd,skd->kgqs",
        query_blocks,
        far_keys.reshape(-1, kv_heads, HD),
        preferred_element_type=jnp.float32,
    )
    scores = jnp.concatenate([far_scores, own_scores], axis=-1)
    query_index = seq_index * tokens_here + jnp.arange(tokens_here, dtype=jnp.int32)
    key_index = (seq_index - span_blocks) * tokens_here + jnp.arange(
        (span_blocks + 1) * tokens_here, dtype=jnp.int32
    )
    gap_grid = query_index[:, None] - key_index[None, :]
    allowed = (gap_grid >= 0) & (gap_grid < WINDOW) & (key_index[None, :] >= 0)
    scores = jnp.where(allowed, scores, big_negative)
    row_max = jnp.max(scores, axis=-1, keepdims=True)
    shifted = jnp.exp(scores - row_max)
    row_sum = jnp.sum(shifted, axis=-1, keepdims=True)
    weights = (shifted / row_sum).astype(jnp.bfloat16)
    every_value = jnp.concatenate([far_values, value_rows], axis=0).reshape(-1, kv_heads, HD)
    mixed = jnp.einsum("kgqs,skd->qkgd", weights, every_value, preferred_element_type=jnp.float32)
    attended = mixed.astype(jnp.bfloat16).reshape(tokens_here, query_heads * HD)
    partial_value = jnp.dot(attended, out_weight, preferred_element_type=jnp.float32)
    unit_dir = direction / jnp.sqrt(jnp.sum(direction * direction) + 1e-06)
    column_width = residual.shape[1]
    tensor_index = lax.axis_index("tensor")
    local_dir = lax.dynamic_slice_in_dim(unit_dir, tensor_index * column_width, column_width, 0)
    base_state = residual.astype(jnp.float32)
    rounded_terms = partial_value.astype(jnp.bfloat16).astype(jnp.float32)
    dot_terms = jnp.sum(rounded_terms * unit_dir[None, :], axis=1) + jnp.sum(
        base_state * local_dir[None, :], axis=1
    )
    along = lax.psum(dot_terms, "tensor")
    summed = lax.psum_scatter(
        partial_value.astype(jnp.bfloat16), "tensor", scatter_dimension=1, tiled=True
    ).astype(jnp.float32)
    hidden_state = base_state + summed
    ablated = (hidden_state - along[:, None] * local_dir[None, :]).astype(jnp.bfloat16)
    return ablated


BF = jnp.bfloat16
F32 = jnp.float32
MESH = pl.DeviceIdType.MESH

def rot(x, cos, sin):
    x = x.astype(F32)
    a, b = x[:, :128], x[:, 128:]
    return jnp.concatenate([a * cos - b * sin, b * cos + a * sin], axis=1)


def cos_sin(x):
    n = jnp.floor(x * 0.15915494309189535 + 0.5)
    r = ((x - n * 6.28125) - n * (507.0 / 262144.0)) - n * 1.2556659146019e-06
    k = jnp.floor(r * 0.6366197723675814 + 0.5)
    y = (r - k * 1.5707963705062866) + k * 4.371139000186241e-08
    z = y * y
    sin = y + y * z * (-1.0 / 6 + z * (1.0 / 120 + z * (-1.0 / 5040 + z * (1.0 / 362880))))
    cos = 1.0 + z * (-0.5 + z * (1.0 / 24 + z * (-1.0 / 720 + z * (1.0 / 40320))))
    odd = jnp.abs(k) == 1.0
    flip = jnp.abs(k) == 2.0
    cos_out = jnp.where(odd, -k * sin, jnp.where(flip, -cos, cos))
    sin_out = jnp.where(odd, k * cos, jnp.where(flip, -sin, sin))
    return cos_out, sin_out


def attend(q, blocks, diag):
    scores = [
        lax.dot_general(k, q, (((1,), (1,)), ((), ())), preferred_element_type=F32)
        for k, _ in blocks
    ]
    if diag:
        s = scores[-1]
        key = lax.broadcasted_iota(jnp.int32, s.shape, 0)
        lane = lax.broadcasted_iota(jnp.int32, s.shape, 1)
        row = (lane // 256) * 128 + lane % 128
        scores[-1] = jnp.where(key <= row, s, big_negative)
    m = functools.reduce(jnp.maximum, [jnp.max(s, axis=0, keepdims=True) for s in scores])
    acc, l = 0.0, 0.0
    for s, (_, v) in zip(scores, blocks):
        p = jnp.exp(s - m)
        l = l + jnp.sum(p, axis=0, keepdims=True)
        acc = acc + lax.dot_general(
            v, p.astype(BF), (((0,), (0,)), ((), ())), preferred_element_type=F32
        )
    return acc, m, l


def merge(state, out, lse):
    acc, m, l = state
    top = jnp.maximum(m, lse)
    mine, other = jnp.exp(m - top), jnp.exp(lse - top)
    return acc * mine + out.astype(F32) * other, top, l * mine + other


def kernel(pos_hbm, freq_ref, q_hbm, k_hbm, v_hbm, res_hbm, dir_hbm, w_hbm, out_ref,
           pos, direction, q, k, v, res, wbuf, urow, ldir, rq, rk, kv0, kv1, rq3, rq2,
           o_a, o_b2, o_b1, l_a, l_b2, l_b1, s_a, s_b2, s_c, t_a, t_b2, t_c,
           st_acc, st_ml, att, keep, dots, turn, last, a_send, a_recv, b_send, b_recv,
           c_send, c_recv, al_send, al_recv,
           lsem, ssem, rsem, xs, xr, als, alr):
    s = lax.axis_index("seq")
    t = lax.axis_index("tensor")
    core = t % 2
    x_here = t // 2
    x_other = 1 - x_here
    core_peer = t + 1 - 2 * core
    x_peer = (t + 2) % 4
    half = wbuf.shape[2]
    width = half // 2
    shift = (width // 128) * 128
    window = half - shift

    local = {}

    def fetch(name, src, dst):
        local[name] = pltpu.make_async_copy(src, dst, lsem.at[len(local)])
        local[name].start()

    fetch("pos", pos_hbm, pos)
    fetch("k", k_hbm, k)
    fetch("q", q_hbm, q)
    fetch("v", v_hbm, v)
    for i, x in enumerate((x_other, x_here)):
        cols = pl.ds(pl.multiple_of(x * half, 128), half)
        fetch(i, w_hbm.at[:, cols], wbuf.at[i])
    fetch("dir", dir_hbm, direction)
    fetch("res", res_hbm, res)

    barrier = pltpu.get_barrier_semaphore()
    for j in (1, 2, 3):
        pl.semaphore_signal(barrier, inc=1, device_id={"seq": (s + j) % 4}, device_id_type=MESH)
        pl.semaphore_signal(barrier, inc=1, device_id={"tensor": (t + j) % 4}, device_id_type=MESH)
    pl.semaphore_wait(barrier, 6)

    copies, index = {}, {}

    def add(name, dev, src, dst, lands_as=None):
        i = index[name] = len(index)
        copies[name] = pltpu.make_async_remote_copy(
            src_ref=src, dst_ref=dst, send_sem=ssem.at[i],
            recv_sem=rsem.at[i if lands_as is None else index[lands_as]],
            device_id={"seq": dev}, device_id_type=MESH)

    for g, name in ((0, "a"), (1, "b")):
        cols = slice(256 * g, 256 * g + 256)
        add("v0" + name + "1", 1, v_hbm.at[:, cols], kv0.at[2 * g + 1])
        add("k0" + name + "1", 1, rk.at[g], kv0.at[2 * g])
    add("v0a2", 2, v_hbm.at[:, 0:256], kv0.at[1])
    add("k0a2", 2, rk.at[0], kv0.at[0])
    add("v1a2", 2, v_hbm.at[:, 0:256], kv1.at[1])
    add("k1a2", 2, rk.at[0], kv1.at[0])
    for c in (0, 1):
        rows = slice(256 * c, 256 * c + 256)
        n = str(c)
        add("q3b2" + n, 2, rq.at[1, rows], rq3.at[1, rows])
        add("q3a2" + n, 2, rq.at[0, rows], rq3.at[0, rows])
        add("o3b" + n, 3, s_b2.at[c], o_b2.at[c])
        add("l3b" + n, 3, t_b2.at[c], l_b2.at[c])
        add("f3b1" + n, 1, rq3.at[1, rows], rq3.at[1, rows])
        add("q2b1" + n, 1, rq.at[1, rows], rq2.at[rows])
        add("o3a" + n, 3, s_a.at[c], o_a.at[c])
        add("l3a" + n, 3, t_a.at[c], l_a.at[c])
        add("o2b" + n, 2, s_c.at[0, c], o_b1.at[c])
        add("l2b" + n, 2, t_c.at[0, c], l_b1.at[c])
        add("o3c" + n, 3, s_c.at[1, c], o_b1.at[c], "o2b" + n)
        add("l3c" + n, 3, t_c.at[1, c], l_b1.at[c], "l2b" + n)

    def start(*names):
        for n in names:
            copies[n].start()

    def recv(*names):
        for n in names:
            copies[n].wait_recv()

    def sent(*names):
        for n in names:
            copies[n].wait_send()

    @pl.when(s == 0)
    def _():
        start("v0b1", "v0a2")

    @pl.when(s == 1)
    def _():
        start("v1a2")

    local["pos"].wait()
    freqs = freq_ref[...]
    tokens = pos[...].astype(F32).reshape(1, 256)
    angles = jnp.concatenate(
        [jnp.broadcast_to(tokens[:, 128 * c:128 * c + 128], (128, 128)).T for c in (0, 1)], axis=0
    ) * freqs
    cos, sin = cos_sin(angles)
    def rotate_keys():
        local["k"].wait()
        for g in (1, 0):
            rk[g] = rot(k[:, 256 * g:256 * g + 256], cos, sin).astype(BF)

    @pl.when(s == 0)
    def _():
        rotate_keys()
        start("k0b1", "k0a2", "v0a1", "k0a1")

    @pl.when(s == 1)
    def _():
        rotate_keys()
        start("k1a2")

    local["q"].wait()
    for g in (1, 0):
        for h in (0, 1):
            at = 256 * (2 * g + h)
            r = (rot(q[:, at:at + 256], cos, sin) * HD ** (-0.5)).astype(BF)
            for c in (0, 1):
                rq[g, 256 * c + 128 * h:256 * c + 128 * h + 128, :] = r[128 * c:128 * c + 128]
        if g == 1:
            @pl.when(s == 3)
            def _():
                start("q3b20")

            @pl.when(s == 2)
            def _():
                start("q2b10", "q2b11")

    @pl.when(s >= 2)
    def _():
        rotate_keys()

    local["v"].wait()

    def own(g):
        return rk[g], v[:, 256 * g:256 * g + 256]

    def first(g):
        return kv0[2 * g], kv0[2 * g + 1]

    def second():
        return kv1[0], kv1[1]

    def put(g, state, chunks):
        acc, _, l = state
        out = acc / l
        for i, c in enumerate(chunks):
            for h in (0, 1):
                at = 256 * i + 128 * h
                col = 256 * (2 * g + h)
                att[128 * c:128 * c + 128, col:col + 256] = out[:, at:at + 128].T.astype(BF)

    def send_state(state, out_to, lse_to, *names):
        acc, m, l = state
        out_to[...] = (acc / l).astype(BF)
        lse_to[...] = jnp.broadcast_to(m + jnp.log(l), lse_to.shape)
        start(*names)

    def hold(g, state):
        acc, m, l = state
        st_acc[g] = acc
        st_ml[g, 0:8] = jnp.broadcast_to(m, (8, 512))
        st_ml[g, 8:16] = jnp.broadcast_to(l, (8, 512))

    def held(g, c):
        lanes = slice(256 * c, 256 * c + 256)
        return st_acc[g, :, lanes], st_ml[g, 0:1, lanes], st_ml[g, 8:9, lanes]

    def prepare_direction():
        local["dir"].wait()
        whole = direction[...].reshape(1, 2 * half)
        scale = 1.0 / jnp.sqrt(jnp.sum(whole * whole, axis=1, keepdims=True) + 1e-06)
        lane = lax.broadcasted_iota(jnp.int32, (1, window), 1)
        shared = jnp.where(core == 0, 0, shift)
        keep_lane = (lane < shared) | (lane >= shared + (window - shift))
        for i, x in enumerate((x_other, x_here)):
            mine = jnp.where(x == 0, whole[:, :half], whole[:, half:]) * scale
            low, high = mine[:, :window], mine[:, shift:]
            urow[2 * i:2 * i + 1] = jnp.where(keep_lane, jnp.where(core == 0, high, low), 0.0)
            urow[2 * i + 1:2 * i + 2] = jnp.where(core == 0, low, high)
        for at in range(0, window, 128):
            ldir[at:at + 128, :] = jnp.broadcast_to(urow[3:4, at:at + 128], (128, 128)).T

    @pl.when(s == 0)
    def _():
        put(1, attend(rq[1], [own(1)], True), (0, 1))
        put(0, attend(rq[0], [own(0)], True), (0, 1))

    @pl.when(s == 2)
    def _():
        recv("q3b20")
        start("f3b10")
        state = attend(rq3[1, 0:256, :], [own(1)], False)
        send_state(state, s_b2.at[0], t_b2.at[0], "o3b0", "l3b0")
        hold(1, attend(rq[1], [own(1)], True))

    @pl.when(s == 3)
    def _():
        start("q3a20", "q3b21", "q3a21")
        hold(0, attend(rq[0], [own(0)], True))
        hold(1, attend(rq[1], [own(1)], True))

    prepare_direction()

    @pl.when(s == 1)
    def _():
        recv("v0b1", "k0b1")
        for c in (0, 1):
            n = str(c)
            rows = slice(256 * c, 256 * c + 256)
            recv("q2b1" + n)
            state = attend(rq2[rows, :], [first(1), own(1)], False)
            send_state(state, s_c.at[0, c], t_c.at[0, c], "o2b" + n, "l2b" + n)
            recv("f3b1" + n)
            state = attend(rq3[1, rows, :], [first(1), own(1)], False)
            send_state(state, s_c.at[1, c], t_c.at[1, c], "o3c" + n, "l3c" + n)
        put(1, attend(rq[1], [first(1), own(1)], True), (0, 1))
        recv("v0a1", "k0a1")
        put(0, attend(rq[0], [first(0), own(0)], True), (0, 1))

    @pl.when(s == 2)
    def _():
        recv("q3b21")
        start("f3b11")
        state = attend(rq3[1, 256:512, :], [own(1)], False)
        send_state(state, s_b2.at[1], t_b2.at[1], "o3b1", "l3b1")
        recv("v1a2", "k1a2", "v0a2", "k0a2")
        for c in (0, 1):
            n = str(c)
            recv("q3a2" + n)
            rows = slice(256 * c, 256 * c + 256)
            state = attend(rq3[0, rows, :], [first(0), second(), own(0)], False)
            send_state(state, s_a.at[c], t_a.at[c], "o3a" + n, "l3a" + n)
        put(0, attend(rq[0], [first(0), second(), own(0)], True), (0, 1))

    def x_copies(src, dst, first, dev):
        part = src.shape[0] // 4
        return [
            pltpu.make_async_remote_copy(
                src_ref=src.at[part * j:part * j + part], dst_ref=dst.at[part * j:part * j + part],
                send_sem=xs.at[first + j], recv_sem=xr.at[first + j],
                device_id={"tensor": dev}, device_id_type=MESH)
            for j in range(4)
        ]

    def begin(parts):
        for part in parts:
            part.start()

    def arrive(parts):
        for part in parts:
            part.wait_recv()

    def leave(parts):
        for part in parts:
            part.wait_send()

    local["res"].wait()
    own_window = pl.ds(pl.multiple_of(core * shift, 128), window)
    peer_window = pl.ds(pl.multiple_of((1 - core) * shift, 128), window)
    own_rows = pl.ds(pl.multiple_of(core * (width - shift), 64), width)
    local_dir = ldir[own_rows, :]
    local[0].wait()
    local[1].wait()
    a_copies, b_copies, al_copies = {}, {}, {}
    for c in (0, 1):
        @pl.when(s == 3)
        def _(c=c):
            n = str(c)
            recv("o3b" + n, "l3b" + n, "o3a" + n, "l3a" + n)
            put(0, merge(held(0, c), o_a[c], l_a[c, 0:1]), (c,))
            state = merge(held(1, c), o_b2[c], l_b2[c, 0:1])
            recv("o2b" + n, "l2b" + n)
            put(1, merge(state, o_b1[c], l_b1[c, 0:1]), (c,))

        @pl.when(s == 2)
        def _(c=c):
            recv("o2b" + str(c), "l2b" + str(c))
            put(1, merge(held(1, c), o_b1[c], l_b1[c, 0:1]), (c,))

        rows = slice(128 * c, 128 * c + 128)
        part = jnp.dot(att[rows, :], wbuf[0, :, peer_window], preferred_element_type=F32)
        a_send[c] = part.astype(BF)
        a_copies[c] = x_copies(a_send.at[c], a_recv.at[c], 4 * c, core_peer)
        begin(a_copies[c])
        dots[rows, :] = part * urow[0:1]
        part = jnp.dot(att[rows, :], wbuf[0, :, own_window], preferred_element_type=F32)
        dots[rows, :] += part * urow[1:2]
        keep[rows, :] = part
        arrive(a_copies[c])
        turn[...] = (keep[rows, :] + a_recv[c].astype(F32)).T
        b_send[c] = turn[own_rows, :].astype(BF)
        b_copies[c] = x_copies(b_send.at[c], b_recv.at[c], 8 + 4 * c, x_peer)
        begin(b_copies[c])

    part = jnp.dot(att[...], wbuf[1, :, peer_window], preferred_element_type=F32)
    c_send[...] = part.astype(BF)
    c_copy = x_copies(c_send, c_recv, 16, core_peer)
    begin(c_copy)
    dots[...] += part * urow[2:3]
    part = jnp.dot(att[...], wbuf[1, :, own_window], preferred_element_type=F32)
    keep[...] = part
    total = jnp.sum(dots[...] + part * urow[3:4], axis=1, keepdims=True)
    for c in (0, 1):
        lanes = slice(128 * c, 128 * c + 128)
        line = jnp.broadcast_to(total[lanes], (128, 128)).T[0:1]
        line = line + jnp.sum(res[:, lanes].astype(F32) * local_dir, axis=0, keepdims=True)
        al_send[:, lanes] = jnp.broadcast_to(line, (8, 128))
    for j in (1, 2, 3):
        al_copies[j] = pltpu.make_async_remote_copy(
            src_ref=al_send, dst_ref=al_recv.at[j - 1],
            send_sem=als.at[j - 1], recv_sem=alr.at[j - 1],
            device_id={"tensor": (t + j) % 4}, device_id_type=MESH)
        al_copies[j].start()
    arrive(c_copy)
    for c in (0, 1):
        lanes = slice(128 * c, 128 * c + 128)
        turn[...] = (keep[lanes, :] + c_recv[lanes, :].astype(F32)).T
        last[:, lanes] = res[:, lanes].astype(F32) + turn[own_rows, :]
    along = al_send[0:1]
    for j in (1, 2, 3):
        al_copies[j].wait_recv()
        along = along + al_recv[j - 1, 0:1]
    for c in (0, 1):
        lanes = slice(128 * c, 128 * c + 128)
        last[:, lanes] = last[:, lanes] - along[:, lanes] * local_dir
        arrive(b_copies[c])
        out_ref[:, lanes] = (last[:, lanes] + b_recv[c].astype(F32)).astype(BF)

    leave(c_copy)
    for j in (1, 2, 3):
        al_copies[j].wait_send()
    for c in (0, 1):
        leave(a_copies[c])
        leave(b_copies[c])

    @pl.when(s == 0)
    def _():
        sent("v0b1", "k0b1", "v0a2", "k0a2", "v0a1", "k0a1")

    @pl.when(s == 1)
    def _():
        sent("v1a2", "k1a2", "o2b0", "l2b0", "o2b1", "l2b1", "o3c0", "l3c0", "o3c1", "l3c1")

    @pl.when(s == 2)
    def _():
        sent("q2b10", "q2b11", "f3b10", "f3b11", "o3b0", "l3b0", "o3b1", "l3b1", "o3a0", "l3a0", "o3a1", "l3a1")

    @pl.when(s == 3)
    def _():
        sent("q3b20", "q3a20", "q3b21", "q3a21")


def fused_body(queries, key_rows, value_rows, positions, residual, direction, out_weight):
    freqs = jnp.power(10000.0, -jnp.arange(HD // 2, dtype=F32) * 2.0 / HD)[None, :]
    rows, width = residual.shape
    depth = out_weight.shape[0]
    window = 2 * width - (width // 128) * 128
    vmem = pl.BlockSpec(memory_space=pltpu.VMEM)
    anywhere = pl.BlockSpec(memory_space=pl.ANY)
    dma = pltpu.SemaphoreType.DMA
    out = pl.pallas_call(
        kernel,
        out_shape=jax.ShapeDtypeStruct((width, rows), BF),
        in_specs=[anywhere, vmem] + [anywhere] * 6,
        out_specs=vmem,
        scratch_shapes=[
            pltpu.VMEM(positions.shape, jnp.int32),
            pltpu.VMEM(direction.shape, F32),
            pltpu.VMEM(queries.shape, BF),
            pltpu.VMEM(key_rows.shape, BF),
            pltpu.VMEM(value_rows.shape, BF),
            pltpu.VMEM((width, rows), BF),
            pltpu.VMEM((2, depth, 2 * width), BF),
            pltpu.VMEM((8, window), F32),
            pltpu.VMEM((window, 128), F32),
            pltpu.VMEM((2, 512, 256), BF),
            pltpu.VMEM((2, 256, 256), BF),
            pltpu.VMEM((4, 256, 256), BF),
            pltpu.VMEM((2, 256, 256), BF),
            pltpu.VMEM((2, 512, 256), BF),
            pltpu.VMEM((512, 256), BF),
            pltpu.VMEM((2, 256, 256), BF),
            pltpu.VMEM((2, 256, 256), BF),
            pltpu.VMEM((2, 256, 256), BF),
            pltpu.VMEM((2, 8, 256), F32),
            pltpu.VMEM((2, 8, 256), F32),
            pltpu.VMEM((2, 8, 256), F32),
            pltpu.VMEM((2, 256, 256), BF),
            pltpu.VMEM((2, 256, 256), BF),
            pltpu.VMEM((2, 2, 256, 256), BF),
            pltpu.VMEM((2, 8, 256), F32),
            pltpu.VMEM((2, 8, 256), F32),
            pltpu.VMEM((2, 2, 8, 256), F32),
            pltpu.VMEM((2, 256, 512), F32),
            pltpu.VMEM((2, 16, 512), F32),
            pltpu.VMEM((256, depth), BF),
            pltpu.VMEM((256, window), F32),
            pltpu.VMEM((256, window), F32),
            pltpu.VMEM((window, 128), F32),
            pltpu.VMEM((width, 256), F32),
            pltpu.VMEM((2, 128, window), BF),
            pltpu.VMEM((2, 128, window), BF),
            pltpu.VMEM((2, width, 128), BF),
            pltpu.VMEM((2, width, 128), BF),
            pltpu.VMEM((256, window), BF),
            pltpu.VMEM((256, window), BF),
            pltpu.VMEM((8, 256), F32),
            pltpu.VMEM((3, 8, 256), F32),
            dma((8,)),
            dma((32,)),
            dma((32,)),
            dma((20,)),
            dma((20,)),
            dma((3,)),
            dma((3,)),
        ],
        compiler_params=pltpu.CompilerParams(
            collective_id=0, has_side_effects=True, vmem_limit_bytes=60 * 1024 * 1024
        ),
    )(positions, freqs, queries, key_rows, value_rows, residual.T, direction, out_weight)
    return out.T


def device_body(*args):
    queries, key_rows, _, _, residual, direction, _ = args
    fits = (
        lax.axis_size("seq") == 4
        and lax.axis_size("tensor") == 4
        and queries.shape == (256, 1024)
        and key_rows.shape == (256, 512)
        and residual.shape[1] * 4 == direction.shape[0]
        and residual.shape[1] % 128 == 64
        and WINDOW == 1024
    )
    return fused_body(*args) if fits else body(*args)


def solution(mesh):
    return jax.shard_map(
        device_body,
        mesh=mesh,
        in_specs=(
            P(("groups", "seq"), "tensor"),
            P(("groups", "seq"), "tensor"),
            P(("groups", "seq"), "tensor"),
            P(("groups", "seq")),
            P(("groups", "seq"), "tensor"),
            P("groups"),
            P("tensor", None),
        ),
        out_specs=P(("groups", "seq"), "tensor"),
        check_vma=False,
    )
```

```python
import functools

import jax
import jax.numpy as jnp
from jax import lax
from jax.experimental import pallas as pl
from jax.experimental.pallas import tpu as pltpu
from jax.sharding import PartitionSpec as P

HD = 256
WINDOW = 1024


big_negative = -1e30


def shifted_2(value, axis, steps):
    count = lax.axis_size(axis)
    first, last = (max(0, -steps), min(count, count - steps))
    return lax.ppermute(value, axis, [(source, source + steps) for source in range(first, last)])


def rotary_tables(positions, head_dim):
    half_dim = head_dim // 2
    freqs = jnp.power(10000.0, -jnp.arange(half_dim, dtype=jnp.float32) * 2.0 / head_dim)
    angles = positions.astype(jnp.float32)[:, None] * freqs[None, :]
    return (jnp.cos(angles)[:, None, :], jnp.sin(angles)[:, None, :])


def rotate_heads(block, cos_table, sin_table, head_dim):
    row_count = block.shape[0]
    head_count = block.shape[1] // head_dim
    half_dim = head_dim // 2
    widened = block.reshape(row_count, head_count, head_dim).astype(jnp.float32)
    first_half = widened[:, :, :half_dim]
    second_half = widened[:, :, half_dim:]
    turned = jnp.concatenate(
        [
            first_half * cos_table - second_half * sin_table,
            second_half * cos_table + first_half * sin_table,
        ],
        axis=-1,
    )
    return turned.reshape(row_count, head_count * head_dim)


def body(queries, key_rows, value_rows, positions, residual, direction, out_weight):
    tokens_here = queries.shape[0]
    query_heads = queries.shape[1] // HD
    kv_heads = key_rows.shape[1] // HD
    group_size = query_heads // kv_heads
    span_blocks = WINDOW // tokens_here
    seq_index = lax.axis_index("seq")
    cos_table, sin_table = rotary_tables(positions, HD)
    rot_queries = (rotate_heads(queries, cos_table, sin_table, HD) * HD ** (-0.5)).astype(
        jnp.bfloat16
    )
    rot_keys = rotate_heads(key_rows, cos_table, sin_table, HD).astype(jnp.bfloat16)
    query_blocks = rot_queries.reshape(tokens_here, kv_heads, group_size, HD)
    own_scores = jnp.einsum(
        "qkgd,skd->kgqs",
        query_blocks,
        rot_keys.reshape(tokens_here, kv_heads, HD),
        preferred_element_type=jnp.float32,
    )
    earlier_keys = []
    earlier_values = []
    for distance in range(span_blocks, 0, -1):
        moved_keys, moved_values = shifted_2((rot_keys, value_rows), "seq", distance)
        earlier_keys.append(moved_keys)
        earlier_values.append(moved_values)
    far_keys = jnp.concatenate(earlier_keys, axis=0)
    far_values = jnp.concatenate(earlier_values, axis=0)
    far_scores = jnp.einsum(
        "qkgd,skd->kgqs",
        query_blocks,
        far_keys.reshape(-1, kv_heads, HD),
        preferred_element_type=jnp.float32,
    )
    scores = jnp.concatenate([far_scores, own_scores], axis=-1)
    query_index = seq_index * tokens_here + jnp.arange(tokens_here, dtype=jnp.int32)
    key_index = (seq_index - span_blocks) * tokens_here + jnp.arange(
        (span_blocks + 1) * tokens_here, dtype=jnp.int32
    )
    gap_grid = query_index[:, None] - key_index[None, :]
    allowed = (gap_grid >= 0) & (gap_grid < WINDOW) & (key_index[None, :] >= 0)
    scores = jnp.where(allowed, scores, big_negative)
    row_max = jnp.max(scores, axis=-1, keepdims=True)
    shifted = jnp.exp(scores - row_max)
    row_sum = jnp.sum(shifted, axis=-1, keepdims=True)
    weights = (shifted / row_sum).astype(jnp.bfloat16)
    every_value = jnp.concatenate([far_values, value_rows], axis=0).reshape(-1, kv_heads, HD)
    mixed = jnp.einsum("kgqs,skd->qkgd", weights, every_value, preferred_element_type=jnp.float32)
    attended = mixed.astype(jnp.bfloat16).reshape(tokens_here, query_heads * HD)
    partial_value = jnp.dot(attended, out_weight, preferred_element_type=jnp.float32)
    unit_dir = direction / jnp.sqrt(jnp.sum(direction * direction) + 1e-06)
    column_width = residual.shape[1]
    tensor_index = lax.axis_index("tensor")
    local_dir = lax.dynamic_slice_in_dim(unit_dir, tensor_index * column_width, column_width, 0)
    base_state = residual.astype(jnp.float32)
    rounded_terms = partial_value.astype(jnp.bfloat16).astype(jnp.float32)
    dot_terms = jnp.sum(rounded_terms * unit_dir[None, :], axis=1) + jnp.sum(
        base_state * local_dir[None, :], axis=1
    )
    along = lax.psum(dot_terms, "tensor")
    summed = lax.psum_scatter(
        partial_value.astype(jnp.bfloat16), "tensor", scatter_dimension=1, tiled=True
    ).astype(jnp.float32)
    hidden_state = base_state + summed
    ablated = (hidden_state - along[:, None] * local_dir[None, :]).astype(jnp.bfloat16)
    return ablated


BF = jnp.bfloat16
F32 = jnp.float32
MESH = pl.DeviceIdType.MESH

def rot(x, cos, sin):
    x = x.astype(F32)
    a, b = x[:, :128], x[:, 128:]
    return jnp.concatenate([a * cos - b * sin, b * cos + a * sin], axis=1)


def cos_sin(x):
    n = jnp.floor(x * 0.15915494309189535 + 0.5)
    r = ((x - n * 6.28125) - n * (507.0 / 262144.0)) - n * 1.2556659146019e-06
    k = jnp.floor(r * 0.6366197723675814 + 0.5)
    y = (r - k * 1.5707963705062866) + k * 4.371139000186241e-08
    z = y * y
    sin = y + y * z * (-1.0 / 6 + z * (1.0 / 120 + z * (-1.0 / 5040 + z * (1.0 / 362880))))
    cos = 1.0 + z * (-0.5 + z * (1.0 / 24 + z * (-1.0 / 720 + z * (1.0 / 40320))))
    odd = jnp.abs(k) == 1.0
    flip = jnp.abs(k) == 2.0
    cos_out = jnp.where(odd, -k * sin, jnp.where(flip, -cos, cos))
    sin_out = jnp.where(odd, k * cos, jnp.where(flip, -sin, sin))
    return cos_out, sin_out


def attend(q, blocks, diag):
    scores = [
        lax.dot_general(k, q, (((1,), (1,)), ((), ())), preferred_element_type=F32)
        for k, _ in blocks
    ]
    if diag:
        s = scores[-1]
        key = lax.broadcasted_iota(jnp.int32, s.shape, 0)
        lane = lax.broadcasted_iota(jnp.int32, s.shape, 1)
        row = (lane // 256) * 128 + lane % 128
        scores[-1] = jnp.where(key <= row, s, big_negative)
    m = functools.reduce(jnp.maximum, [jnp.max(s, axis=0, keepdims=True) for s in scores])
    acc, l = 0.0, 0.0
    for s, (_, v) in zip(scores, blocks):
        p = jnp.exp(s - m)
        l = l + jnp.sum(p, axis=0, keepdims=True)
        acc = acc + lax.dot_general(
            v, p.astype(BF), (((0,), (0,)), ((), ())), preferred_element_type=F32
        )
    return acc, m, l


def merge(state, out, lse):
    acc, m, l = state
    top = jnp.maximum(m, lse)
    mine, other = jnp.exp(m - top), jnp.exp(lse - top)
    return acc * mine + out.astype(F32) * other, top, l * mine + other


def kernel(pos_hbm, freq_ref, q_hbm, k_hbm, v_hbm, res_hbm, dir_hbm, w_hbm, out_ref,
           pos, direction, q, k, v, res, wbuf, urow, ldir, rq, rk, kv0, kv1, rq3, rq2,
           o_a, o_b2, o_b1, l_a, l_b2, l_b1, s_a, s_b2, s_c, t_a, t_b2, t_c,
           st_acc, st_ml, att, keep, dots, turn, last, a_send, a_recv, b_send, b_recv,
           c_send, c_recv, al_send, al_recv,
           lsem, ssem, rsem, xs, xr, als, alr):
    s = lax.axis_index("seq")
    t = lax.axis_index("tensor")
    core = t % 2
    x_here = t // 2
    x_other = 1 - x_here
    core_peer = t + 1 - 2 * core
    x_peer = (t + 2) % 4
    half = wbuf.shape[2]
    width = half // 2
    shift = (width // 128) * 128
    window = half - shift

    local = {}

    def fetch(name, src, dst):
        local[name] = pltpu.make_async_copy(src, dst, lsem.at[len(local)])
        local[name].start()

    fetch("pos", pos_hbm, pos)
    fetch("k", k_hbm, k)
    fetch("q", q_hbm, q)
    fetch("v", v_hbm, v)
    for i, x in enumerate((x_other, x_here)):
        cols = pl.ds(pl.multiple_of(x * half, 128), half)
        fetch(i, w_hbm.at[:, cols], wbuf.at[i])
    fetch("dir", dir_hbm, direction)
    fetch("res", res_hbm, res)

    barrier = pltpu.get_barrier_semaphore()
    for j in (1, 2, 3):
        pl.semaphore_signal(barrier, inc=1, device_id={"seq": (s + j) % 4}, device_id_type=MESH)
        pl.semaphore_signal(barrier, inc=1, device_id={"tensor": (t + j) % 4}, device_id_type=MESH)
    pl.semaphore_wait(barrier, 6)

    copies, index = {}, {}

    def add(name, dev, src, dst, lands_as=None):
        i = index[name] = len(index)
        copies[name] = pltpu.make_async_remote_copy(
            src_ref=src, dst_ref=dst, send_sem=ssem.at[i],
            recv_sem=rsem.at[i if lands_as is None else index[lands_as]],
            device_id={"seq": dev}, device_id_type=MESH)

    for g, name in ((0, "a"), (1, "b")):
        cols = slice(256 * g, 256 * g + 256)
        add("v0" + name + "1", 1, v_hbm.at[:, cols], kv0.at[2 * g + 1])
        add("k0" + name + "1", 1, rk.at[g], kv0.at[2 * g])
    add("v0a2", 2, kv0.at[1], kv0.at[1])
    add("k0a2", 2, kv0.at[0], kv0.at[0])
    add("v1a2", 2, v_hbm.at[:, 0:256], kv1.at[1])
    add("k1a2", 2, rk.at[0], kv1.at[0])
    for c in (0, 1):
        rows = slice(256 * c, 256 * c + 256)
        n = str(c)
        add("q3b2" + n, 2, rq.at[1, rows], rq3.at[1, rows])
        add("q3a2" + n, 2, rq.at[0, rows], rq3.at[0, rows])
        add("o3b" + n, 3, s_b2.at[c], o_b2.at[c])
        add("l3b" + n, 3, t_b2.at[c], l_b2.at[c])
        add("f3b1" + n, 1, rq3.at[1, rows], rq3.at[1, rows])
        add("q2b1" + n, 1, rq.at[1, rows], rq2.at[rows])
        add("o3a" + n, 3, s_a.at[c], o_a.at[c])
        add("l3a" + n, 3, t_a.at[c], l_a.at[c])
        add("o2b" + n, 2, s_c.at[0, c], o_b1.at[c])
        add("l2b" + n, 2, t_c.at[0, c], l_b1.at[c])
        add("o3c" + n, 3, s_c.at[1, c], o_b1.at[c], "o2b" + n)
        add("l3c" + n, 3, t_c.at[1, c], l_b1.at[c], "l2b" + n)

    def start(*names):
        for n in names:
            copies[n].start()

    def recv(*names):
        for n in names:
            copies[n].wait_recv()

    def sent(*names):
        for n in names:
            copies[n].wait_send()

    @pl.when(s == 0)
    def _():
        start("v0b1")

    @pl.when(s == 1)
    def _():
        start("v1a2")

    local["pos"].wait()
    freqs = freq_ref[...]
    tokens = pos[...].astype(F32).reshape(1, 256)
    angles = jnp.concatenate(
        [jnp.broadcast_to(tokens[:, 128 * c:128 * c + 128], (128, 128)).T for c in (0, 1)], axis=0
    ) * freqs
    cos, sin = cos_sin(angles)
    def rotate_keys():
        local["k"].wait()
        for g in (1, 0):
            rk[g] = rot(k[:, 256 * g:256 * g + 256], cos, sin).astype(BF)

    @pl.when(s == 0)
    def _():
        rotate_keys()
        start("k0b1", "v0a1", "k0a1")

    @pl.when(s == 1)
    def _():
        rotate_keys()
        start("k1a2")

    local["q"].wait()
    for g in (1, 0):
        for h in (0, 1):
            at = 256 * (2 * g + h)
            r = (rot(q[:, at:at + 256], cos, sin) * HD ** (-0.5)).astype(BF)
            for c in (0, 1):
                rq[g, 256 * c + 128 * h:256 * c + 128 * h + 128, :] = r[128 * c:128 * c + 128]
        if g == 1:
            @pl.when(s == 3)
            def _():
                start("q3b20")

            @pl.when(s == 2)
            def _():
                start("q2b10", "q2b11")

    @pl.when(s >= 2)
    def _():
        rotate_keys()

    local["v"].wait()

    def own(g):
        return rk[g], v[:, 256 * g:256 * g + 256]

    def first(g):
        return kv0[2 * g], kv0[2 * g + 1]

    def second():
        return kv1[0], kv1[1]

    def put(g, state, chunks):
        acc, _, l = state
        out = acc / l
        for i, c in enumerate(chunks):
            for h in (0, 1):
                at = 256 * i + 128 * h
                col = 256 * (2 * g + h)
                att[128 * c:128 * c + 128, col:col + 256] = out[:, at:at + 128].T.astype(BF)

    def send_state(state, out_to, lse_to, *names):
        acc, m, l = state
        out_to[...] = (acc / l).astype(BF)
        lse_to[...] = jnp.broadcast_to(m + jnp.log(l), lse_to.shape)
        start(*names)

    def hold(g, state):
        acc, m, l = state
        st_acc[g] = acc
        st_ml[g, 0:8] = jnp.broadcast_to(m, (8, 512))
        st_ml[g, 8:16] = jnp.broadcast_to(l, (8, 512))

    def held(g, c):
        lanes = slice(256 * c, 256 * c + 256)
        return st_acc[g, :, lanes], st_ml[g, 0:1, lanes], st_ml[g, 8:9, lanes]

    def prepare_direction():
        local["dir"].wait()
        whole = direction[...].reshape(1, 2 * half)
        scale = 1.0 / jnp.sqrt(jnp.sum(whole * whole, axis=1, keepdims=True) + 1e-06)
        lane = lax.broadcasted_iota(jnp.int32, (1, window), 1)
        shared = jnp.where(core == 0, 0, shift)
        keep_lane = (lane < shared) | (lane >= shared + (window - shift))
        for i, x in enumerate((x_other, x_here)):
            mine = jnp.where(x == 0, whole[:, :half], whole[:, half:]) * scale
            low, high = mine[:, :window], mine[:, shift:]
            urow[2 * i:2 * i + 1] = jnp.where(keep_lane, jnp.where(core == 0, high, low), 0.0)
            urow[2 * i + 1:2 * i + 2] = jnp.where(core == 0, low, high)
        for at in range(0, window, 128):
            ldir[at:at + 128, :] = jnp.broadcast_to(urow[3:4, at:at + 128], (128, 128)).T

    @pl.when(s == 0)
    def _():
        put(1, attend(rq[1], [own(1)], True), (0, 1))
        put(0, attend(rq[0], [own(0)], True), (0, 1))

    @pl.when(s == 2)
    def _():
        recv("q3b20")
        start("f3b10")
        state = attend(rq3[1, 0:256, :], [own(1)], False)
        send_state(state, s_b2.at[0], t_b2.at[0], "o3b0", "l3b0")
        hold(1, attend(rq[1], [own(1)], True))

    @pl.when(s == 3)
    def _():
        start("q3a20", "q3b21", "q3a21")
        hold(0, attend(rq[0], [own(0)], True))
        hold(1, attend(rq[1], [own(1)], True))

    prepare_direction()

    @pl.when(s == 1)
    def _():
        recv("v0b1", "k0b1")
        for c in (0, 1):
            n = str(c)
            rows = slice(256 * c, 256 * c + 256)
            recv("f3b1" + n)
            state = attend(rq3[1, rows, :], [first(1), own(1)], False)
            send_state(state, s_c.at[1, c], t_c.at[1, c], "o3c" + n, "l3c" + n)
            recv("q2b1" + n)
            state = attend(rq2[rows, :], [first(1), own(1)], False)
            send_state(state, s_c.at[0, c], t_c.at[0, c], "o2b" + n, "l2b" + n)
            if c == 0:
                recv("v0a1", "k0a1")
                start("v0a2", "k0a2")
        put(1, attend(rq[1], [first(1), own(1)], True), (0, 1))
        put(0, attend(rq[0], [first(0), own(0)], True), (0, 1))

    @pl.when(s == 2)
    def _():
        recv("q3b21")
        start("f3b11")
        state = attend(rq3[1, 256:512, :], [own(1)], False)
        send_state(state, s_b2.at[1], t_b2.at[1], "o3b1", "l3b1")
        recv("v1a2", "k1a2", "v0a2", "k0a2")
        for c in (0, 1):
            n = str(c)
            recv("q3a2" + n)
            rows = slice(256 * c, 256 * c + 256)
            state = attend(rq3[0, rows, :], [first(0), second(), own(0)], False)
            send_state(state, s_a.at[c], t_a.at[c], "o3a" + n, "l3a" + n)
        put(0, attend(rq[0], [first(0), second(), own(0)], True), (0, 1))

    def x_copies(src, dst, first, dev):
        part = src.shape[0] // 4
        return [
            pltpu.make_async_remote_copy(
                src_ref=src.at[part * j:part * j + part], dst_ref=dst.at[part * j:part * j + part],
                send_sem=xs.at[first + j], recv_sem=xr.at[first + j],
                device_id={"tensor": dev}, device_id_type=MESH)
            for j in range(4)
        ]

    def begin(parts):
        for part in parts:
            part.start()

    def arrive(parts):
        for part in parts:
            part.wait_recv()

    def leave(parts):
        for part in parts:
            part.wait_send()

    local["res"].wait()
    own_window = pl.ds(pl.multiple_of(core * shift, 128), window)
    peer_window = pl.ds(pl.multiple_of((1 - core) * shift, 128), window)
    own_rows = pl.ds(pl.multiple_of(core * (width - shift), 64), width)
    local_dir = ldir[own_rows, :]
    local[0].wait()
    local[1].wait()
    a_copies, b_copies, al_copies = {}, {}, {}
    for c in (0, 1):
        @pl.when(s == 3)
        def _(c=c):
            n = str(c)
            recv("o3b" + n, "l3b" + n, "o3a" + n, "l3a" + n)
            put(0, merge(held(0, c), o_a[c], l_a[c, 0:1]), (c,))
            state = merge(held(1, c), o_b2[c], l_b2[c, 0:1])
            recv("o2b" + n, "l2b" + n)
            put(1, merge(state, o_b1[c], l_b1[c, 0:1]), (c,))

        @pl.when(s == 2)
        def _(c=c):
            recv("o2b" + str(c), "l2b" + str(c))
            put(1, merge(held(1, c), o_b1[c], l_b1[c, 0:1]), (c,))

        rows = slice(128 * c, 128 * c + 128)
        part = jnp.dot(att[rows, :], wbuf[0, :, peer_window], preferred_element_type=F32)
        a_send[c] = part.astype(BF)
        a_copies[c] = x_copies(a_send.at[c], a_recv.at[c], 4 * c, core_peer)
        begin(a_copies[c])
        part = jnp.dot(att[rows, :], wbuf[0, :, own_window], preferred_element_type=F32)
        keep[rows, :] = part
        arrive(a_copies[c])
        turn[...] = (keep[rows, :] + a_recv[c].astype(F32)).T
        b_send[c] = turn[own_rows, :].astype(BF)
        b_copies[c] = x_copies(b_send.at[c], b_recv.at[c], 8 + 4 * c, x_peer)
        begin(b_copies[c])
        dots[rows, :] = a_send[c].astype(F32) * urow[0:1] + keep[rows, :] * urow[1:2]

    part = jnp.dot(att[...], wbuf[1, :, peer_window], preferred_element_type=F32)
    c_send[...] = part.astype(BF)
    c_copy = x_copies(c_send, c_recv, 16, core_peer)
    begin(c_copy)
    part = jnp.dot(att[...], wbuf[1, :, own_window], preferred_element_type=F32)
    keep[...] = part
    total = jnp.sum(
        dots[...] + c_send[...].astype(F32) * urow[2:3] + part * urow[3:4], axis=1, keepdims=True
    )
    for c in (0, 1):
        lanes = slice(128 * c, 128 * c + 128)
        line = jnp.broadcast_to(total[lanes], (128, 128)).T[0:1]
        line = line + jnp.sum(res[:, lanes].astype(F32) * local_dir, axis=0, keepdims=True)
        al_send[:, lanes] = jnp.broadcast_to(line, (8, 128))
    for j in (1, 2, 3):
        al_copies[j] = pltpu.make_async_remote_copy(
            src_ref=al_send, dst_ref=al_recv.at[j - 1],
            send_sem=als.at[j - 1], recv_sem=alr.at[j - 1],
            device_id={"tensor": (t + j) % 4}, device_id_type=MESH)
        al_copies[j].start()
    arrive(c_copy)
    for c in (0, 1):
        lanes = slice(128 * c, 128 * c + 128)
        turn[...] = (keep[lanes, :] + c_recv[lanes, :].astype(F32)).T
        last[:, lanes] = res[:, lanes].astype(F32) + turn[own_rows, :]
    along = al_send[0:1]
    for j in (1, 2, 3):
        al_copies[j].wait_recv()
        along = along + al_recv[j - 1, 0:1]
    for c in (0, 1):
        lanes = slice(128 * c, 128 * c + 128)
        last[:, lanes] = last[:, lanes] - along[:, lanes] * local_dir
        arrive(b_copies[c])
        out_ref[:, lanes] = (last[:, lanes] + b_recv[c].astype(F32)).astype(BF)

    leave(c_copy)
    for j in (1, 2, 3):
        al_copies[j].wait_send()
    for c in (0, 1):
        leave(a_copies[c])
        leave(b_copies[c])

    @pl.when(s == 0)
    def _():
        sent("v0b1", "k0b1", "v0a1", "k0a1")

    @pl.when(s == 1)
    def _():
        sent("v1a2", "k1a2", "v0a2", "k0a2", "o2b0", "l2b0", "o2b1", "l2b1", "o3c0", "l3c0", "o3c1", "l3c1")

    @pl.when(s == 2)
    def _():
        sent("q2b10", "q2b11", "f3b10", "f3b11", "o3b0", "l3b0", "o3b1", "l3b1", "o3a0", "l3a0", "o3a1", "l3a1")

    @pl.when(s == 3)
    def _():
        sent("q3b20", "q3a20", "q3b21", "q3a21")


def fused_body(queries, key_rows, value_rows, positions, residual, direction, out_weight):
    freqs = jnp.power(10000.0, -jnp.arange(HD // 2, dtype=F32) * 2.0 / HD)[None, :]
    rows, width = residual.shape
    depth = out_weight.shape[0]
    window = 2 * width - (width // 128) * 128
    vmem = pl.BlockSpec(memory_space=pltpu.VMEM)
    anywhere = pl.BlockSpec(memory_space=pl.ANY)
    dma = pltpu.SemaphoreType.DMA
    out = pl.pallas_call(
        kernel,
        out_shape=jax.ShapeDtypeStruct((width, rows), BF),
        in_specs=[anywhere, vmem] + [anywhere] * 6,
        out_specs=vmem,
        scratch_shapes=[
            pltpu.VMEM(positions.shape, jnp.int32),
            pltpu.VMEM(direction.shape, F32),
            pltpu.VMEM(queries.shape, BF),
            pltpu.VMEM(key_rows.shape, BF),
            pltpu.VMEM(value_rows.shape, BF),
            pltpu.VMEM((width, rows), BF),
            pltpu.VMEM((2, depth, 2 * width), BF),
            pltpu.VMEM((8, window), F32),
            pltpu.VMEM((window, 128), F32),
            pltpu.VMEM((2, 512, 256), BF),
            pltpu.VMEM((2, 256, 256), BF),
            pltpu.VMEM((4, 256, 256), BF),
            pltpu.VMEM((2, 256, 256), BF),
            pltpu.VMEM((2, 512, 256), BF),
            pltpu.VMEM((512, 256), BF),
            pltpu.VMEM((2, 256, 256), BF),
            pltpu.VMEM((2, 256, 256), BF),
            pltpu.VMEM((2, 256, 256), BF),
            pltpu.VMEM((2, 8, 256), F32),
            pltpu.VMEM((2, 8, 256), F32),
            pltpu.VMEM((2, 8, 256), F32),
            pltpu.VMEM((2, 256, 256), BF),
            pltpu.VMEM((2, 256, 256), BF),
            pltpu.VMEM((2, 2, 256, 256), BF),
            pltpu.VMEM((2, 8, 256), F32),
            pltpu.VMEM((2, 8, 256), F32),
            pltpu.VMEM((2, 2, 8, 256), F32),
            pltpu.VMEM((2, 256, 512), F32),
            pltpu.VMEM((2, 16, 512), F32),
            pltpu.VMEM((256, depth), BF),
            pltpu.VMEM((256, window), F32),
            pltpu.VMEM((256, window), F32),
            pltpu.VMEM((window, 128), F32),
            pltpu.VMEM((width, 256), F32),
            pltpu.VMEM((2, 128, window), BF),
            pltpu.VMEM((2, 128, window), BF),
            pltpu.VMEM((2, width, 128), BF),
            pltpu.VMEM((2, width, 128), BF),
            pltpu.VMEM((256, window), BF),
            pltpu.VMEM((256, window), BF),
            pltpu.VMEM((8, 256), F32),
            pltpu.VMEM((3, 8, 256), F32),
            dma((8,)),
            dma((32,)),
            dma((32,)),
            dma((20,)),
            dma((20,)),
            dma((3,)),
            dma((3,)),
        ],
        compiler_params=pltpu.CompilerParams(
            collective_id=0, has_side_effects=True, vmem_limit_bytes=60 * 1024 * 1024
        ),
    )(positions, freqs, queries, key_rows, value_rows, residual.T, direction, out_weight)
    return out.T


def device_body(*args):
    queries, key_rows, _, _, residual, direction, _ = args
    fits = (
        lax.axis_size("seq") == 4
        and lax.axis_size("tensor") == 4
        and queries.shape == (256, 1024)
        and key_rows.shape == (256, 512)
        and residual.shape[1] * 4 == direction.shape[0]
        and residual.shape[1] % 128 == 64
        and WINDOW == 1024
    )
    return fused_body(*args) if fits else body(*args)


def solution(mesh):
    return jax.shard_map(
        device_body,
        mesh=mesh,
        in_specs=(
            P(("groups", "seq"), "tensor"),
            P(("groups", "seq"), "tensor"),
            P(("groups", "seq"), "tensor"),
            P(("groups", "seq")),
            P(("groups", "seq"), "tensor"),
            P("groups"),
            P("tensor", None),
        ),
        out_specs=P(("groups", "seq"), "tensor"),
        check_vma=False,
    )
```

```python
import functools

import jax
import jax.numpy as jnp
from jax import lax
from jax.experimental import pallas as pl
from jax.experimental.pallas import tpu as pltpu
from jax.sharding import PartitionSpec as P

HD = 256
WINDOW = 1024


big_negative = -1e30


def shifted_2(value, axis, steps):
    count = lax.axis_size(axis)
    first, last = (max(0, -steps), min(count, count - steps))
    return lax.ppermute(value, axis, [(source, source + steps) for source in range(first, last)])


def rotary_tables(positions, head_dim):
    half_dim = head_dim // 2
    freqs = jnp.power(10000.0, -jnp.arange(half_dim, dtype=jnp.float32) * 2.0 / head_dim)
    angles = positions.astype(jnp.float32)[:, None] * freqs[None, :]
    return (jnp.cos(angles)[:, None, :], jnp.sin(angles)[:, None, :])


def rotate_heads(block, cos_table, sin_table, head_dim):
    row_count = block.shape[0]
    head_count = block.shape[1] // head_dim
    half_dim = head_dim // 2
    widened = block.reshape(row_count, head_count, head_dim).astype(jnp.float32)
    first_half = widened[:, :, :half_dim]
    second_half = widened[:, :, half_dim:]
    turned = jnp.concatenate(
        [
            first_half * cos_table - second_half * sin_table,
            second_half * cos_table + first_half * sin_table,
        ],
        axis=-1,
    )
    return turned.reshape(row_count, head_count * head_dim)


def body(queries, key_rows, value_rows, positions, residual, direction, out_weight):
    tokens_here = queries.shape[0]
    query_heads = queries.shape[1] // HD
    kv_heads = key_rows.shape[1] // HD
    group_size = query_heads // kv_heads
    span_blocks = WINDOW // tokens_here
    seq_index = lax.axis_index("seq")
    cos_table, sin_table = rotary_tables(positions, HD)
    rot_queries = (rotate_heads(queries, cos_table, sin_table, HD) * HD ** (-0.5)).astype(
        jnp.bfloat16
    )
    rot_keys = rotate_heads(key_rows, cos_table, sin_table, HD).astype(jnp.bfloat16)
    query_blocks = rot_queries.reshape(tokens_here, kv_heads, group_size, HD)
    own_scores = jnp.einsum(
        "qkgd,skd->kgqs",
        query_blocks,
        rot_keys.reshape(tokens_here, kv_heads, HD),
        preferred_element_type=jnp.float32,
    )
    earlier_keys = []
    earlier_values = []
    for distance in range(span_blocks, 0, -1):
        moved_keys, moved_values = shifted_2((rot_keys, value_rows), "seq", distance)
        earlier_keys.append(moved_keys)
        earlier_values.append(moved_values)
    far_keys = jnp.concatenate(earlier_keys, axis=0)
    far_values = jnp.concatenate(earlier_values, axis=0)
    far_scores = jnp.einsum(
        "qkgd,skd->kgqs",
        query_blocks,
        far_keys.reshape(-1, kv_heads, HD),
        preferred_element_type=jnp.float32,
    )
    scores = jnp.concatenate([far_scores, own_scores], axis=-1)
    query_index = seq_index * tokens_here + jnp.arange(tokens_here, dtype=jnp.int32)
    key_index = (seq_index - span_blocks) * tokens_here + jnp.arange(
        (span_blocks + 1) * tokens_here, dtype=jnp.int32
    )
    gap_grid = query_index[:, None] - key_index[None, :]
    allowed = (gap_grid >= 0) & (gap_grid < WINDOW) & (key_index[None, :] >= 0)
    scores = jnp.where(allowed, scores, big_negative)
    row_max = jnp.max(scores, axis=-1, keepdims=True)
    shifted = jnp.exp(scores - row_max)
    row_sum = jnp.sum(shifted, axis=-1, keepdims=True)
    weights = (shifted / row_sum).astype(jnp.bfloat16)
    every_value = jnp.concatenate([far_values, value_rows], axis=0).reshape(-1, kv_heads, HD)
    mixed = jnp.einsum("kgqs,skd->qkgd", weights, every_value, preferred_element_type=jnp.float32)
    attended = mixed.astype(jnp.bfloat16).reshape(tokens_here, query_heads * HD)
    partial_value = jnp.dot(attended, out_weight, preferred_element_type=jnp.float32)
    unit_dir = direction / jnp.sqrt(jnp.sum(direction * direction) + 1e-06)
    column_width = residual.shape[1]
    tensor_index = lax.axis_index("tensor")
    local_dir = lax.dynamic_slice_in_dim(unit_dir, tensor_index * column_width, column_width, 0)
    base_state = residual.astype(jnp.float32)
    rounded_terms = partial_value.astype(jnp.bfloat16).astype(jnp.float32)
    dot_terms = jnp.sum(rounded_terms * unit_dir[None, :], axis=1) + jnp.sum(
        base_state * local_dir[None, :], axis=1
    )
    along = lax.psum(dot_terms, "tensor")
    summed = lax.psum_scatter(
        partial_value.astype(jnp.bfloat16), "tensor", scatter_dimension=1, tiled=True
    ).astype(jnp.float32)
    hidden_state = base_state + summed
    ablated = (hidden_state - along[:, None] * local_dir[None, :]).astype(jnp.bfloat16)
    return ablated


BF = jnp.bfloat16
F32 = jnp.float32
MESH = pl.DeviceIdType.MESH

def rot(x, cos, sin):
    x = x.astype(F32)
    a, b = x[:, :128], x[:, 128:]
    return jnp.concatenate([a * cos - b * sin, b * cos + a * sin], axis=1)


def cos_sin(x):
    n = jnp.floor(x * 0.15915494309189535 + 0.5)
    r = ((x - n * 6.28125) - n * (507.0 / 262144.0)) - n * 1.2556659146019e-06
    k = jnp.floor(r * 0.6366197723675814 + 0.5)
    y = (r - k * 1.5707963705062866) + k * 4.371139000186241e-08
    z = y * y
    sin = y + y * z * (-1.0 / 6 + z * (1.0 / 120 + z * (-1.0 / 5040 + z * (1.0 / 362880))))
    cos = 1.0 + z * (-0.5 + z * (1.0 / 24 + z * (-1.0 / 720 + z * (1.0 / 40320))))
    odd = jnp.abs(k) == 1.0
    flip = jnp.abs(k) == 2.0
    cos_out = jnp.where(odd, -k * sin, jnp.where(flip, -cos, cos))
    sin_out = jnp.where(odd, k * cos, jnp.where(flip, -sin, sin))
    return cos_out, sin_out


def attend(q, blocks, diag):
    scores = [
        lax.dot_general(k, q, (((1,), (1,)), ((), ())), preferred_element_type=F32)
        for k, _ in blocks
    ]
    if diag:
        s = scores[-1]
        key = lax.broadcasted_iota(jnp.int32, s.shape, 0)
        lane = lax.broadcasted_iota(jnp.int32, s.shape, 1)
        row = (lane // 256) * 128 + lane % 128
        scores[-1] = jnp.where(key <= row, s, big_negative)
    m = functools.reduce(jnp.maximum, [jnp.max(s, axis=0, keepdims=True) for s in scores])
    acc, l = 0.0, 0.0
    for s, (_, v) in zip(scores, blocks):
        p = jnp.exp(s - m)
        l = l + jnp.sum(p, axis=0, keepdims=True)
        acc = acc + lax.dot_general(
            v, p.astype(BF), (((0,), (0,)), ((), ())), preferred_element_type=F32
        )
    return acc, m, l


def merge(state, out, lse):
    acc, m, l = state
    top = jnp.maximum(m, lse)
    mine, other = jnp.exp(m - top), jnp.exp(lse - top)
    return acc * mine + out.astype(F32) * other, top, l * mine + other


def kernel(pos_hbm, freq_ref, q_hbm, k_hbm, v_hbm, res_hbm, dir_hbm, w_hbm, out_ref,
           pos, direction, q, k, v, res, wbuf, urow, ldir, rq, rk, kv0, kv1, rq3, rq2,
           o_a, o_b2, o_b1, l_a, l_b2, l_b1, s_a, s_b2, s_c, t_a, t_b2, t_c,
           st_acc, st_ml, att, keep, dots, turn, last, a_send, a_recv, b_send, b_recv,
           c_send, c_recv, al_send, al_recv,
           lsem, ssem, rsem, xs, xr, als, alr):
    s = lax.axis_index("seq")
    t = lax.axis_index("tensor")
    core = t % 2
    x_here = t // 2
    x_other = 1 - x_here
    core_peer = t + 1 - 2 * core
    x_peer = (t + 2) % 4
    half = wbuf.shape[2]
    width = half // 2
    shift = (width // 128) * 128
    window = half - shift

    local = {}

    def fetch(name, src, dst):
        local[name] = pltpu.make_async_copy(src, dst, lsem.at[len(local)])
        local[name].start()

    fetch("pos", pos_hbm, pos)
    fetch("k", k_hbm, k)
    fetch("q", q_hbm, q)
    fetch("v", v_hbm, v)
    for i, x in enumerate((x_other, x_here)):
        cols = pl.ds(pl.multiple_of(x * half, 128), half)
        fetch(i, w_hbm.at[:, cols], wbuf.at[i])
    fetch("dir", dir_hbm, direction)
    fetch("res", res_hbm, res)

    barrier = pltpu.get_barrier_semaphore()
    for j in (1, 2, 3):
        pl.semaphore_signal(barrier, inc=1, device_id={"seq": (s + j) % 4}, device_id_type=MESH)
        pl.semaphore_signal(barrier, inc=1, device_id={"tensor": (t + j) % 4}, device_id_type=MESH)
    pl.semaphore_wait(barrier, 6)

    copies, index = {}, {}

    def add(name, dev, src, dst, lands_as=None):
        i = index[name] = len(index)
        copies[name] = pltpu.make_async_remote_copy(
            src_ref=src, dst_ref=dst, send_sem=ssem.at[i],
            recv_sem=rsem.at[i if lands_as is None else index[lands_as]],
            device_id={"seq": dev}, device_id_type=MESH)

    for g, name in ((0, "a"), (1, "b")):
        cols = slice(256 * g, 256 * g + 256)
        add("v0" + name + "1", 1, v_hbm.at[:, cols], kv0.at[2 * g + 1])
        add("k0" + name + "1", 1, rk.at[g], kv0.at[2 * g])
    add("v0a2", 2, v_hbm.at[:, 0:256], kv0.at[1])
    add("k0a2", 2, rk.at[0], kv0.at[0])
    add("v1a2", 2, v_hbm.at[:, 0:256], kv1.at[1])
    add("k1a2", 2, rk.at[0], kv1.at[0])
    for c in (0, 1):
        rows = slice(256 * c, 256 * c + 256)
        n = str(c)
        add("q3b2" + n, 2, rq.at[1, rows], rq3.at[1, rows])
        add("q3a2" + n, 2, rq.at[0, rows], rq3.at[0, rows])
        add("o3b" + n, 3, s_b2.at[c], o_b2.at[c])
        add("l3b" + n, 3, t_b2.at[c], l_b2.at[c])
        add("f3b1" + n, 1, rq3.at[1, rows], rq3.at[1, rows])
        add("q2b1" + n, 1, rq.at[1, rows], rq2.at[rows])
        add("o3a" + n, 3, s_a.at[c], o_a.at[c])
        add("l3a" + n, 3, t_a.at[c], l_a.at[c])
        add("o2b" + n, 2, s_c.at[0, c], o_b1.at[c])
        add("l2b" + n, 2, t_c.at[0, c], l_b1.at[c])
        add("o3c" + n, 3, s_c.at[1, c], o_b1.at[c], "o2b" + n)
        add("l3c" + n, 3, t_c.at[1, c], l_b1.at[c], "l2b" + n)

    def start(*names):
        for n in names:
            copies[n].start()

    def recv(*names):
        for n in names:
            copies[n].wait_recv()

    def sent(*names):
        for n in names:
            copies[n].wait_send()

    @pl.when(s == 0)
    def _():
        start("v0b1", "v0a2")

    @pl.when(s == 1)
    def _():
        start("v1a2")

    local["pos"].wait()
    freqs = freq_ref[...]
    tokens = pos[...].astype(F32).reshape(1, 256)
    angles = jnp.concatenate(
        [jnp.broadcast_to(tokens[:, 128 * c:128 * c + 128], (128, 128)).T for c in (0, 1)], axis=0
    ) * freqs
    cos, sin = cos_sin(angles)
    def rotate_keys():
        local["k"].wait()
        for g in (1, 0):
            rk[g] = rot(k[:, 256 * g:256 * g + 256], cos, sin).astype(BF)

    @pl.when(s == 0)
    def _():
        rotate_keys()
        start("k0b1", "k0a2")

    @pl.when(s == 1)
    def _():
        rotate_keys()
        start("k1a2")

    local["q"].wait()
    for g in (1, 0):
        for h in (0, 1):
            at = 256 * (2 * g + h)
            r = (rot(q[:, at:at + 256], cos, sin) * HD ** (-0.5)).astype(BF)
            for c in (0, 1):
                rq[g, 256 * c + 128 * h:256 * c + 128 * h + 128, :] = r[128 * c:128 * c + 128]
        if g == 1:
            @pl.when(s == 3)
            def _():
                start("q3b20")

            @pl.when(s == 2)
            def _():
                start("q2b10", "q2b11")

    @pl.when(s >= 2)
    def _():
        rotate_keys()

    local["v"].wait()

    def own(g):
        return rk[g], v[:, 256 * g:256 * g + 256]

    def first(g):
        return kv0[2 * g], kv0[2 * g + 1]

    def second():
        return kv1[0], kv1[1]

    def put(g, state, chunks):
        acc, _, l = state
        out = acc / l
        for i, c in enumerate(chunks):
            for h in (0, 1):
                at = 256 * i + 128 * h
                col = 256 * (2 * g + h)
                att[128 * c:128 * c + 128, col:col + 256] = out[:, at:at + 128].T.astype(BF)

    def send_state(state, out_to, lse_to, *names):
        acc, m, l = state
        out_to[...] = (acc / l).astype(BF)
        lse_to[...] = jnp.broadcast_to(m + jnp.log(l), lse_to.shape)
        start(*names)

    def hold(g, state):
        acc, m, l = state
        st_acc[g] = acc
        st_ml[g, 0:8] = jnp.broadcast_to(m, (8, 512))
        st_ml[g, 8:16] = jnp.broadcast_to(l, (8, 512))

    def held(g, c):
        lanes = slice(256 * c, 256 * c + 256)
        return st_acc[g, :, lanes], st_ml[g, 0:1, lanes], st_ml[g, 8:9, lanes]

    def prepare_direction():
        local["dir"].wait()
        whole = direction[...].reshape(1, 2 * half)
        scale = 1.0 / jnp.sqrt(jnp.sum(whole * whole, axis=1, keepdims=True) + 1e-06)
        lane = lax.broadcasted_iota(jnp.int32, (1, window), 1)
        shared = jnp.where(core == 0, 0, shift)
        keep_lane = (lane < shared) | (lane >= shared + (window - shift))
        for i, x in enumerate((x_other, x_here)):
            mine = jnp.where(x == 0, whole[:, :half], whole[:, half:]) * scale
            low, high = mine[:, :window], mine[:, shift:]
            urow[2 * i:2 * i + 1] = jnp.where(keep_lane, jnp.where(core == 0, high, low), 0.0)
            urow[2 * i + 1:2 * i + 2] = jnp.where(core == 0, low, high)
        for at in range(0, window, 128):
            ldir[at:at + 128, :] = jnp.broadcast_to(urow[3:4, at:at + 128], (128, 128)).T

    @pl.when(s == 0)
    def _():
        put(1, attend(rq[1], [own(1)], True), (0, 1))
        start("v0a1", "k0a1")
        put(0, attend(rq[0], [own(0)], True), (0, 1))

    @pl.when(s == 2)
    def _():
        recv("q3b20")
        start("f3b10")
        state = attend(rq3[1, 0:256, :], [own(1)], False)
        send_state(state, s_b2.at[0], t_b2.at[0], "o3b0", "l3b0")
        hold(1, attend(rq[1], [own(1)], True))

    @pl.when(s == 3)
    def _():
        start("q3a20", "q3b21", "q3a21")
        hold(0, attend(rq[0], [own(0)], True))
        hold(1, attend(rq[1], [own(1)], True))

    prepare_direction()

    @pl.when(s == 1)
    def _():
        recv("v0b1", "k0b1")
        for c in (0, 1):
            n = str(c)
            rows = slice(256 * c, 256 * c + 256)
            recv("f3b1" + n)
            state = attend(rq3[1, rows, :], [first(1), own(1)], False)
            send_state(state, s_c.at[1, c], t_c.at[1, c], "o3c" + n, "l3c" + n)
            recv("q2b1" + n)
            state = attend(rq2[rows, :], [first(1), own(1)], False)
            send_state(state, s_c.at[0, c], t_c.at[0, c], "o2b" + n, "l2b" + n)
        put(1, attend(rq[1], [first(1), own(1)], True), (0, 1))
        recv("v0a1", "k0a1")
        put(0, attend(rq[0], [first(0), own(0)], True), (0, 1))

    @pl.when(s == 2)
    def _():
        recv("q3b21")
        start("f3b11")
        state = attend(rq3[1, 256:512, :], [own(1)], False)
        send_state(state, s_b2.at[1], t_b2.at[1], "o3b1", "l3b1")
        recv("v1a2", "k1a2", "v0a2", "k0a2")
        for c in (0, 1):
            n = str(c)
            recv("q3a2" + n)
            rows = slice(256 * c, 256 * c + 256)
            state = attend(rq3[0, rows, :], [first(0), second(), own(0)], False)
            send_state(state, s_a.at[c], t_a.at[c], "o3a" + n, "l3a" + n)
        put(0, attend(rq[0], [first(0), second(), own(0)], True), (0, 1))

    def x_copies(src, dst, first, dev):
        part = src.shape[0] // 4
        return [
            pltpu.make_async_remote_copy(
                src_ref=src.at[part * j:part * j + part], dst_ref=dst.at[part * j:part * j + part],
                send_sem=xs.at[first + j], recv_sem=xr.at[first + j],
                device_id={"tensor": dev}, device_id_type=MESH)
            for j in range(4)
        ]

    def begin(parts):
        for part in parts:
            part.start()

    def arrive(parts):
        for part in parts:
            part.wait_recv()

    def leave(parts):
        for part in parts:
            part.wait_send()

    local["res"].wait()
    own_window = pl.ds(pl.multiple_of(core * shift, 128), window)
    peer_window = pl.ds(pl.multiple_of((1 - core) * shift, 128), window)
    own_rows = pl.ds(pl.multiple_of(core * (width - shift), 64), width)
    local_dir = ldir[own_rows, :]
    local[0].wait()
    local[1].wait()
    a_copies, b_copies, al_copies = {}, {}, {}
    for c in (0, 1):
        @pl.when(s == 3)
        def _(c=c):
            n = str(c)
            recv("o3b" + n, "l3b" + n, "o3a" + n, "l3a" + n)
            put(0, merge(held(0, c), o_a[c], l_a[c, 0:1]), (c,))
            state = merge(held(1, c), o_b2[c], l_b2[c, 0:1])
            recv("o2b" + n, "l2b" + n)
            put(1, merge(state, o_b1[c], l_b1[c, 0:1]), (c,))

        @pl.when(s == 2)
        def _(c=c):
            recv("o2b" + str(c), "l2b" + str(c))
            put(1, merge(held(1, c), o_b1[c], l_b1[c, 0:1]), (c,))

        rows = slice(128 * c, 128 * c + 128)
        part = jnp.dot(att[rows, :], wbuf[0, :, peer_window], preferred_element_type=F32)
        a_send[c] = part.astype(BF)
        a_copies[c] = x_copies(a_send.at[c], a_recv.at[c], 4 * c, core_peer)
        begin(a_copies[c])
        part = jnp.dot(att[rows, :], wbuf[0, :, own_window], preferred_element_type=F32)
        keep[rows, :] = part
        arrive(a_copies[c])
        turn[...] = (keep[rows, :] + a_recv[c].astype(F32)).T
        b_send[c] = turn[own_rows, :].astype(BF)
        b_copies[c] = x_copies(b_send.at[c], b_recv.at[c], 8 + 4 * c, x_peer)
        begin(b_copies[c])
        dots[rows, :] = a_send[c].astype(F32) * urow[0:1] + keep[rows, :] * urow[1:2]

    part = jnp.dot(att[...], wbuf[1, :, peer_window], preferred_element_type=F32)
    c_send[...] = part.astype(BF)
    c_copy = x_copies(c_send, c_recv, 16, core_peer)
    begin(c_copy)
    part = jnp.dot(att[...], wbuf[1, :, own_window], preferred_element_type=F32)
    keep[...] = part
    total = jnp.sum(
        dots[...] + c_send[...].astype(F32) * urow[2:3] + part * urow[3:4], axis=1, keepdims=True
    )
    for c in (0, 1):
        lanes = slice(128 * c, 128 * c + 128)
        line = jnp.broadcast_to(total[lanes], (128, 128)).T[0:1]
        line = line + jnp.sum(res[:, lanes].astype(F32) * local_dir, axis=0, keepdims=True)
        al_send[:, lanes] = jnp.broadcast_to(line, (8, 128))
    for j in (1, 2, 3):
        al_copies[j] = pltpu.make_async_remote_copy(
            src_ref=al_send, dst_ref=al_recv.at[j - 1],
            send_sem=als.at[j - 1], recv_sem=alr.at[j - 1],
            device_id={"tensor": (t + j) % 4}, device_id_type=MESH)
        al_copies[j].start()
    arrive(c_copy)
    for c in (0, 1):
        lanes = slice(128 * c, 128 * c + 128)
        turn[...] = (keep[lanes, :] + c_recv[lanes, :].astype(F32)).T
        last[:, lanes] = res[:, lanes].astype(F32) + turn[own_rows, :]
    along = al_send[0:1]
    for j in (1, 2, 3):
        al_copies[j].wait_recv()
        along = along + al_recv[j - 1, 0:1]
    for c in (0, 1):
        lanes = slice(128 * c, 128 * c + 128)
        last[:, lanes] = last[:, lanes] - along[:, lanes] * local_dir
        arrive(b_copies[c])
        out_ref[:, lanes] = (last[:, lanes] + b_recv[c].astype(F32)).astype(BF)

    leave(c_copy)
    for j in (1, 2, 3):
        al_copies[j].wait_send()
    for c in (0, 1):
        leave(a_copies[c])
        leave(b_copies[c])

    @pl.when(s == 0)
    def _():
        sent("v0b1", "k0b1", "v0a2", "k0a2", "v0a1", "k0a1")

    @pl.when(s == 1)
    def _():
        sent("v1a2", "k1a2", "o2b0", "l2b0", "o2b1", "l2b1", "o3c0", "l3c0", "o3c1", "l3c1")

    @pl.when(s == 2)
    def _():
        sent("q2b10", "q2b11", "f3b10", "f3b11", "o3b0", "l3b0", "o3b1", "l3b1", "o3a0", "l3a0", "o3a1", "l3a1")

    @pl.when(s == 3)
    def _():
        sent("q3b20", "q3a20", "q3b21", "q3a21")


def fused_body(queries, key_rows, value_rows, positions, residual, direction, out_weight):
    freqs = jnp.power(10000.0, -jnp.arange(HD // 2, dtype=F32) * 2.0 / HD)[None, :]
    rows, width = residual.shape
    depth = out_weight.shape[0]
    window = 2 * width - (width // 128) * 128
    vmem = pl.BlockSpec(memory_space=pltpu.VMEM)
    anywhere = pl.BlockSpec(memory_space=pl.ANY)
    dma = pltpu.SemaphoreType.DMA
    out = pl.pallas_call(
        kernel,
        out_shape=jax.ShapeDtypeStruct((width, rows), BF),
        in_specs=[anywhere, vmem] + [anywhere] * 6,
        out_specs=vmem,
        scratch_shapes=[
            pltpu.VMEM(positions.shape, jnp.int32),
            pltpu.VMEM(direction.shape, F32),
            pltpu.VMEM(queries.shape, BF),
            pltpu.VMEM(key_rows.shape, BF),
            pltpu.VMEM(value_rows.shape, BF),
            pltpu.VMEM((width, rows), BF),
            pltpu.VMEM((2, depth, 2 * width), BF),
            pltpu.VMEM((8, window), F32),
            pltpu.VMEM((window, 128), F32),
            pltpu.VMEM((2, 512, 256), BF),
            pltpu.VMEM((2, 256, 256), BF),
            pltpu.VMEM((4, 256, 256), BF),
            pltpu.VMEM((2, 256, 256), BF),
            pltpu.VMEM((2, 512, 256), BF),
            pltpu.VMEM((512, 256), BF),
            pltpu.VMEM((2, 256, 256), BF),
            pltpu.VMEM((2, 256, 256), BF),
            pltpu.VMEM((2, 256, 256), BF),
            pltpu.VMEM((2, 8, 256), F32),
            pltpu.VMEM((2, 8, 256), F32),
            pltpu.VMEM((2, 8, 256), F32),
            pltpu.VMEM((2, 256, 256), BF),
            pltpu.VMEM((2, 256, 256), BF),
            pltpu.VMEM((2, 2, 256, 256), BF),
            pltpu.VMEM((2, 8, 256), F32),
            pltpu.VMEM((2, 8, 256), F32),
            pltpu.VMEM((2, 2, 8, 256), F32),
            pltpu.VMEM((2, 256, 512), F32),
            pltpu.VMEM((2, 16, 512), F32),
            pltpu.VMEM((256, depth), BF),
            pltpu.VMEM((256, window), F32),
            pltpu.VMEM((256, window), F32),
            pltpu.VMEM((window, 128), F32),
            pltpu.VMEM((width, 256), F32),
            pltpu.VMEM((2, 128, window), BF),
            pltpu.VMEM((2, 128, window), BF),
            pltpu.VMEM((2, width, 128), BF),
            pltpu.VMEM((2, width, 128), BF),
            pltpu.VMEM((256, window), BF),
            pltpu.VMEM((256, window), BF),
            pltpu.VMEM((8, 256), F32),
            pltpu.VMEM((3, 8, 256), F32),
            dma((8,)),
            dma((32,)),
            dma((32,)),
            dma((20,)),
            dma((20,)),
            dma((3,)),
            dma((3,)),
        ],
        compiler_params=pltpu.CompilerParams(
            collective_id=0, has_side_effects=True, vmem_limit_bytes=60 * 1024 * 1024
        ),
    )(positions, freqs, queries, key_rows, value_rows, residual.T, direction, out_weight)
    return out.T


def device_body(*args):
    queries, key_rows, _, _, residual, direction, _ = args
    fits = (
        lax.axis_size("seq") == 4
        and lax.axis_size("tensor") == 4
        and queries.shape == (256, 1024)
        and key_rows.shape == (256, 512)
        and residual.shape[1] * 4 == direction.shape[0]
        and residual.shape[1] % 128 == 64
        and WINDOW == 1024
    )
    return fused_body(*args) if fits else body(*args)


def solution(mesh):
    return jax.shard_map(
        device_body,
        mesh=mesh,
        in_specs=(
            P(("groups", "seq"), "tensor"),
            P(("groups", "seq"), "tensor"),
            P(("groups", "seq"), "tensor"),
            P(("groups", "seq")),
            P(("groups", "seq"), "tensor"),
            P("groups"),
            P("tensor", None),
        ),
        out_specs=P(("groups", "seq"), "tensor"),
        check_vma=False,
    )
```

```python
import functools

import jax
import jax.numpy as jnp
from jax import lax
from jax.experimental import pallas as pl
from jax.experimental.pallas import tpu as pltpu
from jax.sharding import PartitionSpec as P

HD = 256
WINDOW = 1024


big_negative = -1e30


def shifted_2(value, axis, steps):
    count = lax.axis_size(axis)
    first, last = (max(0, -steps), min(count, count - steps))
    return lax.ppermute(value, axis, [(source, source + steps) for source in range(first, last)])


def rotary_tables(positions, head_dim):
    half_dim = head_dim // 2
    freqs = jnp.power(10000.0, -jnp.arange(half_dim, dtype=jnp.float32) * 2.0 / head_dim)
    angles = positions.astype(jnp.float32)[:, None] * freqs[None, :]
    return (jnp.cos(angles)[:, None, :], jnp.sin(angles)[:, None, :])


def rotate_heads(block, cos_table, sin_table, head_dim):
    row_count = block.shape[0]
    head_count = block.shape[1] // head_dim
    half_dim = head_dim // 2
    widened = block.reshape(row_count, head_count, head_dim).astype(jnp.float32)
    first_half = widened[:, :, :half_dim]
    second_half = widened[:, :, half_dim:]
    turned = jnp.concatenate(
        [
            first_half * cos_table - second_half * sin_table,
            second_half * cos_table + first_half * sin_table,
        ],
        axis=-1,
    )
    return turned.reshape(row_count, head_count * head_dim)


def body(queries, key_rows, value_rows, positions, residual, direction, out_weight):
    tokens_here = queries.shape[0]
    query_heads = queries.shape[1] // HD
    kv_heads = key_rows.shape[1] // HD
    group_size = query_heads // kv_heads
    span_blocks = WINDOW // tokens_here
    seq_index = lax.axis_index("seq")
    cos_table, sin_table = rotary_tables(positions, HD)
    rot_queries = (rotate_heads(queries, cos_table, sin_table, HD) * HD ** (-0.5)).astype(
        jnp.bfloat16
    )
    rot_keys = rotate_heads(key_rows, cos_table, sin_table, HD).astype(jnp.bfloat16)
    query_blocks = rot_queries.reshape(tokens_here, kv_heads, group_size, HD)
    own_scores = jnp.einsum(
        "qkgd,skd->kgqs",
        query_blocks,
        rot_keys.reshape(tokens_here, kv_heads, HD),
        preferred_element_type=jnp.float32,
    )
    earlier_keys = []
    earlier_values = []
    for distance in range(span_blocks, 0, -1):
        moved_keys, moved_values = shifted_2((rot_keys, value_rows), "seq", distance)
        earlier_keys.append(moved_keys)
        earlier_values.append(moved_values)
    far_keys = jnp.concatenate(earlier_keys, axis=0)
    far_values = jnp.concatenate(earlier_values, axis=0)
    far_scores = jnp.einsum(
        "qkgd,skd->kgqs",
        query_blocks,
        far_keys.reshape(-1, kv_heads, HD),
        preferred_element_type=jnp.float32,
    )
    scores = jnp.concatenate([far_scores, own_scores], axis=-1)
    query_index = seq_index * tokens_here + jnp.arange(tokens_here, dtype=jnp.int32)
    key_index = (seq_index - span_blocks) * tokens_here + jnp.arange(
        (span_blocks + 1) * tokens_here, dtype=jnp.int32
    )
    gap_grid = query_index[:, None] - key_index[None, :]
    allowed = (gap_grid >= 0) & (gap_grid < WINDOW) & (key_index[None, :] >= 0)
    scores = jnp.where(allowed, scores, big_negative)
    row_max = jnp.max(scores, axis=-1, keepdims=True)
    shifted = jnp.exp(scores - row_max)
    row_sum = jnp.sum(shifted, axis=-1, keepdims=True)
    weights = (shifted / row_sum).astype(jnp.bfloat16)
    every_value = jnp.concatenate([far_values, value_rows], axis=0).reshape(-1, kv_heads, HD)
    mixed = jnp.einsum("kgqs,skd->qkgd", weights, every_value, preferred_element_type=jnp.float32)
    attended = mixed.astype(jnp.bfloat16).reshape(tokens_here, query_heads * HD)
    partial_value = jnp.dot(attended, out_weight, preferred_element_type=jnp.float32)
    unit_dir = direction / jnp.sqrt(jnp.sum(direction * direction) + 1e-06)
    column_width = residual.shape[1]
    tensor_index = lax.axis_index("tensor")
    local_dir = lax.dynamic_slice_in_dim(unit_dir, tensor_index * column_width, column_width, 0)
    base_state = residual.astype(jnp.float32)
    rounded_terms = partial_value.astype(jnp.bfloat16).astype(jnp.float32)
    dot_terms = jnp.sum(rounded_terms * unit_dir[None, :], axis=1) + jnp.sum(
        base_state * local_dir[None, :], axis=1
    )
    along = lax.psum(dot_terms, "tensor")
    summed = lax.psum_scatter(
        partial_value.astype(jnp.bfloat16), "tensor", scatter_dimension=1, tiled=True
    ).astype(jnp.float32)
    hidden_state = base_state + summed
    ablated = (hidden_state - along[:, None] * local_dir[None, :]).astype(jnp.bfloat16)
    return ablated


BF = jnp.bfloat16
F32 = jnp.float32
MESH = pl.DeviceIdType.MESH

def rot(x, cos, sin):
    x = x.astype(F32)
    a, b = x[:, :128], x[:, 128:]
    return jnp.concatenate([a * cos - b * sin, b * cos + a * sin], axis=1)


def cos_sin(x):
    n = jnp.floor(x * 0.15915494309189535 + 0.5)
    r = ((x - n * 6.28125) - n * (507.0 / 262144.0)) - n * 1.2556659146019e-06
    k = jnp.floor(r * 0.6366197723675814 + 0.5)
    y = (r - k * 1.5707963705062866) + k * 4.371139000186241e-08
    z = y * y
    sin = y + y * z * (-1.0 / 6 + z * (1.0 / 120 + z * (-1.0 / 5040 + z * (1.0 / 362880))))
    cos = 1.0 + z * (-0.5 + z * (1.0 / 24 + z * (-1.0 / 720 + z * (1.0 / 40320))))
    odd = jnp.abs(k) == 1.0
    flip = jnp.abs(k) == 2.0
    cos_out = jnp.where(odd, -k * sin, jnp.where(flip, -cos, cos))
    sin_out = jnp.where(odd, k * cos, jnp.where(flip, -sin, sin))
    return cos_out, sin_out


def attend(q, blocks, diag):
    scores = [
        lax.dot_general(k, q, (((1,), (1,)), ((), ())), preferred_element_type=F32)
        for k, _ in blocks
    ]
    if diag:
        s = scores[-1]
        key = lax.broadcasted_iota(jnp.int32, s.shape, 0)
        lane = lax.broadcasted_iota(jnp.int32, s.shape, 1)
        row = (lane // 256) * 128 + lane % 128
        scores[-1] = jnp.where(key <= row, s, big_negative)
    m = functools.reduce(jnp.maximum, [jnp.max(s, axis=0, keepdims=True) for s in scores])
    acc, l = 0.0, 0.0
    for s, (_, v) in zip(scores, blocks):
        p = jnp.exp(s - m)
        l = l + jnp.sum(p, axis=0, keepdims=True)
        acc = acc + lax.dot_general(
            v, p.astype(BF), (((0,), (0,)), ((), ())), preferred_element_type=F32
        )
    return acc, m, l


def merge(state, out, lse):
    acc, m, l = state
    top = jnp.maximum(m, lse)
    mine, other = jnp.exp(m - top), jnp.exp(lse - top)
    return acc * mine + out.astype(F32) * other, top, l * mine + other


def kernel(pos_hbm, freq_ref, q_hbm, k_hbm, v_hbm, res_hbm, dir_hbm, w_hbm, out_ref,
           pos, direction, q, k, v, res, wbuf, urow, ldir, rq, rk, kv0, kv1, rq3, rq2,
           o_a, o_b2, o_b1, l_a, l_b2, l_b1, s_a, s_b2, s_c, t_a, t_b2, t_c,
           st_acc, st_ml, att, keep, dots, turn, last, a_send, a_recv, b_send, b_recv,
           c_send, c_recv, al_send, al_recv,
           lsem, ssem, rsem, xs, xr, als, alr):
    s = lax.axis_index("seq")
    t = lax.axis_index("tensor")
    core = t % 2
    x_here = t // 2
    x_other = 1 - x_here
    core_peer = t + 1 - 2 * core
    x_peer = (t + 2) % 4
    half = wbuf.shape[2]
    width = half // 2
    shift = (width // 128) * 128
    window = half - shift

    local = {}

    def fetch(name, src, dst):
        local[name] = pltpu.make_async_copy(src, dst, lsem.at[len(local)])
        local[name].start()

    fetch("pos", pos_hbm, pos)
    fetch("k", k_hbm, k)
    fetch("q", q_hbm, q)
    fetch("v", v_hbm, v)
    for i, x in enumerate((x_other, x_here)):
        cols = pl.ds(pl.multiple_of(x * half, 128), half)
        fetch(i, w_hbm.at[:, cols], wbuf.at[i])
    fetch("dir", dir_hbm, direction)
    fetch("res", res_hbm, res)

    barrier = pltpu.get_barrier_semaphore()
    for j in (1, 2, 3):
        pl.semaphore_signal(barrier, inc=1, device_id={"seq": (s + j) % 4}, device_id_type=MESH)
        pl.semaphore_signal(barrier, inc=1, device_id={"tensor": (t + j) % 4}, device_id_type=MESH)
    pl.semaphore_wait(barrier, 6)

    copies, index = {}, {}

    def add(name, dev, src, dst, lands_as=None):
        i = index[name] = len(index)
        copies[name] = pltpu.make_async_remote_copy(
            src_ref=src, dst_ref=dst, send_sem=ssem.at[i],
            recv_sem=rsem.at[i if lands_as is None else index[lands_as]],
            device_id={"seq": dev}, device_id_type=MESH)

    for g, name in ((0, "a"), (1, "b")):
        cols = slice(256 * g, 256 * g + 256)
        add("v0" + name + "1", 1, v_hbm.at[:, cols], kv0.at[2 * g + 1])
        add("k0" + name + "1", 1, rk.at[g], kv0.at[2 * g])
    add("v0a2", 2, v_hbm.at[:, 0:256], kv0.at[1])
    add("k0a2", 2, rk.at[0], kv0.at[0])
    add("v1a2", 2, v_hbm.at[:, 0:256], kv1.at[1])
    add("k1a2", 2, rk.at[0], kv1.at[0])
    for c in (0, 1):
        rows = slice(256 * c, 256 * c + 256)
        n = str(c)
        add("q3b2" + n, 2, rq.at[1, rows], rq3.at[1, rows])
        add("q3a2" + n, 2, rq.at[0, rows], rq3.at[0, rows])
        add("o3b" + n, 3, s_b2.at[c], o_b2.at[c])
        add("l3b" + n, 3, t_b2.at[c], l_b2.at[c])
        add("f3b1" + n, 1, rq3.at[1, rows], rq3.at[1, rows])
        add("q2b1" + n, 1, rq.at[1, rows], rq2.at[rows])
        add("o3a" + n, 3, s_a.at[c], o_a.at[c])
        add("l3a" + n, 3, t_a.at[c], l_a.at[c])
        add("o2b" + n, 2, s_c.at[0, c], o_b1.at[c])
        add("l2b" + n, 2, t_c.at[0, c], l_b1.at[c])
        add("o3c" + n, 3, s_c.at[1, c], o_b1.at[c], "o2b" + n)
        add("l3c" + n, 3, t_c.at[1, c], l_b1.at[c], "l2b" + n)

    def start(*names):
        for n in names:
            copies[n].start()

    def recv(*names):
        for n in names:
            copies[n].wait_recv()

    def sent(*names):
        for n in names:
            copies[n].wait_send()

    @pl.when(s == 0)
    def _():
        start("v0a2")

    @pl.when(s == 1)
    def _():
        start("v1a2")

    local["pos"].wait()
    freqs = freq_ref[...]
    tokens = pos[...].astype(F32).reshape(1, 256)
    angles = jnp.concatenate(
        [jnp.broadcast_to(tokens[:, 128 * c:128 * c + 128], (128, 128)).T for c in (0, 1)], axis=0
    ) * freqs
    cos, sin = cos_sin(angles)
    def rotate_keys():
        local["k"].wait()
        for g in (1, 0):
            rk[g] = rot(k[:, 256 * g:256 * g + 256], cos, sin).astype(BF)

    @pl.when(s == 0)
    def _():
        rotate_keys()
        start("k0a2")

    @pl.when(s == 1)
    def _():
        rotate_keys()
        start("k1a2")

    local["q"].wait()
    for g in (1, 0):
        for h in (0, 1):
            at = 256 * (2 * g + h)
            r = (rot(q[:, at:at + 256], cos, sin) * HD ** (-0.5)).astype(BF)
            for c in (0, 1):
                rq[g, 256 * c + 128 * h:256 * c + 128 * h + 128, :] = r[128 * c:128 * c + 128]
        if g == 1:
            @pl.when(s == 3)
            def _():
                start("q3b20")

            @pl.when(s == 2)
            def _():
                start("q2b10", "q2b11")

    @pl.when(s >= 2)
    def _():
        rotate_keys()

    local["v"].wait()

    def own(g):
        return rk[g], v[:, 256 * g:256 * g + 256]

    def first(g):
        return kv0[2 * g], kv0[2 * g + 1]

    def second():
        return kv1[0], kv1[1]

    def put(g, state, chunks):
        acc, _, l = state
        out = acc / l
        for i, c in enumerate(chunks):
            for h in (0, 1):
                at = 256 * i + 128 * h
                col = 256 * (2 * g + h)
                att[128 * c:128 * c + 128, col:col + 256] = out[:, at:at + 128].T.astype(BF)

    def send_state(state, out_to, lse_to, *names):
        acc, m, l = state
        out_to[...] = (acc / l).astype(BF)
        lse_to[...] = jnp.broadcast_to(m + jnp.log(l), lse_to.shape)
        start(*names)

    def hold(g, state):
        acc, m, l = state
        st_acc[g] = acc
        st_ml[g, 0:8] = jnp.broadcast_to(m, (8, 512))
        st_ml[g, 8:16] = jnp.broadcast_to(l, (8, 512))

    def held(g, c):
        lanes = slice(256 * c, 256 * c + 256)
        return st_acc[g, :, lanes], st_ml[g, 0:1, lanes], st_ml[g, 8:9, lanes]

    def prepare_direction():
        local["dir"].wait()
        whole = direction[...].reshape(1, 2 * half)
        scale = 1.0 / jnp.sqrt(jnp.sum(whole * whole, axis=1, keepdims=True) + 1e-06)
        lane = lax.broadcasted_iota(jnp.int32, (1, window), 1)
        shared = jnp.where(core == 0, 0, shift)
        keep_lane = (lane < shared) | (lane >= shared + (window - shift))
        for i, x in enumerate((x_other, x_here)):
            mine = jnp.where(x == 0, whole[:, :half], whole[:, half:]) * scale
            low, high = mine[:, :window], mine[:, shift:]
            urow[2 * i:2 * i + 1] = jnp.where(keep_lane, jnp.where(core == 0, high, low), 0.0)
            urow[2 * i + 1:2 * i + 2] = jnp.where(core == 0, low, high)
        for at in range(0, window, 128):
            ldir[at:at + 128, :] = jnp.broadcast_to(urow[3:4, at:at + 128], (128, 128)).T

    @pl.when(s == 0)
    def _():
        start("v0b1", "k0b1")
        put(1, attend(rq[1], [own(1)], True), (0, 1))
        start("v0a1", "k0a1")
        put(0, attend(rq[0], [own(0)], True), (0, 1))

    @pl.when(s == 2)
    def _():
        recv("q3b20")
        start("f3b10")
        state = attend(rq3[1, 0:256, :], [own(1)], False)
        send_state(state, s_b2.at[0], t_b2.at[0], "o3b0", "l3b0")
        hold(1, attend(rq[1], [own(1)], True))

    @pl.when(s == 3)
    def _():
        start("q3a20", "q3b21", "q3a21")
        hold(0, attend(rq[0], [own(0)], True))
        hold(1, attend(rq[1], [own(1)], True))

    prepare_direction()

    @pl.when(s == 1)
    def _():
        recv("v0b1", "k0b1")
        for c in (0, 1):
            n = str(c)
            rows = slice(256 * c, 256 * c + 256)
            recv("q2b1" + n)
            state = attend(rq2[rows, :], [first(1), own(1)], False)
            send_state(state, s_c.at[0, c], t_c.at[0, c], "o2b" + n, "l2b" + n)
            recv("f3b1" + n)
            state = attend(rq3[1, rows, :], [first(1), own(1)], False)
            send_state(state, s_c.at[1, c], t_c.at[1, c], "o3c" + n, "l3c" + n)
        put(1, attend(rq[1], [first(1), own(1)], True), (0, 1))
        recv("v0a1", "k0a1")
        put(0, attend(rq[0], [first(0), own(0)], True), (0, 1))

    @pl.when(s == 2)
    def _():
        recv("q3b21")
        start("f3b11")
        state = attend(rq3[1, 256:512, :], [own(1)], False)
        send_state(state, s_b2.at[1], t_b2.at[1], "o3b1", "l3b1")
        recv("v1a2", "k1a2", "v0a2", "k0a2")
        for c in (0, 1):
            n = str(c)
            recv("q3a2" + n)
            rows = slice(256 * c, 256 * c + 256)
            state = attend(rq3[0, rows, :], [first(0), second(), own(0)], False)
            send_state(state, s_a.at[c], t_a.at[c], "o3a" + n, "l3a" + n)
        put(0, attend(rq[0], [first(0), second(), own(0)], True), (0, 1))

    def x_copies(src, dst, first, dev):
        part = src.shape[0] // 4
        return [
            pltpu.make_async_remote_copy(
                src_ref=src.at[part * j:part * j + part], dst_ref=dst.at[part * j:part * j + part],
                send_sem=xs.at[first + j], recv_sem=xr.at[first + j],
                device_id={"tensor": dev}, device_id_type=MESH)
            for j in range(4)
        ]

    def begin(parts):
        for part in parts:
            part.start()

    def arrive(parts):
        for part in parts:
            part.wait_recv()

    def leave(parts):
        for part in parts:
            part.wait_send()

    local["res"].wait()
    own_window = pl.ds(pl.multiple_of(core * shift, 128), window)
    peer_window = pl.ds(pl.multiple_of((1 - core) * shift, 128), window)
    own_rows = pl.ds(pl.multiple_of(core * (width - shift), 64), width)
    local_dir = ldir[own_rows, :]
    local[0].wait()
    local[1].wait()
    a_copies, b_copies, al_copies = {}, {}, {}
    for c in (0, 1):
        @pl.when(s == 3)
        def _(c=c):
            n = str(c)
            recv("o3b" + n, "l3b" + n, "o3a" + n, "l3a" + n)
            put(0, merge(held(0, c), o_a[c], l_a[c, 0:1]), (c,))
            state = merge(held(1, c), o_b2[c], l_b2[c, 0:1])
            recv("o2b" + n, "l2b" + n)
            put(1, merge(state, o_b1[c], l_b1[c, 0:1]), (c,))

        @pl.when(s == 2)
        def _(c=c):
            recv("o2b" + str(c), "l2b" + str(c))
            put(1, merge(held(1, c), o_b1[c], l_b1[c, 0:1]), (c,))

        rows = slice(128 * c, 128 * c + 128)
        part = jnp.dot(att[rows, :], wbuf[0, :, peer_window], preferred_element_type=F32)
        a_send[c] = part.astype(BF)
        a_copies[c] = x_copies(a_send.at[c], a_recv.at[c], 4 * c, core_peer)
        begin(a_copies[c])
        part = jnp.dot(att[rows, :], wbuf[0, :, own_window], preferred_element_type=F32)
        keep[rows, :] = part
        arrive(a_copies[c])
        turn[...] = (keep[rows, :] + a_recv[c].astype(F32)).T
        b_send[c] = turn[own_rows, :].astype(BF)
        b_copies[c] = x_copies(b_send.at[c], b_recv.at[c], 8 + 4 * c, x_peer)
        begin(b_copies[c])
        dots[rows, :] = a_send[c].astype(F32) * urow[0:1] + keep[rows, :] * urow[1:2]

    part = jnp.dot(att[...], wbuf[1, :, peer_window], preferred_element_type=F32)
    c_send[...] = part.astype(BF)
    c_copy = x_copies(c_send, c_recv, 16, core_peer)
    begin(c_copy)
    part = jnp.dot(att[...], wbuf[1, :, own_window], preferred_element_type=F32)
    keep[...] = part
    total = jnp.sum(
        dots[...] + c_send[...].astype(F32) * urow[2:3] + part * urow[3:4], axis=1, keepdims=True
    )
    for c in (0, 1):
        lanes = slice(128 * c, 128 * c + 128)
        line = jnp.broadcast_to(total[lanes], (128, 128)).T[0:1]
        line = line + jnp.sum(res[:, lanes].astype(F32) * local_dir, axis=0, keepdims=True)
        al_send[:, lanes] = jnp.broadcast_to(line, (8, 128))
    for j in (1, 2, 3):
        al_copies[j] = pltpu.make_async_remote_copy(
            src_ref=al_send, dst_ref=al_recv.at[j - 1],
            send_sem=als.at[j - 1], recv_sem=alr.at[j - 1],
            device_id={"tensor": (t + j) % 4}, device_id_type=MESH)
        al_copies[j].start()
    arrive(c_copy)
    for c in (0, 1):
        lanes = slice(128 * c, 128 * c + 128)
        turn[...] = (keep[lanes, :] + c_recv[lanes, :].astype(F32)).T
        last[:, lanes] = res[:, lanes].astype(F32) + turn[own_rows, :]
    along = al_send[0:1]
    for j in (1, 2, 3):
        al_copies[j].wait_recv()
        along = along + al_recv[j - 1, 0:1]
    for c in (0, 1):
        lanes = slice(128 * c, 128 * c + 128)
        last[:, lanes] = last[:, lanes] - along[:, lanes] * local_dir
        arrive(b_copies[c])
        out_ref[:, lanes] = (last[:, lanes] + b_recv[c].astype(F32)).astype(BF)

    leave(c_copy)
    for j in (1, 2, 3):
        al_copies[j].wait_send()
    for c in (0, 1):
        leave(a_copies[c])
        leave(b_copies[c])

    @pl.when(s == 0)
    def _():
        sent("v0b1", "k0b1", "v0a2", "k0a2", "v0a1", "k0a1")

    @pl.when(s == 1)
    def _():
        sent("v1a2", "k1a2", "o2b0", "l2b0", "o2b1", "l2b1", "o3c0", "l3c0", "o3c1", "l3c1")

    @pl.when(s == 2)
    def _():
        sent("q2b10", "q2b11", "f3b10", "f3b11", "o3b0", "l3b0", "o3b1", "l3b1", "o3a0", "l3a0", "o3a1", "l3a1")

    @pl.when(s == 3)
    def _():
        sent("q3b20", "q3a20", "q3b21", "q3a21")


def fused_body(queries, key_rows, value_rows, positions, residual, direction, out_weight):
    freqs = jnp.power(10000.0, -jnp.arange(HD // 2, dtype=F32) * 2.0 / HD)[None, :]
    rows, width = residual.shape
    depth = out_weight.shape[0]
    window = 2 * width - (width // 128) * 128
    vmem = pl.BlockSpec(memory_space=pltpu.VMEM)
    anywhere = pl.BlockSpec(memory_space=pl.ANY)
    dma = pltpu.SemaphoreType.DMA
    out = pl.pallas_call(
        kernel,
        out_shape=jax.ShapeDtypeStruct((width, rows), BF),
        in_specs=[anywhere, vmem] + [anywhere] * 6,
        out_specs=vmem,
        scratch_shapes=[
            pltpu.VMEM(positions.shape, jnp.int32),
            pltpu.VMEM(direction.shape, F32),
            pltpu.VMEM(queries.shape, BF),
            pltpu.VMEM(key_rows.shape, BF),
            pltpu.VMEM(value_rows.shape, BF),
            pltpu.VMEM((width, rows), BF),
            pltpu.VMEM((2, depth, 2 * width), BF),
            pltpu.VMEM((8, window), F32),
            pltpu.VMEM((window, 128), F32),
            pltpu.VMEM((2, 512, 256), BF),
            pltpu.VMEM((2, 256, 256), BF),
            pltpu.VMEM((4, 256, 256), BF),
            pltpu.VMEM((2, 256, 256), BF),
            pltpu.VMEM((2, 512, 256), BF),
            pltpu.VMEM((512, 256), BF),
            pltpu.VMEM((2, 256, 256), BF),
            pltpu.VMEM((2, 256, 256), BF),
            pltpu.VMEM((2, 256, 256), BF),
            pltpu.VMEM((2, 8, 256), F32),
            pltpu.VMEM((2, 8, 256), F32),
            pltpu.VMEM((2, 8, 256), F32),
            pltpu.VMEM((2, 256, 256), BF),
            pltpu.VMEM((2, 256, 256), BF),
            pltpu.VMEM((2, 2, 256, 256), BF),
            pltpu.VMEM((2, 8, 256), F32),
            pltpu.VMEM((2, 8, 256), F32),
            pltpu.VMEM((2, 2, 8, 256), F32),
            pltpu.VMEM((2, 256, 512), F32),
            pltpu.VMEM((2, 16, 512), F32),
            pltpu.VMEM((256, depth), BF),
            pltpu.VMEM((256, window), F32),
            pltpu.VMEM((256, window), F32),
            pltpu.VMEM((window, 128), F32),
            pltpu.VMEM((width, 256), F32),
            pltpu.VMEM((2, 128, window), BF),
            pltpu.VMEM((2, 128, window), BF),
            pltpu.VMEM((2, width, 128), BF),
            pltpu.VMEM((2, width, 128), BF),
            pltpu.VMEM((256, window), BF),
            pltpu.VMEM((256, window), BF),
            pltpu.VMEM((8, 256), F32),
            pltpu.VMEM((3, 8, 256), F32),
            dma((8,)),
            dma((32,)),
            dma((32,)),
            dma((20,)),
            dma((20,)),
            dma((3,)),
            dma((3,)),
        ],
        compiler_params=pltpu.CompilerParams(
            collective_id=0, has_side_effects=True, vmem_limit_bytes=60 * 1024 * 1024
        ),
    )(positions, freqs, queries, key_rows, value_rows, residual.T, direction, out_weight)
    return out.T


def device_body(*args):
    queries, key_rows, _, _, residual, direction, _ = args
    fits = (
        lax.axis_size("seq") == 4
        and lax.axis_size("tensor") == 4
        and queries.shape == (256, 1024)
        and key_rows.shape == (256, 512)
        and residual.shape[1] * 4 == direction.shape[0]
        and residual.shape[1] % 128 == 64
        and WINDOW == 1024
    )
    return fused_body(*args) if fits else body(*args)


def solution(mesh):
    return jax.shard_map(
        device_body,
        mesh=mesh,
        in_specs=(
            P(("groups", "seq"), "tensor"),
            P(("groups", "seq"), "tensor"),
            P(("groups", "seq"), "tensor"),
            P(("groups", "seq")),
            P(("groups", "seq"), "tensor"),
            P("groups"),
            P("tensor", None),
        ),
        out_specs=P(("groups", "seq"), "tensor"),
        check_vma=False,
    )
```
